32 devices in a mesh: dp: 4 (over y, core), fsdp: 8 (over z, x).
Axes of the slice: x: 2, y: 2, z: 4, core: 2. Of those that a mesh axis runs over, the one named last changes fastest.
Arguments:
- tokens: bfloat16 [32, 1024, 768], P(('dp', 'fsdp')), may hold values from -6 to 6
- lengths: int32 [32], P(('dp', 'fsdp')), may hold values from 128 to 1024, as said below
- cotangent: bfloat16 [32, 1024, 768], P(('dp', 'fsdp')), may hold values from -6 to 6
- query_weight: bfloat16 [768, 768], P(('dp', 'fsdp')), may hold values from -0.21875 to 0.21875
- query_bias: bfloat16 [768], P(('dp', 'fsdp')), may hold values from -1.75 to 1.75
- keyval_weight: bfloat16 [768, 128], P(('dp', 'fsdp')), may hold values from -0.21875 to 0.21875
- keyval_bias: bfloat16 [128], P(('dp', 'fsdp')), may hold values from -1.75 to 1.75
- out_weight: bfloat16 [768, 768], P(('dp', 'fsdp')), may hold values from -2.5 to 2.5
- out_bias: bfloat16 [768], P(('dp', 'fsdp')), may hold values from -1.75 to 1.75
- norm_attn_gain: bfloat16 [768], P(('dp', 'fsdp')), may hold values from 0.5 to 1.5
- norm_attn_bias: bfloat16 [768], P(('dp', 'fsdp')), may hold values from -1.75 to 1.75
- norm_mlp_gain: bfloat16 [768], P(('dp', 'fsdp')), may hold values from 0.5 to 1.5
- norm_mlp_bias: bfloat16 [768], P(('dp', 'fsdp')), may hold values from -1.75 to 1.75
- up_weight: bfloat16 [768, 3072], P(('dp', 'fsdp')), may hold values from -0.21875 to 0.21875
- up_bias: bfloat16 [3072], P(('dp', 'fsdp')), may hold values from -1.75 to 1.75
- down_weight: bfloat16 [3072, 768], P(('dp', 'fsdp')), may hold values from -0.109375 to 0.109375
- down_bias: bfloat16 [768], P(('dp', 'fsdp')), may hold values from -1.75 to 1.75
Outputs:
- layer_out: bfloat16 [32, 1024, 768], P(('dp', 'fsdp'))
- grad_tokens: float32 [32, 1024, 768], P(('dp', 'fsdp'))
- grad_query_weight: float32 [768, 768], P(('dp', 'fsdp'))
- grad_query_bias: float32 [768], P(('dp', 'fsdp'))
- grad_keyval_weight: float32 [768, 128], P(('dp', 'fsdp'))
- grad_keyval_bias: float32 [128], P(('dp', 'fsdp'))
- grad_out_weight: float32 [768, 768], P(('dp', 'fsdp'))
- grad_out_bias: float32 [768], P(('dp', 'fsdp'))
- grad_norm_attn_gain: float32 [768], P(('dp', 'fsdp'))
- grad_norm_attn_bias: float32 [768], P(('dp', 'fsdp'))
- grad_norm_mlp_gain: float32 [768], P(('dp', 'fsdp'))
- grad_norm_mlp_bias: float32 [768], P(('dp', 'fsdp'))
- grad_up_weight: float32 [768, 3072], P(('dp', 'fsdp'))
- grad_up_bias: float32 [3072], P(('dp', 'fsdp'))
- grad_down_weight: float32 [3072, 768], P(('dp', 'fsdp'))
- grad_down_bias: float32 [768], P(('dp', 'fsdp'))
The draws below stay inside these ranges and needn't reach their ends.
Inputs may be any that keep to these rules, and one draw needn't show every extreme that they name: `lengths`: some sequence has length exactly 1024 and some exactly 128; most sequences are long, a few short.
All inputs are finite; a program needn't handle non-finite values.
Results may differ from the reference program's by a relative error of at most 0.011.
Values may be sent and summed in bfloat16 or wider, within the bound.
No kernel may reach another device: no remote copies, remote signals or barrier semaphores. Data moves between devices by JAX's collectives and lax.ppermute only.
A program may use at most 256 MiB of HBM per device.

```python
import jax
import jax.numpy as jnp
from jax import lax

D = 768
HEADS = 12
HD = 64
FF = 3072
ROT = 16
SEQ_LEN = 1024
MIN_LEN = 128
BATCH = 32


def draw_lengths(key, part):
    key = jax.random.fold_in(key, 17)
    sub_keys = jax.random.split(key, 4)
    length_span = SEQ_LEN - MIN_LEN + 1
    factor_one = jax.random.randint(sub_keys[0], (BATCH,), 0, length_span)
    factor_two = jax.random.randint(sub_keys[1], (BATCH,), 0, length_span)
    result = SEQ_LEN - factor_one * factor_two // length_span
    longest = jax.random.randint(sub_keys[2], (), 0, BATCH)
    shortest = (longest + 1 + jax.random.randint(sub_keys[3], (), 0, BATCH - 1)) % BATCH
    result = result.at[longest].set(SEQ_LEN).at[shortest].set(MIN_LEN)
    return result.astype(jnp.int32)


def block_levels(rng, dims, shards, least, high):
    level = 1.0
    for dim, blocks in shards:
        draws = jax.random.uniform(jax.random.fold_in(jax.random.fold_in(rng, 6), dim), (blocks,), jnp.float32, least / len(shards), high / len(shards))
        level = level * jnp.repeat(jnp.exp(draws), dims[dim] // blocks).reshape((-1,) + (1,) * (len(dims) - 1 - dim))
    return level


def scatter_about(stream_key, dims, width, bound, cuts=(), held_as=jnp.bfloat16):
    array = jax.random.normal(stream_key, dims, jnp.float32) * width
    if len(cuts) > 0:
        array = block_levels(stream_key, dims, cuts, -0.22, 0.18) * array
    return jnp.clip(array, min=-bound, max=bound).astype(held_as)


def setup_inputs(seed: int = 0) -> dict:
    seeds = jax.random.split(jax.random.key(seed), 18)
    return {
        "tokens": scatter_about(seeds[0], (BATCH, SEQ_LEN, D), 1.0, 6.0, ((0, 32),)),
        "lengths": draw_lengths(jax.random.fold_in(seeds[17], 71), 0),
        "cotangent": scatter_about(seeds[2], (BATCH, SEQ_LEN, D), 1.0, 6.0, ((0, 32),)),
        "query_weight": scatter_about(seeds[3], (D, D), D ** -0.5, 0.21875, ((0, 32),)),
        "query_bias": scatter_about(seeds[4], (D,), 0.3, 1.75, ((0, 32),)),
        "keyval_weight": scatter_about(seeds[5], (D, 2 * HD), D ** -0.5, 0.21875, ((0, 32),)),
        "keyval_bias": scatter_about(seeds[6], (2 * HD,), 0.3, 1.75, ((0, 32),)),
        "out_weight": scatter_about(seeds[7], (D, D), (D // 128) ** -0.5, 2.5, ((0, 32),)),
        "out_bias": scatter_about(seeds[8], (D,), 0.3, 1.75, ((0, 32),)),
        "norm_attn_gain": jnp.clip(1.0 + 0.1 * jax.random.normal(seeds[9], (D,), jnp.float32), 0.5, 1.5).astype(jnp.bfloat16),
        "norm_attn_bias": scatter_about(seeds[10], (D,), 0.3, 1.75, ((0, 32),)),
        "norm_mlp_gain": jnp.clip(1.0 + 0.1 * jax.random.normal(seeds[11], (D,), jnp.float32), 0.5, 1.5).astype(jnp.bfloat16),
        "norm_mlp_bias": scatter_about(seeds[12], (D,), 0.3, 1.75, ((0, 32),)),
        "up_weight": scatter_about(seeds[13], (D, FF), D ** -0.5, 0.21875, ((0, 32),)),
        "up_bias": scatter_about(seeds[14], (FF,), 0.3, 1.75, ((0, 32),)),
        "down_weight": scatter_about(seeds[15], (FF, D), FF ** -0.5, 0.109375, ((0, 32),)),
        "down_bias": scatter_about(seeds[16], (D,), 0.3, 1.75, ((0, 32),)),
    }


eps_norm = 1e-05
neg_big = -1e+30
highest = lax.Precision.HIGHEST

@jax.custom_vjp
def low(v):
    return lax.optimization_barrier(v.astype(jnp.bfloat16)).astype(jnp.float32)

@jax.custom_vjp
def low_back(v):
    return v

def low_keep(v):
    return (low(v), None)

def low_pass(kept, grad):
    return (grad,)

def back_keep(v):
    return (v, None)

def back_low(kept, grad):
    return (low(grad),)
low.defvjp(low_keep, low_pass)
low_back.defvjp(back_keep, back_low)

def layer_norm(token_rows, norm_gain, norm_shift):
    average = lax.optimization_barrier(jnp.mean(token_rows, axis=-1, keepdims=True))
    centred = token_rows - average
    spread = lax.optimization_barrier(jnp.mean(centred * centred, axis=-1, keepdims=True))
    return centred * lax.rsqrt(spread + eps_norm) * norm_gain + norm_shift

def rotary_tables(seq_len, rot_dims):
    half_rot = rot_dims // 2
    inverse_freq = 10000.0 ** (-(2.0 * jnp.arange(half_rot, dtype=jnp.float32)) / rot_dims)
    angles = jnp.arange(seq_len, dtype=jnp.float32)[:, None] * inverse_freq[None, :]
    return (jnp.cos(angles), jnp.sin(angles))

def rotate(values, cosine_table, sine_table):
    half_rot = cosine_table.shape[-1]
    half_one = values[..., :half_rot]
    half_two = values[..., half_rot:2 * half_rot]
    return jnp.concatenate([half_one * cosine_table - half_two * sine_table, half_two * cosine_table + half_one * sine_table, values[..., 2 * half_rot:]], axis=-1)

def attention(query_rot, key_rot, values, length):
    block_rows = min(512, SEQ_LEN)
    block_count = SEQ_LEN // block_rows
    score_scale = HD ** (-0.5)
    key_pos = jnp.arange(SEQ_LEN).astype(jnp.int32)

    def one_block(block_items):
        query_block, block_start = block_items
        scores = low_back(score_scale * jnp.einsum('qhd,kd->hqk', query_block, key_rot, precision=highest))
        query_pos = block_start + jnp.arange(block_rows).astype(jnp.int32)
        allowed = (key_pos[None, :] <= query_pos[:, None]) & (key_pos[None, :] < length)
        scores = jnp.where(allowed[None], scores, neg_big)
        row_max = lax.optimization_barrier(jnp.max(scores, axis=-1, keepdims=True))
        exponent = jnp.exp(scores - row_max)
        softmax_low = low(exponent / lax.optimization_barrier(jnp.sum(exponent, axis=-1, keepdims=True)))
        return jnp.einsum('hqk,kd->qhd', softmax_low, values, precision=highest)
    query_blocks = query_rot.reshape(block_count, block_rows, HEADS, HD)
    starts = (jnp.arange(block_count) * block_rows).astype(jnp.int32)
    mixed_heads = lax.map(jax.checkpoint(one_block), (query_blocks, starts))
    return mixed_heads.reshape(SEQ_LEN, HEADS, HD)

def reference(tokens, lengths, cotangent, query_weight, query_bias, keyval_weight, keyval_bias, out_weight, out_bias, norm_attn_gain, norm_attn_bias, norm_mlp_gain, norm_mlp_bias, up_weight, up_bias, down_weight, down_bias):
    cosine_table, sine_table = rotary_tables(SEQ_LEN, ROT)

    def one_sequence(token_rows, length, params):
        w_query, b_query, w_keyval, b_keyval, w_out, b_out, attn_gain, attn_shift, mlp_gain, mlp_shift, w_up, b_up, w_down, b_down = params
        h_attn = low(layer_norm(token_rows, attn_gain, attn_shift))
        query_lin = low_back(jnp.dot(h_attn, w_query, precision=highest) + b_query)
        keyval_lin = low_back(jnp.dot(h_attn, w_keyval, precision=highest) + b_keyval)
        query_rot = low(rotate(query_lin.reshape(SEQ_LEN, HEADS, HD), cosine_table[:, None, :], sine_table[:, None, :]))
        key_rot = low(rotate(keyval_lin[:, :HD], cosine_table, sine_table))
        values = low(keyval_lin[:, HD:])
        mixed_heads = attention(query_rot, key_rot, values, length)
        mixed_low = low(low_back(mixed_heads.reshape(SEQ_LEN, D)))
        attn_out = jnp.dot(mixed_low, w_out, precision=highest) + b_out
        h_mlp = low(layer_norm(token_rows, mlp_gain, mlp_shift))
        up_lin = low_back(jnp.dot(h_mlp, w_up, precision=highest) + b_up)
        act_low = low(jax.nn.gelu(up_lin, approximate=False))
        mlp_out = jnp.dot(act_low, w_down, precision=highest) + b_down
        row_keep = (jnp.arange(SEQ_LEN).astype(jnp.int32) < length).astype(jnp.float32)
        return token_rows + row_keep[:, None] * (attn_out + mlp_out)

    def whole_layer(token_f, *params):

        def scan_step(running, seq_items):
            return (running, jax.checkpoint(one_sequence)(seq_items[0], seq_items[1], params))
        running, layer_rows = lax.scan(scan_step, jnp.zeros((), jnp.float32), (token_f, lengths))
        return layer_rows
    arrays = tuple((param.astype(jnp.float32) for param in (query_weight, query_bias, keyval_weight, keyval_bias, out_weight, out_bias, norm_attn_gain, norm_attn_bias, norm_mlp_gain, norm_mlp_bias, up_weight, up_bias, down_weight, down_bias)))
    layer_rows, pullback = jax.vjp(whole_layer, tokens.astype(jnp.float32), *arrays)
    grads = pullback(cotangent.astype(jnp.float32))
    return (layer_rows.astype(jnp.bfloat16), grads[0], grads[1], grads[2], grads[3], grads[4], grads[5], grads[6], grads[7], grads[8], grads[9], grads[10], grads[11], grads[12], grads[13], grads[14])
```

```python
import functools

import jax
import jax.numpy as jnp
from jax import lax
from jax.experimental import pallas as pl
from jax.experimental.pallas import tpu as pltpu
from jax.sharding import PartitionSpec as P

f32 = jnp.float32
bf16 = jnp.bfloat16

ROT = 16
EPS = 1e-05
NEG = -1e30
ROOT_HALF = 0.7071067811865476
INV_ROOT_TAU = 0.3989422804014327
LANES = 128
BOTH = ("dp", "fsdp")
VMEM = 60 * 1024 * 1024

QB, OB, GA, BA, GM, BM, DB, UB, KB = 0, 1, 2, 3, 4, 5, 6, 7, 11


def dot(a, b, ca, cb):
    return lax.dot_general(a, b, (((ca,), (cb,)), ((), ())), preferred_element_type=f32)


def params(**kw):
    return pltpu.CompilerParams(vmem_limit_bytes=VMEM, **kw)


def whole(shape):
    return pl.BlockSpec(shape, lambda *_: (0,) * len(shape))


def rotary_tables(seq_len, head_dim):
    half = ROT // 2
    inverse_freq = 10000.0 ** (-(2.0 * jnp.arange(half, dtype=f32)) / ROT)
    angles = jnp.arange(seq_len, dtype=f32)[:, None] * inverse_freq[None, :]
    cos, sin = jnp.cos(angles), jnp.sin(angles)
    one = jnp.ones((seq_len, head_dim - ROT), f32)
    zero = jnp.zeros((seq_len, half), f32)
    none = jnp.zeros((seq_len, head_dim - ROT), f32)
    own = jnp.concatenate([cos, cos, one], 1)
    up = jnp.concatenate([sin, zero, none], 1)
    down = jnp.concatenate([zero, sin, none], 1)
    two = lambda t: jnp.concatenate([t, t], 1)
    return jnp.stack([two(own), two(up), two(down)])


def partners(v):
    half = ROT // 2
    return pltpu.roll(v, LANES - half, 1), pltpu.roll(v, half, 1)


def rotate(v, own, up, down):
    ahead, behind = partners(v)
    return v * own - ahead * up + behind * down


def rotate_back(v, own, up, down):
    ahead, behind = partners(v)
    return v * own + ahead * up - behind * down


def standardise(rows):
    average = jnp.mean(rows, axis=-1, keepdims=True)
    centred = rows - average
    scaled = lax.rsqrt(jnp.mean(centred * centred, axis=-1, keepdims=True) + EPS)
    return centred * scaled, scaled


def norm_back(grad, normed, scaled, gain):
    e = grad * gain
    return scaled * (
        e - jnp.mean(e, axis=-1, keepdims=True) - normed * jnp.mean(e * normed, axis=-1, keepdims=True)
    )


def col_sum(v):
    return jnp.sum(v, axis=0, keepdims=True)


def kept_rows(block, rows, length):
    pos = lax.broadcasted_iota(jnp.int32, (rows, 1), 0) + block * rows
    return (pos < length).astype(f32)


def spread_key_bias(width, kv_width, per_row, per_kv):
    row = lax.broadcasted_iota(jnp.int32, (width, kv_width), 0)
    col = lax.broadcasted_iota(jnp.int32, (width, kv_width), 1)
    owner = col // per_kv
    return (row == owner * per_row + (col - owner * per_kv)).astype(bf16)


def pre_kernel(len_ref, x_ref, cot_ref, w_ref, tab_ref, q_ref, kv_ref, ha_ref, hm_ref, gy_ref, gm_ref, vec_ref, vec_s, *, dims):
    width, kv_width, rows, per_row, per_kv = dims
    i = pl.program_id(0)
    c_out = width + kv_width
    c_vec = c_out + width

    @pl.when(i == 0)
    def _():
        low = w_ref[:, c_vec : c_vec + LANES]
        lines = low.astype(f32).T[:16]
        vec_s[:16, :] = lines
        spread = spread_key_bias(width, kv_width, per_row, per_kv)
        vec_s[16:32, :kv_width] = dot(lines.astype(bf16), spread, 1, 0)
        vec_ref[...] = vec_s[...]

    normed, _ = standardise(x_ref[...].astype(f32))
    vec = vec_s[...]
    ha = (normed * vec[GA : GA + 1] + vec[BA : BA + 1]).astype(bf16)
    hm = (normed * vec[GM : GM + 1] + vec[BM : BM + 1]).astype(bf16)
    ha_ref[...] = ha
    hm_ref[...] = hm
    own, up, down = tab_ref[0], tab_ref[1], tab_ref[2]
    scale = (kv_width // 2) ** -0.5
    for p in range(width // LANES):
        cols = slice(p * LANES, (p + 1) * LANES)
        lin = dot(ha, w_ref[:, cols], 1, 0) + vec[QB : QB + 1, cols]
        rot = rotate(lin, own, up, down).astype(bf16)
        q_ref[:, cols] = (rot.astype(f32) * scale).astype(bf16)
    lin = dot(ha, w_ref[:, width:c_out], 1, 0) + vec[16 + KB : 17 + KB, :kv_width]
    lane = lax.broadcasted_iota(jnp.int32, (rows, kv_width), 1)
    kv_ref[...] = jnp.where(lane < kv_width // 2, rotate(lin, own, up, down), lin).astype(bf16)
    keep = kept_rows(i, rows, len_ref[0])
    gy = (cot_ref[...].astype(f32) * keep).astype(bf16)
    gy_ref[...] = gy
    gm_ref[...] = dot(gy, w_ref[:, c_out:c_vec], 1, 1).astype(bf16)


def pre(length, x, cot, w1, tables, kv_width, shards):
    tokens, width = x.shape
    rows = 256
    blk = pl.BlockSpec((rows, width), lambda i, *_: (i, 0))
    kvb = pl.BlockSpec((rows, kv_width), lambda i, *_: (i, 0))
    dims = (width, kv_width, rows, width // shards, kv_width // shards)
    wide = jax.ShapeDtypeStruct((tokens, width), bf16)
    return pl.pallas_call(
        functools.partial(pre_kernel, dims=dims),
        grid_spec=pltpu.PrefetchScalarGridSpec(
            num_scalar_prefetch=1,
            grid=(tokens // rows,),
            in_specs=[blk, blk, whole(w1.shape), pl.BlockSpec((3, rows, LANES), lambda i, *_: (0, i, 0))],
            out_specs=[blk, kvb, blk, blk, blk, blk, whole((32, width))],
            scratch_shapes=[pltpu.VMEM((32, width), f32)],
        ),
        out_shape=[
            wide,
            jax.ShapeDtypeStruct((tokens, kv_width), bf16),
            wide,
            wide,
            wide,
            wide,
            jax.ShapeDtypeStruct((32, width), f32),
        ],
        compiler_params=params(),
        name="pre",
    )(length, x, cot, w1, tables)


def attn_kernel(len_ref, q_ref, gm_ref, kv_ref, tab_ref, mix_ref, dq_ref, dkv_ref, k0, k1, v0, v1, acc, *, qb):
    p = pl.program_id(0)
    tokens, kv_width = kv_ref.shape
    head = kv_width // 2

    @pl.when(p == 0)
    def _():
        kv = kv_ref[...]
        zero = jnp.zeros((tokens, head), bf16)
        k, v = kv[:, :head], kv[:, head:]
        k0[...] = jnp.concatenate([k, zero], 1)
        k1[...] = jnp.concatenate([zero, k], 1)
        v0[...] = jnp.concatenate([v, zero], 1)
        v1[...] = jnp.concatenate([zero, v], 1)
        acc[...] = jnp.zeros_like(acc)

    last = len_ref[0] - 1
    lane = lax.broadcasted_iota(jnp.int32, (qb, LANES), 1)
    scale = head**-0.5
    for i in range(tokens // qb):
        r = pl.ds(i * qb, qb)
        kn = (i + 1) * qb
        q, gm = q_ref[r, :], gm_ref[r, :]
        q_t, gm_t = q.T, gm.T
        col = lax.broadcasted_iota(jnp.int32, (qb, kn), 1)
        limit = jnp.minimum(lax.broadcasted_iota(jnp.int32, (qb, 1), 0) + i * qb, last)
        allowed = col <= limit
        mixed = jnp.zeros((qb, LANES), f32)
        probs = []
        for h, (k, v) in enumerate(((k0, v0), (k1, v1))):
            s = jnp.where(allowed, dot(q, k[:kn, :], 1, 1), NEG)
            e = jnp.exp(s - jnp.max(s, axis=1, keepdims=True))
            pr = e * (1.0 / jnp.sum(e, axis=1, keepdims=True))
            low = pr.astype(bf16)
            mixed = mixed + dot(low, v[:kn, :], 1, 0)
            acc[head:, :kn] += dot(gm_t[head * h : head * (h + 1), :], low, 1, 0)
            probs.append(pr)
        mix_ref[r, :] = mixed.astype(bf16)
        inner = gm.astype(f32) * mixed
        first = jnp.sum(jnp.where(lane < head, inner, 0.0), axis=1, keepdims=True)
        second = jnp.sum(jnp.where(lane < head, 0.0, inner), axis=1, keepdims=True)
        dq = jnp.zeros((qb, LANES), f32)
        for h, (k, v, row) in enumerate(((k0, v0, first), (k1, v1, second))):
            ds = (probs[h] * (dot(gm, v[:kn, :], 1, 1) - row)).astype(bf16)
            dq = dq + dot(ds, k[:kn, :], 1, 0)
            acc[:head, :kn] += dot(q_t[head * h : head * (h + 1), :], ds, 1, 0)
        dq_ref[r, :] = rotate_back(dq * scale, tab_ref[0, r, :], tab_ref[1, r, :], tab_ref[2, r, :]).astype(bf16)

    @pl.when(p == pl.num_programs(0) - 1)
    def _():
        dkv = acc[...].T
        lanes = lax.broadcasted_iota(jnp.int32, (tokens, kv_width), 1)
        back = rotate_back(dkv, tab_ref[0], tab_ref[1], tab_ref[2])
        dkv_ref[...] = jnp.where(lanes < head, back, dkv).astype(bf16)


def attention(length, q, gm, kv, tables):
    tokens, width = q.shape
    kv_width = kv.shape[1]
    blk = pl.BlockSpec((tokens, LANES), lambda p, *_: (0, p))
    wide = jax.ShapeDtypeStruct((tokens, width), bf16)
    return pl.pallas_call(
        functools.partial(attn_kernel, qb=256),
        grid_spec=pltpu.PrefetchScalarGridSpec(
            num_scalar_prefetch=1,
            grid=(width // LANES,),
            in_specs=[blk, blk, whole((tokens, kv_width)), whole((3, tokens, LANES))],
            out_specs=[blk, blk, whole((tokens, kv_width))],
            scratch_shapes=[pltpu.VMEM((tokens, LANES), bf16)] * 4 + [pltpu.VMEM((kv_width, tokens), f32)],
        ),
        out_shape=[wide, wide, jax.ShapeDtypeStruct((tokens, kv_width), bf16)],
        compiler_params=params(),
        name="attention",
    )(length, q, gm, kv, tables)


def post_kernel(len_ref, x_ref, cot_ref, ha_ref, gy_ref, mix_ref, dq_ref, dkv_ref, w_ref, vec_ref, out_ref, gt_ref, dw_ref, acc, sums, *, dims):
    width, kv_width, rows, per_row, per_kv = dims
    i = pl.program_id(0)
    c_out = width + kv_width
    c_vec = c_out + width

    @pl.when(i == 0)
    def _():
        acc[...] = jnp.zeros_like(acc)
        sums[...] = jnp.zeros_like(sums)

    keep = kept_rows(i, rows, len_ref[0])
    vec = vec_ref[...]
    x = x_ref[...].astype(f32)
    mixed, gy, ha, dq, dkv = mix_ref[...], gy_ref[...], ha_ref[...], dq_ref[...], dkv_ref[...]
    attn_out = dot(mixed, w_ref[:, c_out:c_vec], 1, 0) + vec[OB : OB + 1]
    out_ref[...] = x + keep * attn_out
    acc[:, :width] += dot(ha, dq, 0, 0)
    acc[:, width:c_out] += dot(ha, dkv, 0, 0)
    acc[:, c_out:c_vec] += dot(mixed, gy, 0, 0)
    grad = dot(dq, w_ref[:, :width], 1, 1) + dot(dkv, w_ref[:, width:c_out], 1, 1)
    normed, scaled = standardise(x)
    gt_ref[...] = cot_ref[...].astype(f32) + norm_back(grad, normed, scaled, vec[GA : GA + 1])
    sums[QB : QB + 1] += col_sum(dq.astype(f32))
    sums[OB : OB + 1] += col_sum(gy.astype(f32))
    sums[GA : GA + 1] += col_sum(grad * normed)
    sums[BA : BA + 1] += col_sum(grad)
    sums[8:9, :kv_width] += col_sum(dkv.astype(f32))

    @pl.when(i == pl.num_programs(0) - 1)
    def _():
        dw_ref[:, :c_vec] = acc[...].astype(bf16)
        spread = spread_key_bias(width, kv_width, per_row, per_kv)
        low = sums[...].astype(bf16)
        key = dot(low[8:16, :kv_width], spread, 1, 1)
        row = lax.broadcasted_iota(jnp.int32, (16, width), 0)
        both = jnp.where(row == 8, jnp.concatenate([key, key], 0), low.astype(f32))
        both = jnp.concatenate([both, jnp.zeros((LANES - 16, width), f32)], 0)
        dw_ref[:, c_vec:] = both.T.astype(bf16)


def post(length, x, cot, ha, gy, mixed, dq, dkv, w1, vec, shards):
    tokens, width = x.shape
    kv_width = dkv.shape[1]
    rows = 256
    blk = pl.BlockSpec((rows, width), lambda i, *_: (i, 0))
    kvb = pl.BlockSpec((rows, kv_width), lambda i, *_: (i, 0))
    dims = (width, kv_width, rows, width // shards, kv_width // shards)
    full = jax.ShapeDtypeStruct((tokens, width), f32)
    return pl.pallas_call(
        functools.partial(post_kernel, dims=dims),
        grid_spec=pltpu.PrefetchScalarGridSpec(
            num_scalar_prefetch=1,
            grid=(tokens // rows,),
            in_specs=[blk, blk, blk, blk, blk, blk, kvb, whole(w1.shape), whole(vec.shape)],
            out_specs=[blk, blk, whole(w1.shape)],
            scratch_shapes=[pltpu.VMEM((width, w1.shape[1] - LANES), f32), pltpu.VMEM((16, width), f32)],
        ),
        out_shape=[full, full, jax.ShapeDtypeStruct(w1.shape, bf16)],
        compiler_params=params(),
        name="post",
    )(length, x, cot, ha, gy, mixed, dq, dkv, w1, vec)


def ff_kernel(len_ref, hm_ref, gy_ref, wu_ref, wd_ref, vec_ref, x_ref, base_ref, gt_ref, out_ref, gtok_ref, dwu_ref, dwd_ref, dv_ref, act_s, gup_s, mlp, gh, sums, *, rows):
    j = pl.program_id(0)
    tokens, width = hm_ref.shape
    blocks = tokens // rows

    @pl.when(j == 0)
    def _():
        mlp[...] = jnp.zeros_like(mlp)
        gh[...] = jnp.zeros_like(gh)
        sums[...] = jnp.zeros_like(sums)

    bias = vec_ref[pl.ds(UB + j, 1), :]
    total = jnp.zeros((1, wu_ref.shape[1]), f32)
    for i in range(blocks):
        r = pl.ds(i * rows, rows)
        u = dot(hm_ref[r, :], wu_ref[...], 1, 0) + bias
        cdf = 0.5 * (1.0 + lax.erf(u * ROOT_HALF))
        pdf = jnp.exp(-0.5 * u * u) * INV_ROOT_TAU
        act = (u * cdf).astype(bf16)
        act_s[r, :] = act
        grad = (dot(gy_ref[r, :], wd_ref[...], 1, 1) * (cdf + u * pdf)).astype(bf16)
        gup_s[r, :] = grad
        total = total + col_sum(grad.astype(f32))
        mlp[r, :] += dot(act, wd_ref[...], 1, 0)
        gh[r, :] += dot(grad, wu_ref[...], 1, 1)
    sums[pl.ds(j, 1), :] = total
    dwd_ref[...] = dot(act_s[...], gy_ref[...], 0, 0).astype(bf16)
    dwu_ref[...] = dot(hm_ref[...], gup_s[...], 0, 0).astype(bf16)

    @pl.when(j == pl.num_programs(0) - 1)
    def _():
        gain = vec_ref[GM : GM + 1]
        down_bias = vec_ref[DB : DB + 1]
        d_gain = jnp.zeros((1, width), f32)
        d_shift = jnp.zeros((1, width), f32)
        for i in range(blocks):
            r = pl.ds(i * rows, rows)
            keep = kept_rows(i, rows, len_ref[0])
            out_ref[r, :] = (base_ref[r, :] + keep * (mlp[r, :] + down_bias)).astype(bf16)
            normed, scaled = standardise(x_ref[r, :].astype(f32))
            grad = gh[r, :]
            gtok_ref[r, :] = gt_ref[r, :] + norm_back(grad, normed, scaled, gain)
            d_gain = d_gain + col_sum(grad * normed)
            d_shift = d_shift + col_sum(grad)
        blocks_up = pl.num_programs(0)
        sums[4:5, :] = d_gain
        sums[5:6, :] = d_shift
        both = jnp.concatenate([sums[...], jnp.zeros((LANES - 8, width), f32)], 0)
        dv_ref[...] = both.T.astype(bf16)


def feed_forward(length, hm, gy, w2, vec, x, base, gt):
    tokens, width = x.shape
    blocks = w2.shape[1] // (2 * width)
    one = lambda s: pl.BlockSpec(s, lambda *_: (0, 0), pipeline_mode=pl.Buffered(1))
    up = pl.BlockSpec((width, width), lambda j, *_: (0, j))
    dn = pl.BlockSpec((width, width), lambda j, *_: (0, j + blocks))
    tok = (tokens, width)
    half = jax.ShapeDtypeStruct((width, blocks * width), bf16)
    return pl.pallas_call(
        functools.partial(ff_kernel, rows=256),
        grid_spec=pltpu.PrefetchScalarGridSpec(
            num_scalar_prefetch=1,
            grid=(blocks,),
            in_specs=[one(tok), one(tok), up, dn, one(vec.shape), one(tok), one(tok), one(tok)],
            out_specs=[whole(tok), whole(tok), up, up, whole((width, LANES))],
            scratch_shapes=[
                pltpu.VMEM((tokens, width), bf16),
                pltpu.VMEM((tokens, width), bf16),
                pltpu.VMEM(tok, f32),
                pltpu.VMEM(tok, f32),
                pltpu.VMEM((8, width), f32),
            ],
        ),
        out_shape=[
            jax.ShapeDtypeStruct(tok, bf16),
            jax.ShapeDtypeStruct(tok, f32),
            half,
            half,
            jax.ShapeDtypeStruct((width, LANES), bf16),
        ],
        compiler_params=params(),
        name="feed_forward",
    )(length, hm, gy, w2, w2, vec, x, base, gt)


def bits_of(axis, size):
    return [(axis, b) for b in range(size.bit_length() - 1)]


def swap(v, axis, bit):
    size = lax.axis_size(axis)
    return lax.ppermute(v, axis, [(i, i ^ (1 << bit)) for i in range(size)])


def gather_rows(v, order, index_order):
    rows, cols = v.shape
    cur = v.reshape((1,) * len(index_order) + v.shape)
    for axis, bit in order:
        got = swap(cur.reshape(-1, cols), axis, bit).reshape(cur.shape)
        here = (lax.axis_index(axis) >> bit) & 1
        where = index_order.index((axis, bit))
        low = jnp.where(here == 0, cur, got)
        high = jnp.where(here == 0, got, cur)
        cur = jnp.concatenate([low, high], where)
    return cur.reshape(-1, cols)


def body(
    tokens,
    lengths,
    cotangent,
    query_weight,
    query_bias,
    keyval_weight,
    keyval_bias,
    out_weight,
    out_bias,
    norm_attn_gain,
    norm_attn_bias,
    norm_mlp_gain,
    norm_mlp_bias,
    up_weight,
    up_bias,
    down_weight,
    down_bias,
):
    n_dp, n_fsdp = lax.axis_size("dp"), lax.axis_size("fsdp")
    shards = n_dp * n_fsdp
    rows, width = query_weight.shape
    kv_width = keyval_weight.shape[1]
    ff = up_weight.shape[1]
    blocks = ff // width
    seq_len = tokens.shape[1]
    x = tokens.reshape(seq_len, width)
    cot = cotangent.reshape(seq_len, width)

    up_local = up_weight.reshape(rows, shards, blocks, rows).transpose(0, 2, 1, 3).reshape(rows, ff)
    dn_local = down_weight.reshape(blocks, rows, width).transpose(1, 0, 2).reshape(rows, ff)
    w2 = lax.all_gather(jnp.concatenate([up_local, dn_local], 1), BOTH, axis=0, tiled=True)

    up_bias_cols = up_bias.reshape(blocks, rows)
    key_bias_col = jnp.pad(keyval_bias, (0, rows - keyval_bias.shape[0]))
    vecs = [query_bias, out_bias, norm_attn_gain, norm_attn_bias, norm_mlp_gain, norm_mlp_bias, down_bias]
    vecs = jnp.concatenate([jnp.stack(vecs), up_bias_cols, key_bias_col[None]], 0)
    vecs = jnp.pad(vecs, ((0, LANES - vecs.shape[0]), (0, 0))).T
    local = jnp.concatenate([query_weight, keyval_weight, out_weight, vecs], 1)
    dp_bits, fs_bits = bits_of("dp", n_dp), bits_of("fsdp", n_fsdp)
    index_order = dp_bits[::-1] + fs_bits[::-1]
    order = fs_bits[:0:-1] + dp_bits[:0:-1] + fs_bits[:1] + dp_bits[:1]
    w1 = gather_rows(local, order, index_order)

    tables = rotary_tables(seq_len, kv_width // 2)
    q, kv, ha, hm, gy, gm, vec = pre(lengths, x, cot, w1, tables, kv_width, shards)
    mixed, dq, dkv = attention(lengths, q, gm, kv, tables)
    base, gt, dw1 = post(lengths, x, cot, ha, gy, mixed, dq, dkv, w1, vec, shards)
    own1 = lax.psum_scatter(dw1, BOTH, scatter_dimension=0, tiled=True)
    layer_out, gtok, dwu, dwd, dv = feed_forward(lengths, hm, gy, w2, vec, x, base, gt)
    own2 = lax.psum_scatter(jnp.concatenate([dwu, dwd, dv], 1), BOTH, scatter_dimension=0, tiled=True)

    own1, own2 = own1.astype(f32), own2.astype(f32)
    c_out = width + kv_width
    c_vec = c_out + width
    v1 = own1[:, c_vec:].T
    v2 = own2[:, 2 * ff :].T
    g_up = own2[:, :ff].reshape(rows, blocks, shards, rows).transpose(0, 2, 1, 3).reshape(rows, ff)
    g_dn = own2[:, ff : 2 * ff].reshape(rows, blocks, width).transpose(1, 0, 2).reshape(blocks * rows, width)
    return (
        layer_out.reshape(tokens.shape),
        gtok.reshape(tokens.shape),
        own1[:, :width],
        v1[QB],
        own1[:, width:c_out],
        v1[8, : kv_width // shards],
        own1[:, c_out:c_vec],
        v1[OB],
        v1[GA],
        v1[BA],
        v2[4],
        v2[5],
        g_up,
        v2[:4].reshape(-1),
        g_dn,
        v1[OB],
    )


def solution(mesh):
    mat, vec, seq = P(BOTH, None), P(BOTH), P(BOTH, None, None)
    return jax.shard_map(
        body,
        mesh=mesh,
        in_specs=(seq, vec, seq, mat, vec, mat, vec, mat, vec, vec, vec, vec, vec, mat, vec, mat, vec),
        out_specs=(seq, seq, mat, vec, mat, vec, mat, vec, vec, vec, vec, vec, mat, vec, mat, vec),
        check_vma=False,
    )
```

```python
import functools

import jax
import jax.numpy as jnp
import numpy as np
from jax import lax
from jax.experimental import pallas as pl
from jax.experimental.pallas import tpu as pltpu
from jax.sharding import PartitionSpec as P

f32 = jnp.float32
bf16 = jnp.bfloat16

ROT = 16
EPS = 1e-05
NEG = -1e30
ROOT_HALF = 0.7071067811865476
INV_ROOT_TAU = 0.3989422804014327
LANES = 128
CHUNKS = (2,)
BOTH = ("dp", "fsdp")
VMEM = 60 * 1024 * 1024

QB, OB, GA, BA, GM, BM, DB, UB, KB = 0, 1, 2, 3, 4, 5, 6, 7, 11


def dot(a, b, ca, cb):
    return lax.dot_general(a, b, (((ca,), (cb,)), ((), ())), preferred_element_type=f32)


def params(**kw):
    return pltpu.CompilerParams(vmem_limit_bytes=VMEM, **kw)


def cost(us):
    return pl.CostEstimate(flops=int(us * 1.0e9), bytes_accessed=int(us * 3.0e6), transcendentals=0)


def whole(shape):
    return pl.BlockSpec(shape, lambda *_: (0,) * len(shape))


def rotary_tables(seq_len, head_dim):
    half = ROT // 2
    inverse_freq = np.float32(10000.0) ** (-(np.float32(2.0) * np.arange(half, dtype=np.float32)) / np.float32(ROT))
    angles = np.arange(seq_len, dtype=np.float32)[:, None] * inverse_freq[None, :]
    cos, sin = np.cos(angles.astype(np.float64)), np.sin(angles.astype(np.float64))
    tables = np.zeros((3, seq_len, LANES), np.float32)
    tables[0] = 1.0
    for at in range(0, LANES, head_dim):
        tables[0, :, at : at + half] = cos
        tables[0, :, at + half : at + ROT] = cos
        tables[1, :, at : at + half] = sin
        tables[2, :, at + half : at + ROT] = sin
    return jnp.asarray(tables)


def partners(v):
    half = ROT // 2
    return pltpu.roll(v, LANES - half, 1), pltpu.roll(v, half, 1)


def rotate(v, own, up, down):
    ahead, behind = partners(v)
    return v * own - ahead * up + behind * down


def rotate_back(v, own, up, down):
    ahead, behind = partners(v)
    return v * own + ahead * up - behind * down


def standardise(rows):
    average = jnp.mean(rows, axis=-1, keepdims=True)
    centred = rows - average
    scaled = lax.rsqrt(jnp.mean(centred * centred, axis=-1, keepdims=True) + EPS)
    return centred * scaled, scaled


def norm_back(grad, normed, scaled, gain):
    e = grad * gain
    return scaled * (
        e - jnp.mean(e, axis=-1, keepdims=True) - normed * jnp.mean(e * normed, axis=-1, keepdims=True)
    )


def col_sum(v):
    return jnp.sum(v, axis=0, keepdims=True)


def kept_rows(block, rows, length):
    pos = lax.broadcasted_iota(jnp.int32, (rows, 1), 0) + block * rows
    return (pos < length).astype(f32)


def spread_key_bias(width, kv_width, per_row, per_kv):
    row = lax.broadcasted_iota(jnp.int32, (width, kv_width), 0)
    col = lax.broadcasted_iota(jnp.int32, (width, kv_width), 1)
    owner = col // per_kv
    return (row == owner * per_row + (col - owner * per_kv)).astype(bf16)


def pre_kernel(len_ref, x_ref, cot_ref, w_ref, tab_ref, q_ref, kv_ref, ha_ref, hm_ref, gy_ref, gm_ref, vec_ref, vec_s, *, dims):
    width, kv_width, rows, per_row, per_kv = dims
    i = pl.program_id(0)
    c_out = width + kv_width
    c_vec = c_out + width

    @pl.when(i == 0)
    def _():
        low = w_ref[:, c_vec : c_vec + LANES]
        lines = low.astype(f32).T[:16]
        vec_s[:16, :] = lines
        spread = spread_key_bias(width, kv_width, per_row, per_kv)
        vec_s[16:32, :kv_width] = dot(lines.astype(bf16), spread, 1, 0)
        vec_ref[...] = vec_s[...]

    normed, _ = standardise(x_ref[...].astype(f32))
    vec = vec_s[...]
    ha = (normed * vec[GA : GA + 1] + vec[BA : BA + 1]).astype(bf16)
    hm = (normed * vec[GM : GM + 1] + vec[BM : BM + 1]).astype(bf16)
    ha_ref[...] = ha
    hm_ref[...] = hm
    own, up, down = tab_ref[0], tab_ref[1], tab_ref[2]
    scale = (kv_width // 2) ** -0.5
    lin = dot(ha, w_ref[:, :c_out], 1, 0)
    query = lin[:, :width] + vec[QB : QB + 1]
    for p in range(width // LANES):
        cols = slice(p * LANES, (p + 1) * LANES)
        rot = rotate(query[:, cols], own, up, down).astype(bf16)
        q_ref[:, cols] = (rot.astype(f32) * scale).astype(bf16)
    lin = lin[:, width:] + vec[16 + KB : 17 + KB, :kv_width]
    lane = lax.broadcasted_iota(jnp.int32, (rows, kv_width), 1)
    kv_ref[...] = jnp.where(lane < kv_width // 2, rotate(lin, own, up, down), lin).astype(bf16)
    keep = kept_rows(i, rows, len_ref[0])
    gy = (cot_ref[...].astype(f32) * keep).astype(bf16)
    gy_ref[...] = gy
    gm_ref[...] = dot(gy, w_ref[:, c_out:c_vec], 1, 1).astype(bf16)


def pre(length, x, cot, w1, tables, kv_width, shards):
    tokens, width = x.shape
    rows = 256
    blk = pl.BlockSpec((rows, width), lambda i, *_: (i, 0))
    kvb = pl.BlockSpec((rows, kv_width), lambda i, *_: (i, 0))
    dims = (width, kv_width, rows, width // shards, kv_width // shards)
    wide = jax.ShapeDtypeStruct((tokens, width), bf16)
    return pl.pallas_call(
        functools.partial(pre_kernel, dims=dims),
        grid_spec=pltpu.PrefetchScalarGridSpec(
            num_scalar_prefetch=1,
            grid=(tokens // rows,),
            in_specs=[blk, blk, whole(w1.shape), pl.BlockSpec((3, rows, LANES), lambda i, *_: (0, i, 0))],
            out_specs=[blk, kvb, blk, blk, blk, blk, whole((32, width))],
            scratch_shapes=[pltpu.VMEM((32, width), f32)],
        ),
        out_shape=[
            wide,
            jax.ShapeDtypeStruct((tokens, kv_width), bf16),
            wide,
            wide,
            wide,
            wide,
            jax.ShapeDtypeStruct((32, width), f32),
        ],
        compiler_params=params(),
        cost_estimate=cost(9),
        name="pre",
    )(length, x, cot, w1, tables)


def attn_kernel(len_ref, q_ref, gm_ref, kv_ref, tab_ref, mix_ref, dq_ref, dkv_ref, k0, k1, v0, v1, acc, *, qb):
    p = pl.program_id(0)
    tokens, kv_width = kv_ref.shape
    head = kv_width // 2

    @pl.when(p == 0)
    def _():
        kv = kv_ref[...]
        zero = jnp.zeros((tokens, head), bf16)
        k, v = kv[:, :head], kv[:, head:]
        k0[...] = jnp.concatenate([k, zero], 1)
        k1[...] = jnp.concatenate([zero, k], 1)
        v0[...] = jnp.concatenate([v, zero], 1)
        v1[...] = jnp.concatenate([zero, v], 1)
        acc[...] = jnp.zeros_like(acc)

    last = len_ref[0] - 1
    lane = lax.broadcasted_iota(jnp.int32, (qb, LANES), 1)
    scale = head**-0.5
    for i in range(tokens // qb):
        r = pl.ds(i * qb, qb)
        kn = (i + 1) * qb
        q, gm = q_ref[r, :], gm_ref[r, :]
        q_t, gm_t = q.T, gm.T
        col = lax.broadcasted_iota(jnp.int32, (qb, kn), 1)
        limit = jnp.minimum(lax.broadcasted_iota(jnp.int32, (qb, 1), 0) + i * qb, last)
        allowed = col <= limit
        mixed = jnp.zeros((qb, LANES), f32)
        probs = []
        for h, (k, v) in enumerate(((k0, v0), (k1, v1))):
            s = jnp.where(allowed, dot(q, k[:kn, :], 1, 1), NEG)
            e = jnp.exp(s - jnp.max(s, axis=1, keepdims=True))
            pr = e * (1.0 / jnp.sum(e, axis=1, keepdims=True))
            low = pr.astype(bf16)
            mixed = mixed + dot(low, v[:kn, :], 1, 0)
            acc[head:, :kn] += dot(gm_t[head * h : head * (h + 1), :], low, 1, 0)
            probs.append(pr)
        mix_ref[r, :] = mixed.astype(bf16)
        inner = gm.astype(f32) * mixed
        first = jnp.sum(jnp.where(lane < head, inner, 0.0), axis=1, keepdims=True)
        second = jnp.sum(jnp.where(lane < head, 0.0, inner), axis=1, keepdims=True)
        dq = jnp.zeros((qb, LANES), f32)
        for h, (k, v, row) in enumerate(((k0, v0, first), (k1, v1, second))):
            ds = (probs[h] * (dot(gm, v[:kn, :], 1, 1) - row)).astype(bf16)
            dq = dq + dot(ds, k[:kn, :], 1, 0)
            acc[:head, :kn] += dot(q_t[head * h : head * (h + 1), :], ds, 1, 0)
        dq_ref[r, :] = rotate_back(dq * scale, tab_ref[0, r, :], tab_ref[1, r, :], tab_ref[2, r, :]).astype(bf16)

    @pl.when(p == pl.num_programs(0) - 1)
    def _():
        dkv = acc[...].T
        lanes = lax.broadcasted_iota(jnp.int32, (tokens, kv_width), 1)
        back = rotate_back(dkv, tab_ref[0], tab_ref[1], tab_ref[2])
        dkv_ref[...] = jnp.where(lanes < head, back, dkv).astype(bf16)


def attention(length, q, gm, kv, tables):
    tokens, width = q.shape
    kv_width = kv.shape[1]
    blk = pl.BlockSpec((tokens, LANES), lambda p, *_: (0, p))
    wide = jax.ShapeDtypeStruct((tokens, width), bf16)
    return pl.pallas_call(
        functools.partial(attn_kernel, qb=256),
        grid_spec=pltpu.PrefetchScalarGridSpec(
            num_scalar_prefetch=1,
            grid=(width // LANES,),
            in_specs=[blk, blk, whole((tokens, kv_width)), whole((3, tokens, LANES))],
            out_specs=[blk, blk, whole((tokens, kv_width))],
            scratch_shapes=[pltpu.VMEM((tokens, LANES), bf16)] * 4 + [pltpu.VMEM((kv_width, tokens), f32)],
        ),
        out_shape=[wide, wide, jax.ShapeDtypeStruct((tokens, kv_width), bf16)],
        compiler_params=params(),
        cost_estimate=cost(47),
        name="attention",
    )(length, q, gm, kv, tables)


def split_halves(send_ref, keep_ref, low_s, cols, at, core, half):
    for g in range(low_s.shape[0] // (2 * half)):
        to, base = pl.ds(g * half, half), g * 2 * half
        send_ref[to, at] = low_s[pl.ds(pl.multiple_of(base + (1 - core) * half, half), half), :cols]
        keep_ref[to, at] = low_s[pl.ds(pl.multiple_of(base + core * half, half), half), :cols]


def row_sum(v):
    return jnp.sum(v, axis=1, keepdims=True)


def grads_kernel(info, ha_ref, gy_ref, mix_ref, dq_ref, dkv_ref, w_ref, send_ref, keep_ref, acc, sums, low_s, *, dims, half):
    width, kv_width, rows, per_row, per_kv = dims
    i = pl.program_id(0)
    c_out = width + kv_width
    c_vec = c_out + width

    @pl.when(i == 0)
    def _():
        acc[...] = jnp.zeros_like(acc)
        sums[...] = jnp.zeros_like(sums)

    gy, ha, dq, dkv = gy_ref[...], ha_ref[...], dq_ref[...], dkv_ref[...]
    acc[:, :width] += dot(ha, dq, 0, 0)
    acc[:, width:c_out] += dot(ha, dkv, 0, 0)
    acc[:, c_out:c_vec] += dot(mix_ref[...], gy, 0, 0)
    sums[QB : QB + 1] += col_sum(dq.astype(f32))
    sums[OB : OB + 1] += col_sum(gy.astype(f32))
    sums[8:9, :kv_width] += col_sum(dkv.astype(f32))

    @pl.when(i == pl.num_programs(0) - 1)
    def _():
        w_q, w_kv = w_ref[:, :width].astype(f32), w_ref[:, width:c_out].astype(f32)
        shift = row_sum(w_q * sums[QB : QB + 1]) + row_sum(w_kv * sums[8:9, :kv_width])
        inner = row_sum(w_q * acc[:, :width]) + row_sum(w_kv * acc[:, width:c_out])
        vec = w_ref[:, c_vec:].astype(f32)
        gain = (inner - vec[:, BA : BA + 1] * shift) / vec[:, GA : GA + 1]
        low_s[:, :c_vec] = acc[...].astype(bf16)
        spread = spread_key_bias(width, kv_width, per_row, per_kv)
        low = sums[...].astype(bf16)
        key = dot(low[8:16, :kv_width], spread, 1, 1)
        row = lax.broadcasted_iota(jnp.int32, (16, width), 0)
        both = jnp.where(row == 8, jnp.concatenate([key, key], 0), low.astype(f32))
        both = jnp.concatenate([both, jnp.zeros((LANES - 16, width), f32)], 0).T
        lane = lax.broadcasted_iota(jnp.int32, (width, LANES), 1)
        both = jnp.where(lane == GA, gain, jnp.where(lane == BA, shift, both))
        low_s[:, c_vec:] = both.astype(bf16)
        split_halves(send_ref, keep_ref, low_s, c_vec + LANES, slice(None), info[1], half)


def attention_grads(info, ha, gy, mixed, dq, dkv, w1, shards, half):
    tokens, width = ha.shape
    kv_width = dkv.shape[1]
    rows = 256
    blk = pl.BlockSpec((rows, width), lambda i, *_: (i, 0))
    kvb = pl.BlockSpec((rows, kv_width), lambda i, *_: (i, 0))
    dims = (width, kv_width, rows, width // shards, kv_width // shards)
    cut = (width // 2, w1.shape[1])
    return pl.pallas_call(
        functools.partial(grads_kernel, dims=dims, half=half),
        grid_spec=pltpu.PrefetchScalarGridSpec(
            num_scalar_prefetch=1,
            grid=(tokens // rows,),
            in_specs=[blk, blk, blk, blk, kvb, whole(w1.shape)],
            out_specs=[whole(cut), whole(cut)],
            scratch_shapes=[
                pltpu.VMEM((width, w1.shape[1] - LANES), f32),
                pltpu.VMEM((16, width), f32),
                pltpu.VMEM(w1.shape, bf16),
            ],
        ),
        out_shape=[jax.ShapeDtypeStruct(cut, bf16)] * 2,
        compiler_params=params(),
        cost_estimate=cost(8),
        name="attention_grads",
    )(info, ha, gy, mixed, dq, dkv, w1)


SHIFT, INNER = 8, 9


def ff_kernel(*refs, rows, chunk, first, final, half):
    refs = list(refs)
    take = lambda k: [refs.pop(0) for _ in range(k)]
    info, hm_ref, gy_ref, wu_ref, wd_ref, vec_ref = take(6)
    (col_in,) = (None,) if first else take(1)
    (vcol_ref,) = take(1) if final else (None,)
    act_ref, gup_ref = take(2)
    (col_out,) = (None,) if final else take(1)
    send_ref, keep_ref, cols, low_s = refs
    j = pl.program_id(0)
    tokens, width = hm_ref.shape

    @pl.when(j == 0)
    def _():
        cols[...] = jnp.zeros_like(cols) if first else col_in[...]

    bias = vec_ref[pl.ds(UB + chunk + j, 1), :]
    total = jnp.zeros((1, width), f32)
    for i in range(tokens // rows):
        r = pl.ds(i * rows, rows)
        u = dot(hm_ref[r, :], wu_ref[...], 1, 0) + bias
        cdf = 0.5 * (1.0 + lax.erf(u * ROOT_HALF))
        pdf = jnp.exp(-0.5 * u * u) * INV_ROOT_TAU
        act_ref[r, :] = (u * cdf).astype(bf16)
        grad = (dot(gy_ref[r, :], wd_ref[...], 1, 1) * (cdf + u * pdf)).astype(bf16)
        gup_ref[r, :] = grad
        total = total + col_sum(grad.astype(f32))
    at = pl.multiple_of(j * 2 * width, LANES)
    d_up = dot(hm_ref[...], gup_ref[...], 0, 0)
    low_s[...] = d_up.astype(bf16)
    w_up = wu_ref[...].astype(f32)
    lane = lax.broadcasted_iota(jnp.int32, (width, LANES), 1)
    mine = jnp.where(lane == chunk + j, jnp.broadcast_to(total, (LANES, width)).T, 0.0)
    mine = jnp.where(lane == SHIFT, row_sum(w_up * total), mine)
    cols[...] += jnp.where(lane == INNER, row_sum(w_up * d_up), mine)
    split_halves(send_ref, keep_ref, low_s, width, pl.ds(at, width), info[1], half)
    low_s[...] = dot(act_ref[...], gy_ref[...], 0, 0).astype(bf16)
    at = pl.multiple_of(at + width, LANES)
    split_halves(send_ref, keep_ref, low_s, width, pl.ds(at, width), info[1], half)

    @pl.when(j == pl.num_programs(0) - 1)
    def _():
        if not final:
            col_out[...] = cols[...]
            return
        vec = vcol_ref[...].astype(f32)
        now = cols[...]
        gain = (now[:, INNER : INNER + 1] - vec[:, BM : BM + 1] * now[:, SHIFT : SHIFT + 1]) / vec[:, GM : GM + 1]
        low_s[:, :LANES] = jnp.where(lane == INNER, gain, now).astype(bf16)
        at = pl.ds(send_ref.shape[1] - LANES, LANES)
        split_halves(send_ref, keep_ref, low_s, LANES, at, info[1], half)


def feed_forward(info, hm, gy, w2, vec, w1, state, chunk, count, half):
    tokens, width = hm.shape
    blocks = w2.shape[1] // (2 * width)
    tok = (tokens, width)
    first, final = state is None, chunk + count == blocks
    one = lambda s: pl.BlockSpec(s, lambda *_: (0, 0), pipeline_mode=pl.Buffered(1))
    col = pl.BlockSpec(tok, lambda j, *_: (0, j))
    up = pl.BlockSpec((width, width), lambda j, *_: (0, j + chunk))
    dn = pl.BlockSpec((width, width), lambda j, *_: (0, j + chunk + blocks))
    args = [hm, gy, w2, w2, vec]
    specs = [one(tok), one(tok), up, dn, one(vec.shape)]
    last = w1.shape[1] // LANES - 1
    if not first:
        args += [state]
        specs += [one((width, LANES))]
    if final:
        args += [w1]
        specs += [pl.BlockSpec((width, LANES), lambda *_: (0, last), pipeline_mode=pl.Buffered(1))]
    long = jax.ShapeDtypeStruct((tokens, count * width), bf16)
    shapes, outs = [long, long], [col, col]
    if not final:
        shapes += [jax.ShapeDtypeStruct((width, LANES), f32)]
        outs += [one((width, LANES))]
    cut = (width // 2, count * 2 * width + (LANES if final else 0))
    shapes += [jax.ShapeDtypeStruct(cut, bf16)] * 2
    outs += [one(cut)] * 2
    got = pl.pallas_call(
        functools.partial(ff_kernel, rows=256, chunk=chunk, first=first, final=final, half=half),
        grid_spec=pltpu.PrefetchScalarGridSpec(
            num_scalar_prefetch=1,
            grid=(count,),
            in_specs=specs,
            out_specs=outs,
            scratch_shapes=[pltpu.VMEM((width, LANES), f32), pltpu.VMEM((width, width), bf16)],
        ),
        out_shape=shapes,
        compiler_params=params(),
        cost_estimate=cost(7 * count),
        name="feed_forward",
    )(info, *args)
    act, gup = got[:2]
    return act, gup, None if final else got[2], got[-2], got[-1]


def out_kernel(*refs, pieces, c_out, rows):
    info, x_ref, mix_ref, w1_ref, wd_ref, vec_ref = refs[:6]
    acts, out_ref = refs[6:-1], refs[-1]
    width = x_ref.shape[1]
    total = dot(mix_ref[...], w1_ref[:, c_out : c_out + width], 1, 0) + vec_ref[OB : OB + 1] + vec_ref[DB : DB + 1]
    at = 0
    for act_ref, count in zip(acts, pieces):
        for k in range(count):
            act = act_ref[:, k * width : (k + 1) * width]
            total = total + dot(act, wd_ref[:, at : at + width], 1, 0)
            at += width
    keep = kept_rows(pl.program_id(0), rows, info[0])
    out_ref[...] = (x_ref[...].astype(f32) + keep * total).astype(bf16)


def layer_output(info, x, mixed, w1, w2, vec, acts, c_out):
    tokens, width = x.shape
    rows = 256
    half = w2.shape[1] // 2
    blk = lambda n: pl.BlockSpec((rows, n), lambda i, *_: (i, 0))
    one = lambda s, *at: pl.BlockSpec(s, lambda *_: at, pipeline_mode=pl.Buffered(1))
    return pl.pallas_call(
        functools.partial(out_kernel, pieces=[a.shape[1] // width for a in acts], c_out=c_out, rows=rows),
        grid_spec=pltpu.PrefetchScalarGridSpec(
            num_scalar_prefetch=1,
            grid=(tokens // rows,),
            in_specs=[blk(width), blk(width), one(w1.shape, 0, 0), one((width, half), 0, 1), one(vec.shape, 0, 0)]
            + [blk(a.shape[1]) for a in acts],
            out_specs=blk(width),
        ),
        out_shape=jax.ShapeDtypeStruct((tokens, width), bf16),
        compiler_params=params(),
        cost_estimate=cost(9),
        name="layer_output",
    )(info, x, mixed, w1, w2, vec, *acts)


def token_kernel(*refs, pieces, kv_width):
    x_ref, cot_ref, dq_ref, dkv_ref, w1_ref, wu_ref, vec_ref = refs[:7]
    gups, out_ref = refs[7:-1], refs[-1]
    width = x_ref.shape[1]
    normed, scaled = standardise(x_ref[...].astype(f32))
    grad = dot(dq_ref[...], w1_ref[:, :width], 1, 1) + dot(dkv_ref[...], w1_ref[:, width : width + kv_width], 1, 1)
    total = norm_back(grad, normed, scaled, vec_ref[GA : GA + 1])
    at, grad = 0, None
    for gup_ref, count in zip(gups, pieces):
        part = dot(gup_ref[...], wu_ref[:, at : at + count * width], 1, 1)
        grad = part if grad is None else grad + part
        at += count * width
    total = total + norm_back(grad, normed, scaled, vec_ref[GM : GM + 1])
    out_ref[...] = cot_ref[...].astype(f32) + total


def token_grads(x, cot, dq, dkv, w1, w2, vec, gups):
    tokens, width = x.shape
    rows = 256
    half = w2.shape[1] // 2
    blk = lambda n: pl.BlockSpec((rows, n), lambda i: (i, 0))
    one = lambda s: pl.BlockSpec(s, lambda *_: (0, 0), pipeline_mode=pl.Buffered(1))
    return pl.pallas_call(
        functools.partial(token_kernel, pieces=[g.shape[1] // width for g in gups], kv_width=dkv.shape[1]),
        grid=(tokens // rows,),
        in_specs=[blk(width), blk(width), blk(width), blk(dkv.shape[1]), one(w1.shape), one((width, half)), one(vec.shape)]
        + [blk(g.shape[1]) for g in gups],
        out_specs=blk(width),
        out_shape=jax.ShapeDtypeStruct((tokens, width), f32),
        compiler_params=params(),
        cost_estimate=cost(11),
        name="token_grads",
    )(x, cot, dq, dkv, w1, w2, vec, *gups)


def bits_of(axis, size):
    return [(axis, b) for b in range(size.bit_length() - 1)]


def swap(v, axis, bit):
    size = lax.axis_size(axis)
    return lax.ppermute(v, axis, [(i, i ^ (1 << bit)) for i in range(size)])


def gather_rows(v, order, index_order):
    rows, cols = v.shape
    cur = v.reshape((1,) * len(index_order) + v.shape)
    for axis, bit in order:
        got = swap(cur.reshape(-1, cols), axis, bit).reshape(cur.shape)
        here = (lax.axis_index(axis) >> bit) & 1
        where = index_order.index((axis, bit))
        low = jnp.where(here == 0, cur, got)
        high = jnp.where(here == 0, got, cur)
        cur = jnp.concatenate([low, high], where)
    return cur.reshape(-1, cols)


def add(a, b):
    return (a.astype(f32) + b.astype(f32)).astype(bf16)


def tie(*values):
    return lax.optimization_barrier(values)


class Scatter:
    def __init__(self, send, keep, orders, tail, index_order):
        self.index_order = index_order
        self.cols = send.shape[1]
        dims = [1 if b == ("dp", 0) else 2 for b in index_order]
        self.shape = (*dims, send.shape[0] >> (len(index_order) - 1), self.cols)
        self.steps = [[("dp", 0)]] + [list(s) for s in zip(*orders)] + [[b] for b in tail]
        self.pending = [(send, keep.reshape(self.shape))]
        self.flying = None
        self.result = None

    def ready(self):
        return [send for send, _ in self.pending]

    def start(self):
        bits = self.steps.pop(0)
        self.flying = [(swap(send, *bit), keep) for (send, keep), bit in zip(self.pending, bits)]

    def arrived(self):
        return [got for got, _ in self.flying]

    def finish(self, arrived):
        parts = [add(keep, got.reshape(keep.shape)) for got, (_, keep) in zip(arrived, self.flying)]
        if not self.steps:
            (part,) = parts
            self.result = part.reshape(-1, self.cols)
            return
        bits = self.steps[0]
        if len(parts) > len(bits):
            parts = [jnp.concatenate(parts, -1)]
        if len(parts) < len(bits):
            (part,) = parts
            step = self.cols // LANES // len(bits) * LANES
            edges = [k * step for k in range(len(bits))] + [self.cols]
            parts = [part[..., lo:hi] for lo, hi in zip(edges, edges[1:])]
        self.pending = []
        for part, (axis, bit) in zip(parts, bits):
            here, where = (lax.axis_index(axis) >> bit) & 1, self.index_order.index((axis, bit))
            send = lax.dynamic_slice_in_dim(part, 1 - here, 1, where)
            keep = lax.dynamic_slice_in_dim(part, here, 1, where)
            self.pending.append((send.reshape(-1, part.shape[-1]), keep))


def beside(streams, work, *inputs):
    streams = [s for s in streams if s.result is None]
    ready = [s.ready() for s in streams]
    ready, inputs = tie(ready, inputs)
    for stream, sends in zip(streams, ready):
        stream.pending = [(send, keep) for send, (_, keep) in zip(sends, stream.pending)]
        stream.start()
    out = work(*inputs)
    arrived, out = tie([s.arrived() for s in streams], out)
    for stream, a in zip(streams, arrived):
        stream.finish(a)
    return out


def body(
    tokens,
    lengths,
    cotangent,
    query_weight,
    query_bias,
    keyval_weight,
    keyval_bias,
    out_weight,
    out_bias,
    norm_attn_gain,
    norm_attn_bias,
    norm_mlp_gain,
    norm_mlp_bias,
    up_weight,
    up_bias,
    down_weight,
    down_bias,
):
    n_dp, n_fsdp = lax.axis_size("dp"), lax.axis_size("fsdp")
    shards = n_dp * n_fsdp
    rows, width = query_weight.shape
    kv_width = keyval_weight.shape[1]
    ff = up_weight.shape[1]
    blocks = ff // width
    seq_len = tokens.shape[1]
    x = tokens.reshape(seq_len, width)
    cot = cotangent.reshape(seq_len, width)

    up_local = up_weight.reshape(rows, shards, blocks, rows).transpose(0, 2, 1, 3).reshape(rows, ff)
    dn_local = down_weight.reshape(blocks, rows, width).transpose(1, 0, 2).reshape(rows, ff)
    w2 = lax.all_gather(jnp.concatenate([up_local, dn_local], 1), BOTH, axis=0, tiled=True)

    up_bias_cols = up_bias.reshape(blocks, rows)
    key_bias_col = jnp.pad(keyval_bias, (0, rows - keyval_bias.shape[0]))
    vecs = [query_bias, out_bias, norm_attn_gain, norm_attn_bias, norm_mlp_gain, norm_mlp_bias, down_bias]
    vecs = jnp.concatenate([jnp.stack(vecs), up_bias_cols, key_bias_col[None]], 0)
    vecs = jnp.pad(vecs, ((0, LANES - vecs.shape[0]), (0, 0))).T
    local = jnp.concatenate([query_weight, keyval_weight, out_weight, vecs], 1)
    dp_bits, fs_bits = bits_of("dp", n_dp), bits_of("fsdp", n_fsdp)
    index_order = dp_bits[::-1] + fs_bits[::-1]
    order = fs_bits[:0:-1] + dp_bits[:0:-1] + fs_bits[:1] + dp_bits[:1]
    w1 = gather_rows(local, order, index_order)

    tables = rotary_tables(seq_len, kv_width // 2)
    q, kv, ha, hm, gy, gm, vec = pre(lengths, x, cot, w1, tables, kv_width, shards)
    mixed, dq, dkv = attention(lengths, q, gm, kv, tables)
    half = rows * n_fsdp
    core = lax.axis_index("dp") & 1
    info = jnp.concatenate([lengths, core[None].astype(jnp.int32)])
    x_bits, y_bits, z_bits = fs_bits[:1], dp_bits[1:], fs_bits[1:]
    send, keep = attention_grads(info, ha, gy, mixed, dq, dkv, w1, shards, half)
    attn = Scatter(send, keep, [z_bits], x_bits + y_bits, index_order)
    xy = [x_bits + y_bits, y_bits + x_bits]

    hm, gy = beside([attn], lambda *v: v, hm, gy)
    n0 = CHUNKS[0]
    act0, gup0, state, send, keep = beside(
        [attn], lambda hm, gy: feed_forward(info, hm, gy, w2, vec, w1, None, 0, n0, half), hm, gy
    )
    ff0 = Scatter(send, keep, xy, z_bits, index_order)
    n1 = blocks - n0
    act1, gup1, _, send, keep = beside(
        [attn, ff0], lambda hm, gy, state: feed_forward(info, hm, gy, w2, vec, w1, state, n0, n1, half), hm, gy, state
    )
    ff1 = Scatter(send, keep, xy, z_bits, index_order)
    layer_out = beside(
        [ff1, ff0, attn], lambda x, *acts: layer_output(info, x, mixed, w1, w2, vec, acts, width + kv_width), x, act0, act1
    )
    gtok = beside(
        [ff0, ff1, attn], lambda cot, *gups: token_grads(x, cot, dq, dkv, w1, w2, vec, gups), cot, gup0, gup1
    )
    while any(s.result is None for s in (attn, ff0, ff1)):
        beside([ff0, ff1, attn], lambda *v: v)
    own1, own_a, own_b = attn.result, ff0.result, ff1.result
    own_v = own_b[:, -LANES:]
    pieces = [own_a.reshape(rows, n0, 2, width), own_b[:, : n1 * 2 * width].reshape(rows, n1, 2, width)]
    pieces = jnp.concatenate(pieces, 1).astype(f32)

    own1 = own1.astype(f32)
    c_out = width + kv_width
    c_vec = c_out + width
    v1 = own1[:, c_vec:].T
    v2 = own_v.astype(f32).T
    g_up = pieces[:, :, 0].reshape(rows, blocks, shards, rows).transpose(0, 2, 1, 3).reshape(rows, ff)
    g_dn = pieces[:, :, 1].transpose(1, 0, 2).reshape(blocks * rows, width)
    return (
        layer_out.reshape(tokens.shape),
        gtok.reshape(tokens.shape),
        own1[:, :width],
        v1[QB],
        own1[:, width:c_out],
        v1[8, : kv_width // shards],
        own1[:, c_out:c_vec],
        v1[OB],
        v1[GA],
        v1[BA],
        v2[INNER],
        v2[SHIFT],
        g_up,
        v2[:4].reshape(-1),
        g_dn,
        v1[OB],
    )


def solution(mesh):
    mat, vec, seq = P(BOTH, None), P(BOTH), P(BOTH, None, None)
    return jax.shard_map(
        body,
        mesh=mesh,
        in_specs=(seq, vec, seq, mat, vec, mat, vec, mat, vec, vec, vec, vec, vec, mat, vec, mat, vec),
        out_specs=(seq, seq, mat, vec, mat, vec, mat, vec, vec, vec, vec, vec, mat, vec, mat, vec),
        check_vma=False,
    )
```

```python
import functools

import jax
import jax.numpy as jnp
import numpy as np
from jax import lax
from jax.experimental import pallas as pl
from jax.experimental.pallas import tpu as pltpu
from jax.sharding import PartitionSpec as P

f32 = jnp.float32
bf16 = jnp.bfloat16

ROT = 16
EPS = 1e-05
NEG = -1e30
ROOT_HALF = 0.7071067811865476
INV_ROOT_TAU = 0.3989422804014327
LANES = 128
BOTH = ("dp", "fsdp")
VMEM = 24 * 1024 * 1024

SHIFT, INNER = 8, 9
QB, OB, GA, BA, GM, BM, DB, UB, KB = 0, 1, 2, 3, 4, 5, 6, 7, 11


def dot(a, b, ca, cb):
    return lax.dot_general(a, b, (((ca,), (cb,)), ((), ())), preferred_element_type=f32)


def params(**kw):
    return pltpu.CompilerParams(vmem_limit_bytes=VMEM, **kw)


def cost(us):
    return pl.CostEstimate(flops=int(us * 1.0e9), bytes_accessed=int(us * 3.0e6), transcendentals=0)


def whole(shape):
    return pl.BlockSpec(shape, lambda *_: (0,) * len(shape))


def rotary_tables(seq_len, head_dim):
    half = ROT // 2
    inverse_freq = np.float32(10000.0) ** (-(np.float32(2.0) * np.arange(half, dtype=np.float32)) / np.float32(ROT))
    angles = np.arange(seq_len, dtype=np.float32)[:, None] * inverse_freq[None, :]
    cos, sin = np.cos(angles.astype(np.float64)), np.sin(angles.astype(np.float64))
    tables = np.zeros((3, seq_len, LANES), np.float32)
    tables[0] = 1.0
    for at in range(0, LANES, head_dim):
        tables[0, :, at : at + half] = cos
        tables[0, :, at + half : at + ROT] = cos
        tables[1, :, at : at + half] = sin
        tables[2, :, at + half : at + ROT] = sin
    return jnp.asarray(tables)


def partners(v):
    half = ROT // 2
    return pltpu.roll(v, LANES - half, 1), pltpu.roll(v, half, 1)


def rotate(v, own, up, down):
    ahead, behind = partners(v)
    return v * own - ahead * up + behind * down


def rotate_back(v, own, up, down):
    ahead, behind = partners(v)
    return v * own + ahead * up - behind * down


def standardise(rows):
    average = jnp.mean(rows, axis=-1, keepdims=True)
    centred = rows - average
    scaled = lax.rsqrt(jnp.mean(centred * centred, axis=-1, keepdims=True) + EPS)
    return centred * scaled, scaled


def norm_back(grad, normed, scaled, gain):
    e = grad * gain
    return scaled * (
        e - jnp.mean(e, axis=-1, keepdims=True) - normed * jnp.mean(e * normed, axis=-1, keepdims=True)
    )


def col_sum(v):
    return jnp.sum(v, axis=0, keepdims=True)


def kept_rows(block, rows, length):
    pos = lax.broadcasted_iota(jnp.int32, (rows, 1), 0) + block * rows
    return (pos < length).astype(f32)


def spread_key_bias(width, kv_width, per_row, per_kv):
    row = lax.broadcasted_iota(jnp.int32, (width, kv_width), 0)
    col = lax.broadcasted_iota(jnp.int32, (width, kv_width), 1)
    owner = col // per_kv
    return (row == owner * per_row + (col - owner * per_kv)).astype(bf16)


def assemble(to, at, mine, other, core, half):
    for g in range(to.shape[0] // (2 * half)):
        rows, base = slice(g * half, (g + 1) * half), g * 2 * half
        to[pl.ds(pl.multiple_of(base + core * half, half), half), at] = mine[rows, :]
        to[pl.ds(pl.multiple_of(base + (1 - core) * half, half), half), at] = other[rows, :]


def pre_kernel(info, x_ref, cot_ref, a0, a1, b0, b1, tab_ref, q_ref, kv_ref, ha_ref, hm_ref, gy_ref, gm_ref, vec_ref, w_ref, vec_s, *, dims, half):
    width, kv_width, rows, per_row, per_kv = dims
    i = pl.program_id(0)
    c_out = width + kv_width
    c_vec = c_out + width

    @pl.when(i == 0)
    def _():
        assemble(w_ref, slice(0, c_out), a0, a1, info[1], half)
        assemble(w_ref, slice(c_out, c_vec + LANES), b0, b1, info[1], half)
        low = w_ref[:, c_vec : c_vec + LANES]
        lines = low.astype(f32).T[:16]
        vec_s[:16, :] = lines
        spread = spread_key_bias(width, kv_width, per_row, per_kv)
        vec_s[16:32, :kv_width] = dot(lines.astype(bf16), spread, 1, 0)
        vec_ref[...] = vec_s[...]

    normed, _ = standardise(x_ref[...].astype(f32))
    vec = vec_s[...]
    ha = (normed * vec[GA : GA + 1] + vec[BA : BA + 1]).astype(bf16)
    hm = (normed * vec[GM : GM + 1] + vec[BM : BM + 1]).astype(bf16)
    ha_ref[...] = ha
    hm_ref[...] = hm
    own, up, down = tab_ref[0], tab_ref[1], tab_ref[2]
    scale = (kv_width // 2) ** -0.5
    lin = dot(ha, w_ref[:, :c_out], 1, 0)
    query = lin[:, :width] + vec[QB : QB + 1]
    for p in range(width // LANES):
        cols = slice(p * LANES, (p + 1) * LANES)
        rot = rotate(query[:, cols], own, up, down).astype(bf16)
        q_ref[:, cols] = (rot.astype(f32) * scale).astype(bf16)
    lin = lin[:, width:] + vec[16 + KB : 17 + KB, :kv_width]
    lane = lax.broadcasted_iota(jnp.int32, (rows, kv_width), 1)
    kv_ref[...] = jnp.where(lane < kv_width // 2, rotate(lin, own, up, down), lin).astype(bf16)
    keep = kept_rows(i, rows, info[0])
    gy = (cot_ref[...].astype(f32) * keep).astype(bf16)
    gy_ref[...] = gy
    gm_ref[...] = dot(gy, w_ref[:, c_out:c_vec], 1, 1).astype(bf16)


def pre(info, x, cot, a, b, tables, kv_width, shards, half):
    tokens, width = x.shape
    rows = 256
    blk = pl.BlockSpec((rows, width), lambda i, *_: (i, 0))
    kvb = pl.BlockSpec((rows, kv_width), lambda i, *_: (i, 0))
    dims = (width, kv_width, rows, width // shards, kv_width // shards)
    wide = jax.ShapeDtypeStruct((tokens, width), bf16)
    one = lambda v: pl.BlockSpec(v.shape, lambda *_: (0, 0), pipeline_mode=pl.Buffered(1))
    w1 = (width, 2 * width + kv_width + LANES)
    return pl.pallas_call(
        functools.partial(pre_kernel, dims=dims, half=half),
        grid_spec=pltpu.PrefetchScalarGridSpec(
            num_scalar_prefetch=1,
            grid=(tokens // rows,),
            in_specs=[blk, blk, one(a[0]), one(a[1]), one(b[0]), one(b[1])]
            + [pl.BlockSpec((3, rows, LANES), lambda i, *_: (0, i, 0))],
            out_specs=[blk, kvb, blk, blk, blk, blk, whole((32, width)), whole(w1)],
            scratch_shapes=[pltpu.VMEM((32, width), f32)],
        ),
        out_shape=[
            wide,
            jax.ShapeDtypeStruct((tokens, kv_width), bf16),
            wide,
            wide,
            wide,
            wide,
            jax.ShapeDtypeStruct((32, width), f32),
            jax.ShapeDtypeStruct(w1, bf16),
        ],
        compiler_params=params(),
        cost_estimate=cost(9),
        name="pre",
    )(info, x, cot, *a, *b, tables)


def attn_kernel(len_ref, q_ref, gm_ref, kv_ref, tab_ref, *refs, qb, first, final):
    if not first:
        acc_in, refs = refs[0], refs[3:]
    mix_ref, dq_ref, dkv_ref, k0, k1, v0, v1, acc = refs
    p = pl.program_id(0)
    tokens, kv_width = kv_ref.shape
    head = kv_width // 2

    @pl.when(p == 0)
    def _():
        kv = kv_ref[...]
        zero = jnp.zeros((tokens, head), bf16)
        k, v = kv[:, :head], kv[:, head:]
        k0[...] = jnp.concatenate([k, zero], 1)
        k1[...] = jnp.concatenate([zero, k], 1)
        v0[...] = jnp.concatenate([v, zero], 1)
        v1[...] = jnp.concatenate([zero, v], 1)
        acc[...] = jnp.zeros_like(acc) if first else acc_in[...]

    last = len_ref[0] - 1
    scale = head**-0.5
    pads = ((k0, v0), (k1, v1))
    units = [(i, h) for i in range(tokens // qb) for h in range(LANES // head)]
    scored, weighed, mixes, dqs = {}, {}, {}, {}

    def score(unit):
        i, h = unit
        r, kn = pl.ds(i * qb, qb), (i + 1) * qb
        k, v = pads[h]
        scored[unit] = (dot(q_ref[r, :], k[:kn, :], 1, 1), dot(gm_ref[r, :], v[:kn, :], 1, 1))

    def weigh(unit):
        i, h = unit
        r, kn = pl.ds(i * qb, qb), (i + 1) * qb
        s, dp = scored.pop(unit)
        col = lax.broadcasted_iota(jnp.int32, (qb, kn), 1)
        limit = jnp.minimum(lax.broadcasted_iota(jnp.int32, (qb, 1), 0) + i * qb, last)
        s = jnp.where(col <= limit, s, NEG)
        e = jnp.exp(s - jnp.max(s, axis=1, keepdims=True))
        pr = e * (1.0 / jnp.sum(e, axis=1, keepdims=True))
        low = pr.astype(bf16)
        mixed = dot(low, pads[h][1][:kn, :], 1, 0)
        acc[head:, :kn] += dot(gm_ref[r, head * h : head * (h + 1)].T, low, 1, 0)
        weighed[unit] = (pr, dp, mixed)

    def back(unit):
        i, h = unit
        r, kn = pl.ds(i * qb, qb), (i + 1) * qb
        pr, dp, mixed = weighed.pop(unit)
        row = jnp.sum(gm_ref[r, :].astype(f32) * mixed, axis=1, keepdims=True)
        ds = (pr * (dp - row)).astype(bf16)
        dq = dot(ds, pads[h][0][:kn, :], 1, 0)
        acc[:head, :kn] += dot(q_ref[r, head * h : head * (h + 1)].T, ds, 1, 0)
        if h == 0:
            mixes[i], dqs[i] = mixed, dq
        else:
            mix_ref[r, :] = (mixes.pop(i) + mixed).astype(bf16)
            dq = (dqs.pop(i) + dq) * scale
            dq_ref[r, :] = rotate_back(dq, tab_ref[0, r, :], tab_ref[1, r, :], tab_ref[2, r, :]).astype(bf16)

    for t in range(len(units) + 3):
        for stage, lag in ((score, 0), (weigh, 1), (back, 3)):
            if 0 <= t - lag < len(units):
                stage(units[t - lag])

    @pl.when(p == pl.num_programs(0) - 1)
    def _():
        if not final:
            dkv_ref[...] = acc[...]
            return
        dkv = acc[...].T
        lanes = lax.broadcasted_iota(jnp.int32, (tokens, kv_width), 1)
        back = rotate_back(dkv, tab_ref[0], tab_ref[1], tab_ref[2])
        dkv_ref[...] = jnp.where(lanes < head, back, dkv).astype(bf16)


def attention(info, q, gm, kv, tables, state, start, count):
    tokens, width = q.shape
    kv_width = kv.shape[1]
    first, final = state is None, start + count == width // LANES
    blk = pl.BlockSpec((tokens, LANES), lambda p, *_: (0, p + start))
    wide = jax.ShapeDtypeStruct((tokens, width), bf16)
    sums = (kv_width, tokens)
    args, specs, alias = [q, gm, kv, tables], [blk, blk, whole((tokens, kv_width)), whole((3, tokens, LANES))], {}
    if not first:
        args += list(state)
        specs += [whole(sums), pl.BlockSpec(memory_space=pl.ANY), pl.BlockSpec(memory_space=pl.ANY)]
        alias = {6: 0, 7: 1}
    dkv = ((tokens, kv_width), bf16) if final else (sums, f32)
    mixed, dq, dkv = pl.pallas_call(
        functools.partial(attn_kernel, qb=256, first=first, final=final),
        grid_spec=pltpu.PrefetchScalarGridSpec(
            num_scalar_prefetch=1,
            grid=(count,),
            in_specs=specs,
            out_specs=[blk, blk, whole(dkv[0])],
            scratch_shapes=[pltpu.VMEM((tokens, LANES), bf16)] * 4 + [pltpu.VMEM(sums, f32)],
        ),
        out_shape=[wide, wide, jax.ShapeDtypeStruct(*dkv)],
        input_output_aliases=alias,
        compiler_params=params(),
        cost_estimate=cost(8 * count),
        name="attention",
    )(info, *args)
    return dkv, mixed, dq


def split_halves(send_ref, keep_ref, low_s, cols, at, core, half):
    for g in range(low_s.shape[0] // (2 * half)):
        to, base = pl.ds(g * half, half), g * 2 * half
        send_ref[to, at] = low_s[pl.ds(pl.multiple_of(base + (1 - core) * half, half), half), :cols]
        keep_ref[to, at] = low_s[pl.ds(pl.multiple_of(base + core * half, half), half), :cols]


def row_sum(v):
    return jnp.sum(v, axis=1, keepdims=True)


def grads_kernel(info, ha_ref, gy_ref, mix_ref, dq_ref, dkv_ref, w_ref, send_ref, keep_ref, sums, cols, low_s, *, dims, half):
    width, kv_width, step, per_row, per_kv = dims
    j = pl.program_id(0)
    c_out = width + kv_width
    c_vec = c_out + width
    core = info[1]

    @pl.when(j == 0)
    def _():
        cols[...] = jnp.zeros_like(cols)
        sums[...] = jnp.zeros_like(sums)

    def put(value, at, size):
        low_s[:, :size] = value.astype(bf16)
        split_halves(send_ref, keep_ref, low_s, size, pl.ds(at, size), core, half)

    def weight_sums(w, grad, lines):
        w = w.astype(f32)
        cols[:, SHIFT : SHIFT + 1] += row_sum(w * lines)
        cols[:, INNER : INNER + 1] += row_sum(w * grad)

    at = pl.multiple_of(j * step, LANES)
    grad = dot(ha_ref[...], dq_ref[...], 0, 0)
    lines = col_sum(dq_ref[...].astype(f32))
    sums[QB : QB + 1, pl.ds(at, step)] = lines
    sums[OB : OB + 1, pl.ds(at, step)] = col_sum(gy_ref[...].astype(f32))
    weight_sums(w_ref[:, pl.ds(at, step)], grad, lines)
    put(grad, at, step)
    put(dot(mix_ref[...], gy_ref[...], 0, 0), pl.multiple_of(c_out + at, LANES), step)

    @pl.when(j == pl.num_programs(0) - 1)
    def _():
        grad = dot(ha_ref[...], dkv_ref[...], 0, 0)
        lines = col_sum(dkv_ref[...].astype(f32))
        weight_sums(w_ref[:, width:c_out], grad, lines)
        put(grad, width, kv_width)
        vec = w_ref[:, c_vec:].astype(f32)
        shift = cols[:, SHIFT : SHIFT + 1]
        gain = (cols[:, INNER : INNER + 1] - vec[:, BA : BA + 1] * shift) / vec[:, GA : GA + 1]
        spread = spread_key_bias(width, kv_width, per_row, per_kv)
        key = dot(jnp.broadcast_to(lines, (16, kv_width)).astype(bf16), spread, 1, 1)
        row = lax.broadcasted_iota(jnp.int32, (16, width), 0)
        both = jnp.where(row == 8, key, sums[...])
        both = jnp.concatenate([both, jnp.zeros((LANES - 16, width), f32)], 0).T
        lane = lax.broadcasted_iota(jnp.int32, (width, LANES), 1)
        put(jnp.where(lane == GA, gain, jnp.where(lane == BA, shift, both)), c_vec, LANES)


def attention_grads(info, ha, gy, mixed, dq, dkv, w1, shards, half):
    tokens, width = ha.shape
    kv_width = dkv.shape[1]
    step = 2 * LANES
    one = lambda s: pl.BlockSpec(s, lambda *_: (0, 0), pipeline_mode=pl.Buffered(1))
    col = pl.BlockSpec((tokens, step), lambda j, *_: (0, j))
    dims = (width, kv_width, step, width // shards, kv_width // shards)
    cut = (width // 2, w1.shape[1])
    return pl.pallas_call(
        functools.partial(grads_kernel, dims=dims, half=half),
        grid_spec=pltpu.PrefetchScalarGridSpec(
            num_scalar_prefetch=1,
            grid=(width // step,),
            in_specs=[one(ha.shape), col, one(mixed.shape), col, one(dkv.shape), one(w1.shape)],
            out_specs=[one(cut), one(cut)],
            scratch_shapes=[
                pltpu.VMEM((16, width), f32),
                pltpu.VMEM((width, LANES), f32),
                pltpu.VMEM((width, step), bf16),
            ],
        ),
        out_shape=[jax.ShapeDtypeStruct(cut, bf16)] * 2,
        compiler_params=params(),
        cost_estimate=cost(8),
        name="attention_grads",
    )(info, ha, gy, mixed, dq, dkv, w1)


def ff_kernel(*refs, rows, chunk, first, final, half):
    refs = list(refs)
    take = lambda k: [refs.pop(0) for _ in range(k)]
    info, hm_ref, gy_ref, u0, u1, d0, d1, vec_ref = take(8)
    (col_in,) = (None,) if first else take(1)
    (vcol_ref,) = take(1) if final else (None,)
    act_ref, gup_ref = take(2)
    (col_out,) = (None,) if final else take(1)
    send_ref, keep_ref, cols, low_s, wu_ref, wd_ref = refs
    j = pl.program_id(0)
    assemble(wu_ref, slice(None), u0, u1, info[1], half)
    assemble(wd_ref, slice(None), d0, d1, info[1], half)
    tokens, width = hm_ref.shape

    @pl.when(j == 0)
    def _():
        cols[...] = jnp.zeros_like(cols) if first else col_in[...]

    bias = vec_ref[pl.ds(UB + chunk + j, 1), :]
    total = jnp.zeros((1, width), f32)
    for i in range(tokens // rows):
        r = pl.ds(i * rows, rows)
        u = dot(hm_ref[r, :], wu_ref[...], 1, 0) + bias
        cdf = 0.5 * (1.0 + lax.erf(u * ROOT_HALF))
        pdf = jnp.exp(-0.5 * u * u) * INV_ROOT_TAU
        act_ref[r, :] = (u * cdf).astype(bf16)
        grad = (dot(gy_ref[r, :], wd_ref[...], 1, 1) * (cdf + u * pdf)).astype(bf16)
        gup_ref[r, :] = grad
        total = total + col_sum(grad.astype(f32))
    at = pl.multiple_of(j * 2 * width, LANES)
    d_up = dot(hm_ref[...], gup_ref[...], 0, 0)
    low_s[...] = d_up.astype(bf16)
    w_up = wu_ref[...].astype(f32)
    lane = lax.broadcasted_iota(jnp.int32, (width, LANES), 1)
    mine = jnp.where(lane == chunk + j, jnp.broadcast_to(total, (LANES, width)).T, 0.0)
    mine = jnp.where(lane == SHIFT, row_sum(w_up * total), mine)
    cols[...] += jnp.where(lane == INNER, row_sum(w_up * d_up), mine)
    split_halves(send_ref, keep_ref, low_s, width, pl.ds(at, width), info[1], half)
    low_s[...] = dot(act_ref[...], gy_ref[...], 0, 0).astype(bf16)
    at = pl.multiple_of(at + width, LANES)
    split_halves(send_ref, keep_ref, low_s, width, pl.ds(at, width), info[1], half)

    @pl.when(j == pl.num_programs(0) - 1)
    def _():
        if not final:
            col_out[...] = cols[...]
            return
        vec = vcol_ref[...].astype(f32)
        now = cols[...]
        gain = (now[:, INNER : INNER + 1] - vec[:, BM : BM + 1] * now[:, SHIFT : SHIFT + 1]) / vec[:, GM : GM + 1]
        low_s[:, :LANES] = jnp.where(lane == INNER, gain, now).astype(bf16)
        at = pl.ds(send_ref.shape[1] - LANES, LANES)
        split_halves(send_ref, keep_ref, low_s, LANES, at, info[1], half)


def feed_forward(info, hm, gy, up_rows, dn_rows, vec, w1, state, chunk, count, half):
    tokens, width = hm.shape
    blocks = up_rows[0].shape[1] // width
    tok = (tokens, width)
    first, final = state is None, chunk + count == blocks
    one = lambda s: pl.BlockSpec(s, lambda *_: (0, 0), pipeline_mode=pl.Buffered(1))
    col = pl.BlockSpec(tok, lambda j, *_: (0, j))
    wgt = pl.BlockSpec((width // 2, width), lambda j, *_: (0, j + chunk))
    args = [hm, gy, *up_rows, *dn_rows, vec]
    specs = [one(tok), one(tok), wgt, wgt, wgt, wgt, one(vec.shape)]
    last = w1.shape[1] // LANES - 1
    if not first:
        args += [state]
        specs += [one((width, LANES))]
    if final:
        args += [w1]
        specs += [pl.BlockSpec((width, LANES), lambda *_: (0, last), pipeline_mode=pl.Buffered(1))]
    long = jax.ShapeDtypeStruct((tokens, count * width), bf16)
    shapes, outs = [long, long], [col, col]
    if not final:
        shapes += [jax.ShapeDtypeStruct((width, LANES), f32)]
        outs += [one((width, LANES))]
    cut = (width // 2, count * 2 * width + (LANES if final else 0))
    shapes += [jax.ShapeDtypeStruct(cut, bf16)] * 2
    outs += [one(cut)] * 2
    got = pl.pallas_call(
        functools.partial(ff_kernel, rows=256, chunk=chunk, first=first, final=final, half=half),
        grid_spec=pltpu.PrefetchScalarGridSpec(
            num_scalar_prefetch=1,
            grid=(count,),
            in_specs=specs,
            out_specs=outs,
            scratch_shapes=[pltpu.VMEM((width, LANES), f32)] + [pltpu.VMEM((width, width), bf16)] * 3,
        ),
        out_shape=shapes,
        compiler_params=params(),
        cost_estimate=cost(7 * count),
        name="feed_forward",
    )(info, *args)
    act, gup = got[:2]
    return act, gup, None if final else got[2], got[-2], got[-1]


def out_kernel(*refs, pieces, c_out, rows, half):
    info, x_ref, mix_ref, w1_ref, d0, d1, vec_ref = refs[:7]
    acts, out_ref, wd_ref = refs[7:-2], refs[-2], refs[-1]

    @pl.when(pl.program_id(0) == 0)
    def _():
        assemble(wd_ref, slice(None), d0, d1, info[1], half)

    width = x_ref.shape[1]
    total = dot(mix_ref[...], w1_ref[:, c_out : c_out + width], 1, 0) + vec_ref[OB : OB + 1] + vec_ref[DB : DB + 1]
    at = 0
    for act_ref, count in zip(acts, pieces):
        for k in range(count):
            act = act_ref[:, k * width : (k + 1) * width]
            total = total + dot(act, wd_ref[:, at : at + width], 1, 0)
            at += width
    keep = kept_rows(pl.program_id(0), rows, info[0])
    out_ref[...] = (x_ref[...].astype(f32) + keep * total).astype(bf16)


def layer_output(info, x, mixed, w1, dn_rows, vec, acts, c_out, half):
    tokens, width = x.shape
    rows = 256
    long = dn_rows[0].shape[1]
    blk = lambda n: pl.BlockSpec((rows, n), lambda i, *_: (i, 0))
    one = lambda s, *at: pl.BlockSpec(s, lambda *_: at, pipeline_mode=pl.Buffered(1))
    return pl.pallas_call(
        functools.partial(out_kernel, pieces=[a.shape[1] // width for a in acts], c_out=c_out, rows=rows, half=half),
        grid_spec=pltpu.PrefetchScalarGridSpec(
            num_scalar_prefetch=1,
            grid=(tokens // rows,),
            in_specs=[blk(width), blk(width), one(w1.shape, 0, 0)]
            + [one((width // 2, long), 0, 0)] * 2
            + [one(vec.shape, 0, 0)]
            + [blk(a.shape[1]) for a in acts],
            out_specs=blk(width),
            scratch_shapes=[pltpu.VMEM((width, long), bf16)],
        ),
        out_shape=jax.ShapeDtypeStruct((tokens, width), bf16),
        compiler_params=params(),
        cost_estimate=cost(9),
        name="layer_output",
    )(info, x, mixed, w1, *dn_rows, vec, *acts)


def token_kernel(*refs, pieces, kv_width, half):
    info, x_ref, cot_ref, dq_ref, dkv_ref, w1_ref, u0, u1, vec_ref = refs[:9]
    gups, out_ref, wu_ref = refs[9:-2], refs[-2], refs[-1]

    @pl.when(pl.program_id(0) == 0)
    def _():
        assemble(wu_ref, slice(None), u0, u1, info[1], half)

    width = x_ref.shape[1]
    normed, scaled = standardise(x_ref[...].astype(f32))
    grad = dot(dq_ref[...], w1_ref[:, :width], 1, 1) + dot(dkv_ref[...], w1_ref[:, width : width + kv_width], 1, 1)
    total = norm_back(grad, normed, scaled, vec_ref[GA : GA + 1])
    at, grad = 0, None
    for gup_ref, count in zip(gups, pieces):
        part = dot(gup_ref[...], wu_ref[:, at : at + count * width], 1, 1)
        grad = part if grad is None else grad + part
        at += count * width
    total = total + norm_back(grad, normed, scaled, vec_ref[GM : GM + 1])
    out_ref[...] = cot_ref[...].astype(f32) + total


def token_grads(info, x, cot, dq, dkv, w1, up_rows, vec, gups, half):
    tokens, width = x.shape
    rows = 256
    long = up_rows[0].shape[1]
    blk = lambda n: pl.BlockSpec((rows, n), lambda i, *_: (i, 0))
    one = lambda s: pl.BlockSpec(s, lambda *_: (0, 0), pipeline_mode=pl.Buffered(1))
    pieces = [g.shape[1] // width for g in gups]
    return pl.pallas_call(
        functools.partial(token_kernel, pieces=pieces, kv_width=dkv.shape[1], half=half),
        grid_spec=pltpu.PrefetchScalarGridSpec(
            num_scalar_prefetch=1,
            grid=(tokens // rows,),
            in_specs=[blk(width), blk(width), blk(width), blk(dkv.shape[1]), one(w1.shape)]
            + [one((width // 2, long))] * 2
            + [one(vec.shape)]
            + [blk(g.shape[1]) for g in gups],
            out_specs=blk(width),
            scratch_shapes=[pltpu.VMEM((width, long), bf16)],
        ),
        out_shape=jax.ShapeDtypeStruct((tokens, width), f32),
        compiler_params=params(),
        cost_estimate=cost(11),
        name="token_grads",
    )(info, x, cot, dq, dkv, w1, *up_rows, vec, *gups)


def end_kernel(*refs, width, kv_width, blocks, counts, shards):
    pairs, outs = refs[: -13], refs[-13:]
    gq, gkv, go, gu, gd = outs[:5]
    sums = [pairs[2 * k][...].astype(f32) + pairs[2 * k + 1][...].astype(f32) for k in range(len(pairs) // 2)]
    rows = sums[0].shape[0]
    c_out = width + kv_width
    gq[...] = sums[0][:, :width]
    gkv[...] = sums[0][:, width:c_out]
    go[...] = sums[0][:, c_out : c_out + width]
    ups = []
    for part, count in zip(sums[1:], counts):
        for k in range(count):
            at = 2 * k * width
            gd[len(ups) * rows : (len(ups) + 1) * rows, :] = part[:, at + width : at + 2 * width]
            ups.append(part[:, at : at + width])
    if shards * blocks <= 128:
        pieces = [ups[q][:, i * rows : (i + 1) * rows] for i in range(shards) for q in range(blocks)]
        gu[...] = jnp.concatenate(pieces, 1)
    else:
        gu[...] = jnp.concatenate(ups, 1)
    square = lambda v: jnp.concatenate([v, jnp.zeros((LANES - rows, LANES), f32)], 0).T
    v1 = square(sums[0][:, c_out + width :])
    v2 = square(sums[-1][:, -LANES:])
    lines = [v1[QB], v1[8], v1[OB], v1[GA], v1[BA], v2[INNER], v2[SHIFT]]
    for ref, line in zip(outs[5:12], lines):
        ref[...] = line[None, : ref.shape[1]]
    outs[12][...] = v2[:blocks, :rows]


def end(streams, width, kv_width, blocks, counts, shards):
    pairs = [v for s in streams for v in s.result]
    rows = pairs[0].shape[0]
    ff = blocks * width
    shapes = [(rows, width), (rows, kv_width), (rows, width), (rows, ff), (blocks * rows, width)]
    shapes += [(1, rows), (1, kv_width // shards)] + [(1, rows)] * 5 + [(blocks, rows)]
    return pl.pallas_call(
        functools.partial(
            end_kernel, width=width, kv_width=kv_width, blocks=blocks, counts=counts, shards=shards
        ),
        out_shape=[jax.ShapeDtypeStruct(s, f32) for s in shapes],
        compiler_params=params(),
        cost_estimate=cost(3),
        name="end",
    )(*pairs)


def bits_of(axis, size):
    return [(axis, b) for b in range(size.bit_length() - 1)]


def swap(v, axis, bit):
    size = lax.axis_size(axis)
    return lax.ppermute(v, axis, [(i, i ^ (1 << bit)) for i in range(size)])


def add(a, b):
    return (a.astype(f32) + b.astype(f32)).astype(bf16)


def tie(*values):
    return lax.optimization_barrier(values)


class Scatter:
    def __init__(self, halves, parts, tail, index_order):
        self.index_order = index_order
        dims = [1 if b == ("dp", 0) else 2 for b in index_order]
        self.pending = []
        for send, keep in halves:
            rows = send.shape[0] >> (len(index_order) - 1)
            self.pending.append((send, keep.reshape(*dims, rows, send.shape[1])))
        self.cols = sum(send.shape[1] for send, _ in halves)
        self.steps = [[("dp", 0)] * len(halves)] + [list(s) for s in zip(*parts)] + [[b] for b in tail]
        self.flying = None
        self.result = None
        self.first = True

    def ready(self):
        return [send for send, _ in self.pending]

    def set_ready(self, values):
        self.pending = [(send, keep) for send, (_, keep) in zip(values, self.pending)]

    def start(self):
        bits = self.steps.pop(0)
        self.flying = [(swap(send, *bit), keep) for (send, keep), bit in zip(self.pending, bits)]

    def arrived(self):
        return [got for got, _ in self.flying]

    def finish(self, arrived):
        if not self.steps:
            ((got, (_, keep)),) = zip(arrived, self.flying)
            self.result = (keep.reshape(got.shape), got)
            return
        parts = [add(keep, got.reshape(keep.shape)) for got, (_, keep) in zip(arrived, self.flying)]
        bits = self.steps[0]
        if len(parts) > 1 and (self.first or len(parts) != len(bits)):
            parts = [jnp.concatenate(parts, -1)]
        if len(parts) < len(bits):
            (part,) = parts
            step = self.cols // LANES // len(bits) * LANES
            edges = [k * step for k in range(len(bits))] + [self.cols]
            parts = [part[..., lo:hi] for lo, hi in zip(edges, edges[1:])]
        self.first = False
        self.pending = []
        for part, (axis, bit) in zip(parts, bits):
            here, where = (lax.axis_index(axis) >> bit) & 1, self.index_order.index((axis, bit))
            send = lax.dynamic_slice_in_dim(part, 1 - here, 1, where)
            keep = lax.dynamic_slice_in_dim(part, here, 1, where)
            self.pending.append((send.reshape(-1, part.shape[-1]), keep))


class Gather:
    def __init__(self, local, head, orders, index_order):
        self.index_order = index_order
        self.pending = [local.reshape((1,) * len(index_order) + local.shape)]
        self.steps = [[b] for b in head] + [list(s) for s in zip(*orders)] + [[("dp", 0)] * len(orders)]
        self.flying = None
        self.result = None

    def ready(self):
        return self.pending

    def set_ready(self, values):
        self.pending = values

    def start(self):
        bits = self.steps.pop(0)
        if len(bits) > len(self.pending):
            (cur,) = self.pending
            step = cur.shape[-1] // len(bits)
            self.pending = [cur[..., k * step : (k + 1) * step] for k in range(len(bits))]
        self.flying = [(swap(cur.reshape(-1, cur.shape[-1]), *bit), cur, bit) for cur, bit in zip(self.pending, bits)]

    def arrived(self):
        return [got for got, _, _ in self.flying]

    def finish(self, arrived):
        if not self.steps:
            self.result = [(cur.reshape(got.shape), got) for got, (_, cur, _) in zip(arrived, self.flying)]
            return
        self.pending = []
        for got, (_, cur, (axis, bit)) in zip(arrived, self.flying):
            got = got.reshape(cur.shape)
            here = (lax.axis_index(axis) >> bit) & 1
            low = jnp.where(here == 0, cur, got)
            high = jnp.where(here == 0, got, cur)
            self.pending.append(jnp.concatenate([low, high], self.index_order.index((axis, bit))))


def launch(streams, *values):
    streams = [s for s in streams if s.result is None]
    ready, values = tie([s.ready() for s in streams], values)
    for stream, sends in zip(streams, ready):
        stream.set_ready(sends)
        stream.start()
    return values


def land(streams, *values):
    streams = [s for s in streams if s.result is None]
    arrived, values = tie([s.arrived() for s in streams], values)
    for stream, a in zip(streams, arrived):
        stream.finish(a)
    return values


def beside(streams, work, *inputs):
    out = work(*launch(streams, *inputs))
    return land(streams, *out) if isinstance(out, (tuple, list)) else land(streams, out)[0]


def body(
    tokens,
    lengths,
    cotangent,
    query_weight,
    query_bias,
    keyval_weight,
    keyval_bias,
    out_weight,
    out_bias,
    norm_attn_gain,
    norm_attn_bias,
    norm_mlp_gain,
    norm_mlp_bias,
    up_weight,
    up_bias,
    down_weight,
    down_bias,
):
    n_dp, n_fsdp = lax.axis_size("dp"), lax.axis_size("fsdp")
    shards = n_dp * n_fsdp
    rows, width = query_weight.shape
    kv_width = keyval_weight.shape[1]
    ff = up_weight.shape[1]
    blocks = ff // width
    seq_len = tokens.shape[1]
    x = tokens.reshape(seq_len, width)
    cot = cotangent.reshape(seq_len, width)

    half = rows * n_fsdp
    info = jnp.concatenate([lengths, (lax.axis_index("dp") & 1)[None].astype(jnp.int32)])
    dp_bits, fs_bits = bits_of("dp", n_dp), bits_of("fsdp", n_fsdp)
    index_order = dp_bits[::-1] + fs_bits[::-1]
    x_bits, y_bits, z_bits = fs_bits[:1], dp_bits[1:], fs_bits[1:]
    xy = [x_bits + y_bits, y_bits + x_bits]

    up_bias_cols = up_bias.reshape(blocks, rows)
    key_bias_col = jnp.pad(keyval_bias, (0, rows - keyval_bias.shape[0]))
    vecs = [query_bias, out_bias, norm_attn_gain, norm_attn_bias, norm_mlp_gain, norm_mlp_bias, down_bias]
    vecs = jnp.concatenate([jnp.stack(vecs), up_bias_cols, key_bias_col[None]], 0)
    vecs = jnp.pad(vecs, ((0, LANES - vecs.shape[0]), (0, 0))).T
    first = Gather(jnp.concatenate([query_weight, keyval_weight, out_weight, vecs], 1), z_bits[::-1], xy, index_order)
    up_weight, down_weight = launch([first], up_weight, down_weight)
    up_local = up_weight.reshape(rows, shards, blocks, rows).transpose(0, 2, 1, 3).reshape(rows, ff)
    dn_local = down_weight.reshape(blocks, rows, width).transpose(1, 0, 2).reshape(rows, ff)
    up_local, dn_local = land([first], up_local, dn_local)
    for _ in z_bits[1:]:
        up_local, dn_local = land([first], *launch([first], up_local, dn_local))
    ups = Gather(up_local, z_bits[::-1], [x_bits + y_bits], index_order)
    dns = Gather(dn_local, z_bits[::-1], [y_bits + x_bits], index_order)
    (x,) = land([first, ups], *launch([first, ups], x))
    (x,) = land([first, dns], *launch([first, dns], x))
    (x,) = land([first, ups], *launch([first, ups], x))
    while first.result is None:
        (x,) = land([first], *launch([first], x))

    tables = rotary_tables(seq_len, kv_width // 2)
    one, two = first.result
    q, kv, ha, hm, gy, gm, vec, w1 = beside(
        [dns], lambda x: pre(info, x, cot, one, two, tables, kv_width, shards, half), x
    )
    pairs = width // LANES
    second = [ups, dns]
    state = beside(second, lambda q: attention(info, q, gm, kv, tables, None, 0, 2), q)
    (state,) = launch(second, state)
    for start in range(2, pairs, 2):
        state = attention(info, q, gm, kv, tables, state, start, 2)
    dkv, mixed, dq = land(second, *state)
    send, keep = beside(second, lambda mixed: attention_grads(info, ha, gy, mixed, dq, dkv, w1, shards, half), mixed)
    while any(s.result is None for s in second):
        send, keep = beside(second, lambda *v: v, send, keep)
    (up_rows,), (dn_rows,) = ups.result, dns.result

    attn = Scatter([(send, keep)], [z_bits[:1] + x_bits + y_bits], z_bits[1:], index_order)
    hm, gy = beside([attn], lambda *v: v, hm, gy)
    ff_part = lambda chunk, count: lambda hm, gy, *state: feed_forward(
        info, hm, gy, up_rows, dn_rows, vec, w1, state[0] if state else None, chunk, count, half
    )
    n0 = blocks - 2
    act0, gup0, state, send, keep = beside([attn], ff_part(0, n0), hm, gy)
    ff0 = Scatter([(send, keep)], xy, z_bits, index_order)
    act1, gup1, state, send, keep = beside([attn, ff0], ff_part(n0, 1), hm, gy, state)
    halves = [(send, keep)]
    act2, gup2, _, send, keep = beside([attn, ff0], ff_part(n0 + 1, 1), hm, gy, state)
    ff1 = Scatter(halves + [(send, keep)], xy, z_bits, index_order)
    layer_out = beside(
        [ff1, ff0, attn],
        lambda x, *acts: layer_output(info, x, mixed, w1, dn_rows, vec, acts, width + kv_width, half),
        *(x, act0, act1, act2),
    )
    gtok = beside(
        [ff1, ff0, attn],
        lambda cot, *gups: token_grads(info, x, cot, dq, dkv, w1, up_rows, vec, gups, half),
        *(cot, gup0, gup1, gup2),
    )
    streams = [attn, ff0, ff1]
    while any(s.result is None for s in streams):
        beside(streams, lambda *v: v)
    gq, gkv, go, gu, gd, *lines, g_up_bias = end(streams, width, kv_width, blocks, (n0, 2), shards)
    if shards * blocks > 128:
        gu = gu.reshape(rows, blocks, shards, rows).transpose(0, 2, 1, 3).reshape(rows, ff)
    bq, bkv, bo, ga, ba, g_gain, g_shift = (v.reshape(-1) for v in lines)
    return (
        layer_out.reshape(tokens.shape),
        gtok.reshape(tokens.shape),
        gq,
        bq,
        gkv,
        bkv,
        go,
        bo,
        ga,
        ba,
        g_gain,
        g_shift,
        gu,
        g_up_bias.reshape(-1),
        gd,
        bo,
    )


def solution(mesh):
    mat, vec, seq = P(BOTH, None), P(BOTH), P(BOTH, None, None)
    return jax.shard_map(
        body,
        mesh=mesh,
        in_specs=(seq, vec, seq, mat, vec, mat, vec, mat, vec, vec, vec, vec, vec, mat, vec, mat, vec),
        out_specs=(seq, seq, mat, vec, mat, vec, mat, vec, vec, vec, vec, vec, mat, vec, mat, vec),
        check_vma=False,
    )
```

```python
import functools

import jax
import jax.numpy as jnp
import numpy as np
from jax import lax
from jax.experimental import pallas as pl
from jax.experimental.pallas import tpu as pltpu
from jax.sharding import PartitionSpec as P

f32 = jnp.float32
bf16 = jnp.bfloat16

ROT = 16
EPS = 1e-05
NEG = -1e30
ROOT_HALF = 0.7071067811865476
INV_ROOT_TAU = 0.3989422804014327
LANES = 128
BOTH = ("dp", "fsdp")
VMEM = 24 * 1024 * 1024

SHIFT, INNER = 8, 9
QB, OB, GA, BA, GM, BM, DB, UB, KB = 0, 1, 2, 3, 4, 5, 6, 7, 11


def dot(a, b, ca, cb):
    return lax.dot_general(a, b, (((ca,), (cb,)), ((), ())), preferred_element_type=f32)


def params(**kw):
    return pltpu.CompilerParams(vmem_limit_bytes=VMEM, **kw)


def cost(us):
    return pl.CostEstimate(flops=int(us * 1.0e9), bytes_accessed=int(us * 3.0e6), transcendentals=0)


def in_hbm(*arrays):
    return [pltpu.with_memory_space_constraint(a, pltpu.HBM) for a in arrays]


def whole(shape):
    return pl.BlockSpec(shape, lambda *_: (0,) * len(shape))


def rotary_tables(seq_len, head_dim):
    half = ROT // 2
    inverse_freq = np.float32(10000.0) ** (-(np.float32(2.0) * np.arange(half, dtype=np.float32)) / np.float32(ROT))
    angles = np.arange(seq_len, dtype=np.float32)[:, None] * inverse_freq[None, :]
    cos, sin = np.cos(angles.astype(np.float64)), np.sin(angles.astype(np.float64))
    tables = np.zeros((3, seq_len, LANES), np.float32)
    tables[0] = 1.0
    for at in range(0, LANES, head_dim):
        tables[0, :, at : at + half] = cos
        tables[0, :, at + half : at + ROT] = cos
        tables[1, :, at : at + half] = sin
        tables[2, :, at + half : at + ROT] = sin
    return jnp.asarray(tables)


def partners(v):
    half = ROT // 2
    return pltpu.roll(v, LANES - half, 1), pltpu.roll(v, half, 1)


def rotate(v, own, up, down):
    ahead, behind = partners(v)
    return v * own - ahead * up + behind * down


def rotate_back(v, own, up, down):
    ahead, behind = partners(v)
    return v * own + ahead * up - behind * down


def standardise(rows):
    average = jnp.mean(rows, axis=-1, keepdims=True)
    centred = rows - average
    scaled = lax.rsqrt(jnp.mean(centred * centred, axis=-1, keepdims=True) + EPS)
    return centred * scaled, scaled


def norm_back(grad, normed, scaled, gain):
    e = grad * gain
    return scaled * (
        e - jnp.mean(e, axis=-1, keepdims=True) - normed * jnp.mean(e * normed, axis=-1, keepdims=True)
    )


def col_sum(v):
    return jnp.sum(v, axis=0, keepdims=True)


def kept_rows(block, rows, length):
    pos = lax.broadcasted_iota(jnp.int32, (rows, 1), 0) + block * rows
    return (pos < length).astype(f32)


def spread_key_bias(width, kv_width, per_row, per_kv):
    row = lax.broadcasted_iota(jnp.int32, (width, kv_width), 0)
    col = lax.broadcasted_iota(jnp.int32, (width, kv_width), 1)
    owner = col // per_kv
    return (row == owner * per_row + (col - owner * per_kv)).astype(bf16)


def assemble(to, at, mine, other, core, half):
    for g in range(to.shape[0] // (2 * half)):
        rows, base = slice(g * half, (g + 1) * half), g * 2 * half
        to[pl.ds(pl.multiple_of(base + core * half, half), half), at] = mine[rows, :]
        to[pl.ds(pl.multiple_of(base + (1 - core) * half, half), half), at] = other[rows, :]


def pre_kernel(info, x_ref, cot_ref, a0, a1, b0, b1, tab_ref, q_ref, kv_ref, ha_ref, hm_ref, gy_ref, gm_ref, vec_ref, w_ref, vec_s, *, dims, half):
    width, kv_width, rows, per_row, per_kv = dims
    i = pl.program_id(0)
    c_out = width + kv_width
    c_vec = c_out + width

    @pl.when(i == 0)
    def _():
        assemble(w_ref, slice(0, c_out), a0, a1, info[1], half)
        assemble(w_ref, slice(c_out, c_vec + LANES), b0, b1, info[1], half)
        low = w_ref[:, c_vec : c_vec + LANES]
        lines = low.astype(f32).T[:16]
        vec_s[:16, :] = lines
        spread = spread_key_bias(width, kv_width, per_row, per_kv)
        vec_s[16:32, :kv_width] = dot(lines.astype(bf16), spread, 1, 0)
        vec_ref[...] = vec_s[...]

    normed, _ = standardise(x_ref[...].astype(f32))
    vec = vec_s[...]
    ha = (normed * vec[GA : GA + 1] + vec[BA : BA + 1]).astype(bf16)
    hm = (normed * vec[GM : GM + 1] + vec[BM : BM + 1]).astype(bf16)
    ha_ref[...] = ha
    hm_ref[...] = hm
    own, up, down = tab_ref[0], tab_ref[1], tab_ref[2]
    scale = (kv_width // 2) ** -0.5
    lin = dot(ha, w_ref[:, :c_out], 1, 0)
    query = lin[:, :width] + vec[QB : QB + 1]
    for p in range(width // LANES):
        cols = slice(p * LANES, (p + 1) * LANES)
        rot = rotate(query[:, cols], own, up, down).astype(bf16)
        q_ref[:, cols] = (rot.astype(f32) * scale).astype(bf16)
    lin = lin[:, width:] + vec[16 + KB : 17 + KB, :kv_width]
    lane = lax.broadcasted_iota(jnp.int32, (rows, kv_width), 1)
    kv_ref[...] = jnp.where(lane < kv_width // 2, rotate(lin, own, up, down), lin).astype(bf16)
    keep = kept_rows(i, rows, info[0])
    gy = (cot_ref[...].astype(f32) * keep).astype(bf16)
    gy_ref[...] = gy
    gm_ref[...] = dot(gy, w_ref[:, c_out:c_vec], 1, 1).astype(bf16)


def pre(info, x, cot, a, b, tables, kv_width, shards, half):
    tokens, width = x.shape
    rows = 256
    blk = pl.BlockSpec((rows, width), lambda i, *_: (i, 0))
    kvb = pl.BlockSpec((rows, kv_width), lambda i, *_: (i, 0))
    dims = (width, kv_width, rows, width // shards, kv_width // shards)
    wide = jax.ShapeDtypeStruct((tokens, width), bf16)
    one = lambda v: pl.BlockSpec(v.shape, lambda *_: (0, 0), pipeline_mode=pl.Buffered(1))
    w1 = (width, 2 * width + kv_width + LANES)
    return pl.pallas_call(
        functools.partial(pre_kernel, dims=dims, half=half),
        grid_spec=pltpu.PrefetchScalarGridSpec(
            num_scalar_prefetch=1,
            grid=(tokens // rows,),
            in_specs=[blk, blk, one(a[0]), one(a[1]), one(b[0]), one(b[1])]
            + [pl.BlockSpec((3, rows, LANES), lambda i, *_: (0, i, 0))],
            out_specs=[blk, kvb, blk, blk, blk, blk, whole((32, width)), whole(w1)],
            scratch_shapes=[pltpu.VMEM((32, width), f32)],
        ),
        out_shape=[
            wide,
            jax.ShapeDtypeStruct((tokens, kv_width), bf16),
            wide,
            wide,
            wide,
            wide,
            jax.ShapeDtypeStruct((32, width), f32),
            jax.ShapeDtypeStruct(w1, bf16),
        ],
        compiler_params=params(),
        cost_estimate=cost(9),
        name="pre",
    )(info, x, cot, *a, *b, tables)


def attn_kernel(len_ref, q_ref, gm_ref, kv_ref, tab_ref, *refs, qb, first, final):
    if not first:
        acc_in, refs = refs[0], refs[3:]
    mix_ref, dq_ref, dkv_ref, k0, k1, v0, v1, acc = refs
    p = pl.program_id(0)
    tokens, kv_width = kv_ref.shape
    head = kv_width // 2

    @pl.when(p == 0)
    def _():
        kv = kv_ref[...]
        zero = jnp.zeros((tokens, head), bf16)
        k, v = kv[:, :head], kv[:, head:]
        k0[...] = jnp.concatenate([k, zero], 1)
        k1[...] = jnp.concatenate([zero, k], 1)
        v0[...] = jnp.concatenate([v, zero], 1)
        v1[...] = jnp.concatenate([zero, v], 1)
        acc[...] = jnp.zeros_like(acc) if first else acc_in[...]

    last = len_ref[0] - 1
    scale = head**-0.5
    pads = ((k0, v0), (k1, v1))
    units = [(i, h) for i in range(tokens // qb) for h in range(LANES // head)]
    scored, weighed, mixes, dqs = {}, {}, {}, {}

    def score(unit):
        i, h = unit
        r, kn = pl.ds(i * qb, qb), (i + 1) * qb
        k, v = pads[h]
        scored[unit] = (dot(q_ref[r, :], k[:kn, :], 1, 1), dot(gm_ref[r, :], v[:kn, :], 1, 1))

    def weigh(unit):
        i, h = unit
        r, kn = pl.ds(i * qb, qb), (i + 1) * qb
        s, dp = scored.pop(unit)
        col = lax.broadcasted_iota(jnp.int32, (qb, kn), 1)
        limit = jnp.minimum(lax.broadcasted_iota(jnp.int32, (qb, 1), 0) + i * qb, last)
        s = jnp.where(col <= limit, s, NEG)
        e = jnp.exp(s - jnp.max(s, axis=1, keepdims=True))
        pr = e * (1.0 / jnp.sum(e, axis=1, keepdims=True))
        low = pr.astype(bf16)
        mixed = dot(low, pads[h][1][:kn, :], 1, 0)
        acc[head:, :kn] += dot(gm_ref[r, head * h : head * (h + 1)].T, low, 1, 0)
        weighed[unit] = (pr, dp, mixed)

    def back(unit):
        i, h = unit
        r, kn = pl.ds(i * qb, qb), (i + 1) * qb
        pr, dp, mixed = weighed.pop(unit)
        row = jnp.sum(gm_ref[r, :].astype(f32) * mixed, axis=1, keepdims=True)
        ds = (pr * (dp - row)).astype(bf16)
        dq = dot(ds, pads[h][0][:kn, :], 1, 0)
        acc[:head, :kn] += dot(q_ref[r, head * h : head * (h + 1)].T, ds, 1, 0)
        if h == 0:
            mixes[i], dqs[i] = mixed, dq
        else:
            mix_ref[r, :] = (mixes.pop(i) + mixed).astype(bf16)
            dq = (dqs.pop(i) + dq) * scale
            dq_ref[r, :] = rotate_back(dq, tab_ref[0, r, :], tab_ref[1, r, :], tab_ref[2, r, :]).astype(bf16)

    for t in range(len(units) + 3):
        for stage, lag in ((score, 0), (weigh, 1), (back, 3)):
            if 0 <= t - lag < len(units):
                stage(units[t - lag])

    @pl.when(p == pl.num_programs(0) - 1)
    def _():
        if not final:
            dkv_ref[...] = acc[...]
            return
        dkv = acc[...].T
        lanes = lax.broadcasted_iota(jnp.int32, (tokens, kv_width), 1)
        back = rotate_back(dkv, tab_ref[0], tab_ref[1], tab_ref[2])
        dkv_ref[...] = jnp.where(lanes < head, back, dkv).astype(bf16)


def attention(info, q, gm, kv, tables, state, start, count):
    tokens, width = q.shape
    kv_width = kv.shape[1]
    first, final = state is None, start + count == width // LANES
    blk = pl.BlockSpec((tokens, LANES), lambda p, *_: (0, p + start))
    wide = jax.ShapeDtypeStruct((tokens, width), bf16)
    sums = (kv_width, tokens)
    args, specs, alias = [q, gm, kv, tables], [blk, blk, whole((tokens, kv_width)), whole((3, tokens, LANES))], {}
    if not first:
        args += list(state)
        specs += [whole(sums), pl.BlockSpec(memory_space=pl.ANY), pl.BlockSpec(memory_space=pl.ANY)]
        alias = {6: 0, 7: 1}
    dkv = ((tokens, kv_width), bf16) if final else (sums, f32)
    mixed, dq, dkv = pl.pallas_call(
        functools.partial(attn_kernel, qb=256, first=first, final=final),
        grid_spec=pltpu.PrefetchScalarGridSpec(
            num_scalar_prefetch=1,
            grid=(count,),
            in_specs=specs,
            out_specs=[blk, blk, whole(dkv[0])],
            scratch_shapes=[pltpu.VMEM((tokens, LANES), bf16)] * 4 + [pltpu.VMEM(sums, f32)],
        ),
        out_shape=[wide, wide, jax.ShapeDtypeStruct(*dkv)],
        input_output_aliases=alias,
        compiler_params=params(),
        cost_estimate=cost(8 * count),
        name="attention",
    )(info, *args)
    return dkv, mixed, dq


def split_halves(send_ref, keep_ref, low_s, cols, at, core, half):
    for g in range(low_s.shape[0] // (2 * half)):
        to, base = pl.ds(g * half, half), g * 2 * half
        send_ref[to, at] = low_s[pl.ds(pl.multiple_of(base + (1 - core) * half, half), half), :cols]
        keep_ref[to, at] = low_s[pl.ds(pl.multiple_of(base + core * half, half), half), :cols]


def row_sum(v):
    return jnp.sum(v, axis=1, keepdims=True)


def grads_kernel(info, ha_ref, gy_ref, mix_ref, dq_ref, dkv_ref, w_ref, send_ref, keep_ref, sums, cols, low_s, *, dims, half):
    width, kv_width, step, per_row, per_kv = dims
    j = pl.program_id(0)
    c_out = width + kv_width
    c_vec = c_out + width
    core = info[1]

    @pl.when(j == 0)
    def _():
        cols[...] = jnp.zeros_like(cols)
        sums[...] = jnp.zeros_like(sums)

    def put(value, at, size):
        low_s[:, :size] = value.astype(bf16)
        split_halves(send_ref, keep_ref, low_s, size, pl.ds(at, size), core, half)

    def weight_sums(w, grad, lines):
        w = w.astype(f32)
        cols[:, SHIFT : SHIFT + 1] += row_sum(w * lines)
        cols[:, INNER : INNER + 1] += row_sum(w * grad)

    at = pl.multiple_of(j * step, LANES)
    grad = dot(ha_ref[...], dq_ref[...], 0, 0)
    lines = col_sum(dq_ref[...].astype(f32))
    sums[QB : QB + 1, pl.ds(at, step)] = lines
    sums[OB : OB + 1, pl.ds(at, step)] = col_sum(gy_ref[...].astype(f32))
    weight_sums(w_ref[:, pl.ds(at, step)], grad, lines)
    put(grad, at, step)
    put(dot(mix_ref[...], gy_ref[...], 0, 0), pl.multiple_of(c_out + at, LANES), step)

    @pl.when(j == pl.num_programs(0) - 1)
    def _():
        grad = dot(ha_ref[...], dkv_ref[...], 0, 0)
        lines = col_sum(dkv_ref[...].astype(f32))
        weight_sums(w_ref[:, width:c_out], grad, lines)
        put(grad, width, kv_width)
        vec = w_ref[:, c_vec:].astype(f32)
        shift = cols[:, SHIFT : SHIFT + 1]
        gain = (cols[:, INNER : INNER + 1] - vec[:, BA : BA + 1] * shift) / vec[:, GA : GA + 1]
        spread = spread_key_bias(width, kv_width, per_row, per_kv)
        key = dot(jnp.broadcast_to(lines, (16, kv_width)).astype(bf16), spread, 1, 1)
        row = lax.broadcasted_iota(jnp.int32, (16, width), 0)
        both = jnp.where(row == 8, key, sums[...])
        both = jnp.concatenate([both, jnp.zeros((LANES - 16, width), f32)], 0).T
        lane = lax.broadcasted_iota(jnp.int32, (width, LANES), 1)
        put(jnp.where(lane == GA, gain, jnp.where(lane == BA, shift, both)), c_vec, LANES)


def attention_grads(info, ha, gy, mixed, dq, dkv, w1, shards, half):
    tokens, width = ha.shape
    kv_width = dkv.shape[1]
    step = 2 * LANES
    one = lambda s: pl.BlockSpec(s, lambda *_: (0, 0), pipeline_mode=pl.Buffered(1))
    col = pl.BlockSpec((tokens, step), lambda j, *_: (0, j))
    dims = (width, kv_width, step, width // shards, kv_width // shards)
    cut = (width // 2, w1.shape[1])
    return pl.pallas_call(
        functools.partial(grads_kernel, dims=dims, half=half),
        grid_spec=pltpu.PrefetchScalarGridSpec(
            num_scalar_prefetch=1,
            grid=(width // step,),
            in_specs=[one(ha.shape), col, one(mixed.shape), col, one(dkv.shape), one(w1.shape)],
            out_specs=[one(cut), one(cut)],
            scratch_shapes=[
                pltpu.VMEM((16, width), f32),
                pltpu.VMEM((width, LANES), f32),
                pltpu.VMEM((width, step), bf16),
            ],
        ),
        out_shape=[jax.ShapeDtypeStruct(cut, bf16)] * 2,
        compiler_params=params(),
        cost_estimate=cost(8),
        name="attention_grads",
    )(info, ha, gy, mixed, dq, dkv, w1)


def ff_kernel(*refs, rows, chunk, first, final, half):
    refs = list(refs)
    take = lambda k: [refs.pop(0) for _ in range(k)]
    info, hm_ref, gy_ref, u0, u1, d0, d1, vec_ref = take(8)
    (col_in,) = (None,) if first else take(1)
    (vcol_ref,) = take(1) if final else (None,)
    act_ref, gup_ref = take(2)
    (col_out,) = (None,) if final else take(1)
    send_ref, keep_ref, cols, low_s, wu_ref, wd_ref = refs
    j = pl.program_id(0)
    assemble(wu_ref, slice(None), u0, u1, info[1], half)
    assemble(wd_ref, slice(None), d0, d1, info[1], half)
    tokens, width = hm_ref.shape

    @pl.when(j == 0)
    def _():
        cols[...] = jnp.zeros_like(cols) if first else col_in[...]

    bias = vec_ref[pl.ds(UB + chunk + j, 1), :]
    total = jnp.zeros((1, width), f32)
    for i in range(tokens // rows):
        r = pl.ds(i * rows, rows)
        u = dot(hm_ref[r, :], wu_ref[...], 1, 0) + bias
        cdf = 0.5 * (1.0 + lax.erf(u * ROOT_HALF))
        pdf = jnp.exp(-0.5 * u * u) * INV_ROOT_TAU
        act_ref[r, :] = (u * cdf).astype(bf16)
        grad = (dot(gy_ref[r, :], wd_ref[...], 1, 1) * (cdf + u * pdf)).astype(bf16)
        gup_ref[r, :] = grad
        total = total + col_sum(grad.astype(f32))
    at = pl.multiple_of(j * 2 * width, LANES)
    d_up = dot(hm_ref[...], gup_ref[...], 0, 0)
    low_s[...] = d_up.astype(bf16)
    w_up = wu_ref[...].astype(f32)
    lane = lax.broadcasted_iota(jnp.int32, (width, LANES), 1)
    mine = jnp.where(lane == chunk + j, jnp.broadcast_to(total, (LANES, width)).T, 0.0)
    mine = jnp.where(lane == SHIFT, row_sum(w_up * total), mine)
    cols[...] += jnp.where(lane == INNER, row_sum(w_up * d_up), mine)
    split_halves(send_ref, keep_ref, low_s, width, pl.ds(at, width), info[1], half)
    low_s[...] = dot(act_ref[...], gy_ref[...], 0, 0).astype(bf16)
    at = pl.multiple_of(at + width, LANES)
    split_halves(send_ref, keep_ref, low_s, width, pl.ds(at, width), info[1], half)

    @pl.when(j == pl.num_programs(0) - 1)
    def _():
        if not final:
            col_out[...] = cols[...]
            return
        vec = vcol_ref[...].astype(f32)
        now = cols[...]
        gain = (now[:, INNER : INNER + 1] - vec[:, BM : BM + 1] * now[:, SHIFT : SHIFT + 1]) / vec[:, GM : GM + 1]
        low_s[:, :LANES] = jnp.where(lane == INNER, gain, now).astype(bf16)
        at = pl.ds(send_ref.shape[1] - LANES, LANES)
        split_halves(send_ref, keep_ref, low_s, LANES, at, info[1], half)


def feed_forward(info, hm, gy, up_rows, dn_rows, vec, w1, state, chunk, count, half):
    tokens, width = hm.shape
    blocks = up_rows[0].shape[1] // width
    tok = (tokens, width)
    first, final = state is None, chunk + count == blocks
    one = lambda s: pl.BlockSpec(s, lambda *_: (0, 0), pipeline_mode=pl.Buffered(1))
    col = pl.BlockSpec(tok, lambda j, *_: (0, j))
    wgt = pl.BlockSpec((width // 2, width), lambda j, *_: (0, j + chunk))
    args = [hm, gy, *in_hbm(*up_rows, *dn_rows), vec]
    specs = [one(tok), one(tok), wgt, wgt, wgt, wgt, one(vec.shape)]
    last = w1.shape[1] // LANES - 1
    if not first:
        args += [state]
        specs += [one((width, LANES))]
    if final:
        args += [w1]
        specs += [pl.BlockSpec((width, LANES), lambda *_: (0, last), pipeline_mode=pl.Buffered(1))]
    long = pltpu.HBM((tokens, count * width), bf16)
    shapes, outs = [long, long], [col, col]
    if not final:
        shapes += [jax.ShapeDtypeStruct((width, LANES), f32)]
        outs += [one((width, LANES))]
    cut = (width // 2, count * 2 * width + (LANES if final else 0))
    shapes += [jax.ShapeDtypeStruct(cut, bf16)] * 2
    outs += [one(cut)] * 2
    got = pl.pallas_call(
        functools.partial(ff_kernel, rows=256, chunk=chunk, first=first, final=final, half=half),
        grid_spec=pltpu.PrefetchScalarGridSpec(
            num_scalar_prefetch=1,
            grid=(count,),
            in_specs=specs,
            out_specs=outs,
            scratch_shapes=[pltpu.VMEM((width, LANES), f32)] + [pltpu.VMEM((width, width), bf16)] * 3,
        ),
        out_shape=shapes,
        compiler_params=params(),
        cost_estimate=cost(7 * count),
        name="feed_forward",
    )(info, *args)
    act, gup = got[:2]
    return act, gup, None if final else got[2], got[-2], got[-1]


def out_kernel(*refs, pieces, c_out, rows, half):
    info, x_ref, mix_ref, w1_ref, d0, d1, vec_ref = refs[:7]
    acts, out_ref, wd_ref = refs[7:-2], refs[-2], refs[-1]

    @pl.when(pl.program_id(0) == 0)
    def _():
        assemble(wd_ref, slice(None), d0, d1, info[1], half)

    width = x_ref.shape[1]
    total = dot(mix_ref[...], w1_ref[:, c_out : c_out + width], 1, 0) + vec_ref[OB : OB + 1] + vec_ref[DB : DB + 1]
    at = 0
    for act_ref, count in zip(acts, pieces):
        for k in range(count):
            act = act_ref[:, k * width : (k + 1) * width]
            total = total + dot(act, wd_ref[:, at : at + width], 1, 0)
            at += width
    keep = kept_rows(pl.program_id(0), rows, info[0])
    out_ref[...] = (x_ref[...].astype(f32) + keep * total).astype(bf16)


def layer_output(info, x, mixed, w1, dn_rows, vec, acts, c_out, half):
    tokens, width = x.shape
    rows = 256
    long = dn_rows[0].shape[1]
    blk = lambda n: pl.BlockSpec((rows, n), lambda i, *_: (i, 0))
    one = lambda s, *at: pl.BlockSpec(s, lambda *_: at, pipeline_mode=pl.Buffered(1))
    return pl.pallas_call(
        functools.partial(out_kernel, pieces=[a.shape[1] // width for a in acts], c_out=c_out, rows=rows, half=half),
        grid_spec=pltpu.PrefetchScalarGridSpec(
            num_scalar_prefetch=1,
            grid=(tokens // rows,),
            in_specs=[blk(width), blk(width), one(w1.shape, 0, 0)]
            + [one((width // 2, long), 0, 0)] * 2
            + [one(vec.shape, 0, 0)]
            + [blk(a.shape[1]) for a in acts],
            out_specs=blk(width),
            scratch_shapes=[pltpu.VMEM((width, long), bf16)],
        ),
        out_shape=jax.ShapeDtypeStruct((tokens, width), bf16),
        compiler_params=params(),
        cost_estimate=cost(9),
        name="layer_output",
    )(info, x, mixed, w1, *in_hbm(*dn_rows), vec, *in_hbm(*acts))


def token_kernel(*refs, pieces, kv_width, half):
    info, x_ref, cot_ref, dq_ref, dkv_ref, w1_ref, u0, u1, vec_ref = refs[:9]
    gups, out_ref, wu_ref = refs[9:-2], refs[-2], refs[-1]

    @pl.when(pl.program_id(0) == 0)
    def _():
        assemble(wu_ref, slice(None), u0, u1, info[1], half)

    width = x_ref.shape[1]
    normed, scaled = standardise(x_ref[...].astype(f32))
    grad = dot(dq_ref[...], w1_ref[:, :width], 1, 1) + dot(dkv_ref[...], w1_ref[:, width : width + kv_width], 1, 1)
    total = norm_back(grad, normed, scaled, vec_ref[GA : GA + 1])
    at, grad = 0, None
    for gup_ref, count in zip(gups, pieces):
        part = dot(gup_ref[...], wu_ref[:, at : at + count * width], 1, 1)
        grad = part if grad is None else grad + part
        at += count * width
    total = total + norm_back(grad, normed, scaled, vec_ref[GM : GM + 1])
    out_ref[...] = cot_ref[...].astype(f32) + total


def token_grads(info, x, cot, dq, dkv, w1, up_rows, vec, gups, half):
    tokens, width = x.shape
    rows = 256
    long = up_rows[0].shape[1]
    blk = lambda n: pl.BlockSpec((rows, n), lambda i, *_: (i, 0))
    one = lambda s: pl.BlockSpec(s, lambda *_: (0, 0), pipeline_mode=pl.Buffered(1))
    pieces = [g.shape[1] // width for g in gups]
    return pl.pallas_call(
        functools.partial(token_kernel, pieces=pieces, kv_width=dkv.shape[1], half=half),
        grid_spec=pltpu.PrefetchScalarGridSpec(
            num_scalar_prefetch=1,
            grid=(tokens // rows,),
            in_specs=[blk(width), blk(width), blk(width), blk(dkv.shape[1]), one(w1.shape)]
            + [one((width // 2, long))] * 2
            + [one(vec.shape)]
            + [blk(g.shape[1]) for g in gups],
            out_specs=blk(width),
            scratch_shapes=[pltpu.VMEM((width, long), bf16)],
        ),
        out_shape=jax.ShapeDtypeStruct((tokens, width), f32),
        compiler_params=params(),
        cost_estimate=cost(11),
        name="token_grads",
    )(info, x, cot, dq, dkv, w1, *in_hbm(*up_rows), vec, *in_hbm(*gups))


def end_kernel(*refs, sizes, width, kv_width, blocks, counts, shards):
    terms, outs = list(refs[:-13]), refs[-13:]
    gq, gkv, go, gu, gd = outs[:5]
    sums = [sum(terms.pop(0)[...].astype(f32) for _ in range(size)) for size in sizes]
    rows = sums[0].shape[0]
    c_out = width + kv_width
    gq[...] = sums[0][:, :width]
    gkv[...] = sums[0][:, width:c_out]
    go[...] = sums[0][:, c_out : c_out + width]
    ups = []
    for part, count in zip(sums[1:], counts):
        for k in range(count):
            at = 2 * k * width
            gd[len(ups) * rows : (len(ups) + 1) * rows, :] = part[:, at + width : at + 2 * width]
            ups.append(part[:, at : at + width])
    if shards * blocks <= 128:
        pieces = [ups[q][:, i * rows : (i + 1) * rows] for i in range(shards) for q in range(blocks)]
        gu[...] = jnp.concatenate(pieces, 1)
    else:
        gu[...] = jnp.concatenate(ups, 1)
    square = lambda v: jnp.concatenate([v, jnp.zeros((LANES - rows, LANES), f32)], 0).T
    v1 = square(sums[0][:, c_out + width :])
    v2 = square(sums[-1][:, -LANES:])
    lines = [v1[QB], v1[8], v1[OB], v1[GA], v1[BA], v2[INNER], v2[SHIFT]]
    for ref, line in zip(outs[5:12], lines):
        ref[...] = line[None, : ref.shape[1]]
    outs[12][...] = v2[:blocks, :rows]


def end(streams, width, kv_width, blocks, counts, shards):
    terms = [v for s in streams for v in s.result]
    sizes = [len(s.result) for s in streams]
    rows = terms[0].shape[0]
    ff = blocks * width
    shapes = [(rows, width), (rows, kv_width), (rows, width), (rows, ff), (blocks * rows, width)]
    shapes += [(1, rows), (1, kv_width // shards)] + [(1, rows)] * 5 + [(blocks, rows)]
    return pl.pallas_call(
        functools.partial(
            end_kernel, sizes=sizes, width=width, kv_width=kv_width, blocks=blocks, counts=counts, shards=shards
        ),
        out_shape=[jax.ShapeDtypeStruct(s, f32) for s in shapes],
        compiler_params=params(),
        cost_estimate=cost(3),
        name="end",
    )(*terms)


def bits_of(axis, size):
    return [(axis, b) for b in range(size.bit_length() - 1)]


def swap(v, axis, bit):
    size = lax.axis_size(axis)
    return lax.ppermute(v, axis, [(i, i ^ (1 << bit)) for i in range(size)])


def total(terms):
    return sum(t.astype(f32) for t in terms).astype(bf16)


def tie(*values):
    return lax.optimization_barrier(values)


class Scatter:
    def __init__(self, halves, parts, tail, index_order):
        self.index_order = index_order
        dims = [1 if b == ("dp", 0) else 2 for b in index_order]
        self.pending = []
        for send, keep in halves:
            rows = send.shape[0] >> (len(index_order) - 1)
            self.pending.append((send, [keep.reshape(*dims, rows, send.shape[1])]))
        self.cols = sum(send.shape[1] for send, _ in halves)
        self.steps = [[("dp", 0)] * len(halves)] + [list(s) for s in zip(*parts)] + [[b] for b in tail]
        self.flying = None
        self.result = None

    def ready(self):
        return [send for send, _ in self.pending]

    def set_ready(self, values):
        self.pending = [(send, keep) for send, (_, keep) in zip(values, self.pending)]

    def start(self):
        bits = self.steps.pop(0)
        self.flying = [(swap(send, *bit), keep) for (send, keep), bit in zip(self.pending, bits)]

    def arrived(self):
        return [got for got, _ in self.flying]

    def finish(self, arrived):
        parts = [keep + [got.reshape(keep[0].shape)] for got, (_, keep) in zip(arrived, self.flying)]
        if not self.steps:
            (terms,) = parts
            self.result = [t.reshape(-1, self.cols) for t in terms]
            return
        bits = self.steps[0]
        if len(parts) > len(bits):
            parts = [[jnp.concatenate([total(terms) for terms in parts], -1)]]
        if len(parts) < len(bits):
            (terms,) = parts
            step = self.cols // LANES // len(bits) * LANES
            edges = [k * step for k in range(len(bits))] + [self.cols]
            parts = [[t[..., lo:hi] for t in terms] for lo, hi in zip(edges, edges[1:])]
        self.pending = []
        for terms, (axis, bit) in zip(parts, bits):
            here, where = (lax.axis_index(axis) >> bit) & 1, self.index_order.index((axis, bit))
            send = total([lax.dynamic_slice_in_dim(t, 1 - here, 1, where) for t in terms])
            keep = [lax.dynamic_slice_in_dim(t, here, 1, where) for t in terms]
            if len(keep) > 2:
                keep = [total(keep)]
            self.pending.append((send.reshape(-1, send.shape[-1]), keep))


class Gather:
    def __init__(self, local, head, orders, index_order):
        self.index_order = index_order
        self.pending = [local.reshape((1,) * len(index_order) + local.shape)]
        self.steps = [[b] for b in head] + [list(s) for s in zip(*orders)] + [[("dp", 0)] * len(orders)]
        self.flying = None
        self.result = None

    def ready(self):
        return self.pending

    def set_ready(self, values):
        self.pending = values

    def start(self):
        bits = self.steps.pop(0)
        if len(bits) > len(self.pending):
            (cur,) = self.pending
            step = cur.shape[-1] // len(bits)
            self.pending = [cur[..., k * step : (k + 1) * step] for k in range(len(bits))]
        self.flying = [(swap(cur.reshape(-1, cur.shape[-1]), *bit), cur, bit) for cur, bit in zip(self.pending, bits)]

    def arrived(self):
        return [got for got, _, _ in self.flying]

    def finish(self, arrived):
        if not self.steps:
            self.result = [(cur.reshape(got.shape), got) for got, (_, cur, _) in zip(arrived, self.flying)]
            return
        self.pending = []
        for got, (_, cur, (axis, bit)) in zip(arrived, self.flying):
            got = got.reshape(cur.shape)
            here = (lax.axis_index(axis) >> bit) & 1
            low = jnp.where(here == 0, cur, got)
            high = jnp.where(here == 0, got, cur)
            self.pending.append(jnp.concatenate([low, high], self.index_order.index((axis, bit))))


def launch(streams, *values):
    streams = [s for s in streams if s.result is None]
    ready, values = tie([s.ready() for s in streams], values)
    for stream, sends in zip(streams, ready):
        stream.set_ready(sends)
        stream.start()
    return values


def land(streams, *values):
    streams = [s for s in streams if s.result is None]
    if any(isinstance(s, Gather) for s in streams):
        arrived, values = tie([s.arrived() for s in streams], values)
    else:
        arrived = [tie(s.arrived(), values)[0] for s in streams]
    for stream, got in zip(streams, arrived):
        stream.finish(got)
    return values


def beside(streams, work, *inputs):
    out = work(*launch(streams, *inputs))
    return land(streams, *out) if isinstance(out, (tuple, list)) else land(streams, out)[0]


def body(
    tokens,
    lengths,
    cotangent,
    query_weight,
    query_bias,
    keyval_weight,
    keyval_bias,
    out_weight,
    out_bias,
    norm_attn_gain,
    norm_attn_bias,
    norm_mlp_gain,
    norm_mlp_bias,
    up_weight,
    up_bias,
    down_weight,
    down_bias,
):
    n_dp, n_fsdp = lax.axis_size("dp"), lax.axis_size("fsdp")
    shards = n_dp * n_fsdp
    rows, width = query_weight.shape
    kv_width = keyval_weight.shape[1]
    ff = up_weight.shape[1]
    blocks = ff // width
    seq_len = tokens.shape[1]
    x = tokens.reshape(seq_len, width)
    cot = cotangent.reshape(seq_len, width)

    half = rows * n_fsdp
    info = jnp.concatenate([lengths, (lax.axis_index("dp") & 1)[None].astype(jnp.int32)])
    dp_bits, fs_bits = bits_of("dp", n_dp), bits_of("fsdp", n_fsdp)
    index_order = dp_bits[::-1] + fs_bits[::-1]
    x_bits, y_bits, z_bits = fs_bits[:1], dp_bits[1:], fs_bits[1:]
    xy = [x_bits + y_bits, y_bits + x_bits]

    up_bias_cols = up_bias.reshape(blocks, rows)
    key_bias_col = jnp.pad(keyval_bias, (0, rows - keyval_bias.shape[0]))
    vecs = [query_bias, out_bias, norm_attn_gain, norm_attn_bias, norm_mlp_gain, norm_mlp_bias, down_bias]
    vecs = jnp.concatenate([jnp.stack(vecs), up_bias_cols, key_bias_col[None]], 0)
    vecs = jnp.pad(vecs, ((0, LANES - vecs.shape[0]), (0, 0))).T
    first = Gather(jnp.concatenate([query_weight, keyval_weight, out_weight, vecs], 1), z_bits[::-1], xy, index_order)
    up_weight, down_weight = land([first], *launch([first], up_weight, down_weight))
    up_weight, down_weight = launch([first], up_weight, down_weight)
    up_local = up_weight.reshape(rows, shards, blocks, rows).transpose(0, 2, 1, 3).reshape(rows, ff)
    dn_local = down_weight.reshape(blocks, rows, width).transpose(1, 0, 2).reshape(rows, ff)
    up_local, dn_local = land([first], up_local, dn_local)
    for _ in z_bits[2:]:
        up_local, dn_local = land([first], *launch([first], up_local, dn_local))
    ups = Gather(up_local, z_bits[::-1], [x_bits + y_bits], index_order)
    dns = Gather(dn_local, z_bits[::-1], [y_bits + x_bits], index_order)
    (x,) = land([first, ups], *launch([first, ups], x))
    (x,) = land([first, dns], *launch([first, dns], x))
    while first.result is None:
        (x,) = land([first], *launch([first], x))

    tables = rotary_tables(seq_len, kv_width // 2)
    one, two = first.result
    q, kv, ha, hm, gy, gm, vec, w1 = beside(
        [ups, dns], lambda x: pre(info, x, cot, one, two, tables, kv_width, shards, half), x
    )
    pairs = width // LANES
    second = [ups, dns]
    state = beside(second, lambda q: attention(info, q, gm, kv, tables, None, 0, 2), q)
    (state,) = launch(second, state)
    for start in range(2, pairs, 2):
        state = attention(info, q, gm, kv, tables, state, start, 2)
    dkv, mixed, dq = land(second, *state)
    send, keep = beside(second, lambda mixed: attention_grads(info, ha, gy, mixed, dq, dkv, w1, shards, half), mixed)
    while any(s.result is None for s in second):
        send, keep = beside(second, lambda *v: v, send, keep)
    (up_rows,), (dn_rows,) = ups.result, dns.result

    attn = Scatter([(send, keep)], [z_bits[:1] + x_bits + y_bits], z_bits[1:], index_order)
    ff_part = lambda chunk, count: lambda hm, gy, *state: feed_forward(
        info, hm, gy, up_rows, dn_rows, vec, w1, state[0] if state else None, chunk, count, half
    )
    n0 = blocks // 2
    hm, gy = beside([attn], lambda *v: v, hm, gy)
    act0, gup0, state, send, keep = beside([attn], ff_part(0, n0), hm, gy)
    ff0 = Scatter([(send, keep)], xy, z_bits, index_order)
    hm, gy, state = launch([attn], hm, gy, state)
    hm, gy, state = beside([ff0], lambda *v: v, hm, gy, state)
    act1, gup1, _, send, keep = beside([ff0], ff_part(n0, blocks - n0), hm, gy, state)
    send, keep = land([attn], send, keep)
    ff1 = Scatter([(send, keep)], xy, z_bits, index_order)
    layer_out = beside(
        [ff0, ff1, attn],
        lambda x, *acts: layer_output(info, x, mixed, w1, dn_rows, vec, acts, width + kv_width, half),
        *(x, act0, act1),
    )
    gtok = beside(
        [ff1, ff0, attn],
        lambda cot, *gups: token_grads(info, x, cot, dq, dkv, w1, up_rows, vec, gups, half),
        *(cot, gup0, gup1),
    )
    streams = [attn, ff0, ff1]
    while any(s.result is None for s in streams):
        beside(streams, lambda *v: v)
    gq, gkv, go, gu, gd, *lines, g_up_bias = end(streams, width, kv_width, blocks, (n0, blocks - n0), shards)
    if shards * blocks > 128:
        gu = gu.reshape(rows, blocks, shards, rows).transpose(0, 2, 1, 3).reshape(rows, ff)
    bq, bkv, bo, ga, ba, g_gain, g_shift = (v.reshape(-1) for v in lines)
    return (
        layer_out.reshape(tokens.shape),
        gtok.reshape(tokens.shape),
        gq,
        bq,
        gkv,
        bkv,
        go,
        bo,
        ga,
        ba,
        g_gain,
        g_shift,
        gu,
        g_up_bias.reshape(-1),
        gd,
        bo,
    )


def solution(mesh):
    mat, vec, seq = P(BOTH, None), P(BOTH), P(BOTH, None, None)
    return jax.shard_map(
        body,
        mesh=mesh,
        in_specs=(seq, vec, seq, mat, vec, mat, vec, mat, vec, vec, vec, vec, vec, mat, vec, mat, vec),
        out_specs=(seq, seq, mat, vec, mat, vec, mat, vec, vec, vec, vec, vec, mat, vec, mat, vec),
        check_vma=False,
    )
```

```python
import functools

import jax
import jax.numpy as jnp
import numpy as np
from jax import lax
from jax.experimental import pallas as pl
from jax.experimental.pallas import tpu as pltpu
from jax.sharding import PartitionSpec as P

f32 = jnp.float32
bf16 = jnp.bfloat16

ROT = 16
EPS = 1e-05
NEG = -1e30
ROOT_HALF = 0.7071067811865476
INV_ROOT_TAU = 0.3989422804014327
LANES = 128
BOTH = ("dp", "fsdp")
VMEM = 28 * 1024 * 1024

SHIFT, INNER = 8, 9
QB, OB, GA, BA, GM, BM, DB, UB, KB = 0, 1, 2, 3, 4, 5, 6, 7, 11


def dot(a, b, ca, cb):
    return lax.dot_general(a, b, (((ca,), (cb,)), ((), ())), preferred_element_type=f32)


def params(**kw):
    return pltpu.CompilerParams(vmem_limit_bytes=VMEM, **kw)


def cost(us):
    return pl.CostEstimate(flops=int(us * 1.0e9), bytes_accessed=int(us * 3.0e6), transcendentals=0)


def in_hbm(*arrays):
    return [pltpu.with_memory_space_constraint(a, pltpu.HBM) for a in arrays]


def last_lanes(w):
    at = w.shape[1] // LANES - 1
    return pl.BlockSpec((w.shape[0], LANES), lambda *_: (0, at), pipeline_mode=pl.Buffered(1))


def whole(shape):
    return pl.BlockSpec(shape, lambda *_: (0,) * len(shape))


def rotary_tables(seq_len, head_dim):
    half = ROT // 2
    inverse_freq = np.float32(10000.0) ** (-(np.float32(2.0) * np.arange(half, dtype=np.float32)) / np.float32(ROT))
    angles = np.arange(seq_len, dtype=np.float32)[:, None] * inverse_freq[None, :]
    cos, sin = np.cos(angles.astype(np.float64)), np.sin(angles.astype(np.float64))
    tables = np.zeros((3, seq_len, LANES), np.float32)
    tables[0] = 1.0
    for at in range(0, LANES, head_dim):
        tables[0, :, at : at + half] = cos
        tables[0, :, at + half : at + ROT] = cos
        tables[1, :, at : at + half] = sin
        tables[2, :, at + half : at + ROT] = sin
    return jnp.asarray(tables)


def partners(v):
    half = ROT // 2
    return pltpu.roll(v, LANES - half, 1), pltpu.roll(v, half, 1)


def rotate(v, own, up, down):
    ahead, behind = partners(v)
    return v * own - ahead * up + behind * down


def rotate_back(v, own, up, down):
    ahead, behind = partners(v)
    return v * own + ahead * up - behind * down


def standardise(rows):
    average = jnp.mean(rows, axis=-1, keepdims=True)
    centred = rows - average
    scaled = lax.rsqrt(jnp.mean(centred * centred, axis=-1, keepdims=True) + EPS)
    return centred * scaled, scaled


def norm_back(grad, normed, scaled, gain):
    e = grad * gain
    return scaled * (
        e - jnp.mean(e, axis=-1, keepdims=True) - normed * jnp.mean(e * normed, axis=-1, keepdims=True)
    )


def col_sum(v):
    return jnp.sum(v, axis=0, keepdims=True)


def kept_rows(block, rows, length):
    pos = lax.broadcasted_iota(jnp.int32, (rows, 1), 0) + block * rows
    return (pos < length).astype(f32)


def spread_key_bias(width, kv_width, per_row, per_kv):
    row = lax.broadcasted_iota(jnp.int32, (width, kv_width), 0)
    col = lax.broadcasted_iota(jnp.int32, (width, kv_width), 1)
    owner = col // per_kv
    return (row == owner * per_row + (col - owner * per_kv)).astype(bf16)


def assemble(to, at, mine, other, core, half):
    for g in range(to.shape[0] // (2 * half)):
        rows, base = slice(g * half, (g + 1) * half), g * 2 * half
        to[pl.ds(pl.multiple_of(base + core * half, half), half), at] = mine[rows, :]
        to[pl.ds(pl.multiple_of(base + (1 - core) * half, half), half), at] = other[rows, :]


def pre_kernel(info, x_ref, cot_ref, a0, a1, b0, b1, tab_ref, q_ref, kv_ref, ha_ref, hm_ref, gy_ref, gm_ref, vec_ref, wq_ref, wo_ref, vec_s, *, dims, half):
    width, kv_width, rows, per_row, per_kv = dims
    i = pl.program_id(0)
    @pl.when(i == 0)
    def _():
        assemble(wq_ref, slice(None), a0, a1, info[1], half)
        assemble(wo_ref, slice(None), b0, b1, info[1], half)
        low = wo_ref[:, width:]
        lines = low.astype(f32).T[:16]
        vec_s[:16, :] = lines
        spread = spread_key_bias(width, kv_width, per_row, per_kv)
        vec_s[16:32, :kv_width] = dot(lines.astype(bf16), spread, 1, 0)
        vec_ref[...] = vec_s[...]

    normed, _ = standardise(x_ref[...].astype(f32))
    vec = vec_s[...]
    ha = (normed * vec[GA : GA + 1] + vec[BA : BA + 1]).astype(bf16)
    hm = (normed * vec[GM : GM + 1] + vec[BM : BM + 1]).astype(bf16)
    ha_ref[...] = ha
    hm_ref[...] = hm
    own, up, down = tab_ref[0], tab_ref[1], tab_ref[2]
    scale = (kv_width // 2) ** -0.5
    lin = dot(ha, wq_ref[...], 1, 0)
    query = lin[:, :width] + vec[QB : QB + 1]
    for p in range(width // LANES):
        cols = slice(p * LANES, (p + 1) * LANES)
        rot = rotate(query[:, cols], own, up, down).astype(bf16)
        q_ref[:, cols] = (rot.astype(f32) * scale).astype(bf16)
    lin = lin[:, width:] + vec[16 + KB : 17 + KB, :kv_width]
    lane = lax.broadcasted_iota(jnp.int32, (rows, kv_width), 1)
    kv_ref[...] = jnp.where(lane < kv_width // 2, rotate(lin, own, up, down), lin).astype(bf16)
    keep = kept_rows(i, rows, info[0])
    gy = (cot_ref[...].astype(f32) * keep).astype(bf16)
    gy_ref[...] = gy
    gm_ref[...] = dot(gy, wo_ref[:, :width], 1, 1).astype(bf16)


def pre(info, x, cot, a, b, tables, kv_width, shards, half):
    tokens, width = x.shape
    rows = 256
    blk = pl.BlockSpec((rows, width), lambda i, *_: (i, 0))
    kvb = pl.BlockSpec((rows, kv_width), lambda i, *_: (i, 0))
    dims = (width, kv_width, rows, width // shards, kv_width // shards)
    wide = jax.ShapeDtypeStruct((tokens, width), bf16)
    one = lambda v: pl.BlockSpec(v.shape, lambda *_: (0, 0), pipeline_mode=pl.Buffered(1))
    w_q, w_o = (width, width + kv_width), (width, width + LANES)
    return pl.pallas_call(
        functools.partial(pre_kernel, dims=dims, half=half),
        grid_spec=pltpu.PrefetchScalarGridSpec(
            num_scalar_prefetch=1,
            grid=(tokens // rows,),
            in_specs=[blk, blk, one(a[0]), one(a[1]), one(b[0]), one(b[1])]
            + [pl.BlockSpec((3, rows, LANES), lambda i, *_: (0, i, 0))],
            out_specs=[blk, kvb, blk, blk, blk, blk, whole((32, width)), whole(w_q), whole(w_o)],
            scratch_shapes=[pltpu.VMEM((32, width), f32)],
        ),
        out_shape=[
            wide,
            jax.ShapeDtypeStruct((tokens, kv_width), bf16),
            wide,
            wide,
            wide,
            wide,
            jax.ShapeDtypeStruct((32, width), f32),
            jax.ShapeDtypeStruct(w_q, bf16),
            jax.ShapeDtypeStruct(w_o, bf16),
        ],
        compiler_params=params(),
        cost_estimate=cost(9),
        name="pre",
    )(info, x, cot, *a, *b, tables)


def attn_kernel(len_ref, q_ref, gm_ref, kv_ref, tab_ref, *refs, qb, first, final):
    if not first:
        acc_in, refs = refs[0], refs[3:]
    mix_ref, dq_ref, dkv_ref, k0, k1, v0, v1, acc = refs
    p = pl.program_id(0)
    tokens, kv_width = kv_ref.shape
    head = kv_width // 2

    @pl.when(p == 0)
    def _():
        kv = kv_ref[...]
        zero = jnp.zeros((tokens, head), bf16)
        k, v = kv[:, :head], kv[:, head:]
        k0[...] = jnp.concatenate([k, zero], 1)
        k1[...] = jnp.concatenate([zero, k], 1)
        v0[...] = jnp.concatenate([v, zero], 1)
        v1[...] = jnp.concatenate([zero, v], 1)
        acc[...] = jnp.zeros_like(acc) if first else acc_in[...]

    last = len_ref[0] - 1
    scale = head**-0.5
    pads = ((k0, v0), (k1, v1))
    units = [(i, h) for i in range(tokens // qb) for h in range(LANES // head)]
    scored, weighed, mixes, dqs = {}, {}, {}, {}

    def score(unit):
        i, h = unit
        r, kn = pl.ds(i * qb, qb), (i + 1) * qb
        k, v = pads[h]
        scored[unit] = (dot(q_ref[r, :], k[:kn, :], 1, 1), dot(gm_ref[r, :], v[:kn, :], 1, 1))

    def weigh(unit):
        i, h = unit
        r, kn = pl.ds(i * qb, qb), (i + 1) * qb
        s, dp = scored.pop(unit)
        col = lax.broadcasted_iota(jnp.int32, (qb, kn), 1)
        limit = jnp.minimum(lax.broadcasted_iota(jnp.int32, (qb, 1), 0) + i * qb, last)
        s = jnp.where(col <= limit, s, NEG)
        e = jnp.exp(s - jnp.max(s, axis=1, keepdims=True))
        pr = e * (1.0 / jnp.sum(e, axis=1, keepdims=True))
        low = pr.astype(bf16)
        mixed = dot(low, pads[h][1][:kn, :], 1, 0)
        acc[head:, :kn] += dot(gm_ref[r, head * h : head * (h + 1)].T, low, 1, 0)
        weighed[unit] = (pr, dp, mixed)

    def back(unit):
        i, h = unit
        r, kn = pl.ds(i * qb, qb), (i + 1) * qb
        pr, dp, mixed = weighed.pop(unit)
        row = jnp.sum(gm_ref[r, :].astype(f32) * mixed, axis=1, keepdims=True)
        ds = (pr * (dp - row)).astype(bf16)
        dq = dot(ds, pads[h][0][:kn, :], 1, 0)
        acc[:head, :kn] += dot(q_ref[r, head * h : head * (h + 1)].T, ds, 1, 0)
        if h == 0:
            mixes[i], dqs[i] = mixed, dq
        else:
            mix_ref[r, :] = (mixes.pop(i) + mixed).astype(bf16)
            dq = (dqs.pop(i) + dq) * scale
            dq_ref[r, :] = rotate_back(dq, tab_ref[0, r, :], tab_ref[1, r, :], tab_ref[2, r, :]).astype(bf16)

    for t in range(len(units) + 3):
        for stage, lag in ((score, 0), (weigh, 1), (back, 3)):
            if 0 <= t - lag < len(units):
                stage(units[t - lag])

    @pl.when(p == pl.num_programs(0) - 1)
    def _():
        if not final:
            dkv_ref[...] = acc[...]
            return
        dkv = acc[...].T
        lanes = lax.broadcasted_iota(jnp.int32, (tokens, kv_width), 1)
        back = rotate_back(dkv, tab_ref[0], tab_ref[1], tab_ref[2])
        dkv_ref[...] = jnp.where(lanes < head, back, dkv).astype(bf16)


def attention(info, q, gm, kv, tables, state, start, count):
    tokens, width = q.shape
    kv_width = kv.shape[1]
    first, final = state is None, start + count == width // LANES
    blk = pl.BlockSpec((tokens, LANES), lambda p, *_: (0, p + start))
    wide = jax.ShapeDtypeStruct((tokens, width), bf16)
    sums = (kv_width, tokens)
    args, specs, alias = [q, gm, kv, tables], [blk, blk, whole((tokens, kv_width)), whole((3, tokens, LANES))], {}
    if not first:
        args += list(state)
        specs += [whole(sums), pl.BlockSpec(memory_space=pl.ANY), pl.BlockSpec(memory_space=pl.ANY)]
        alias = {6: 0, 7: 1}
    dkv = ((tokens, kv_width), bf16) if final else (sums, f32)
    mixed, dq, dkv = pl.pallas_call(
        functools.partial(attn_kernel, qb=256, first=first, final=final),
        grid_spec=pltpu.PrefetchScalarGridSpec(
            num_scalar_prefetch=1,
            grid=(count,),
            in_specs=specs,
            out_specs=[blk, blk, whole(dkv[0])],
            scratch_shapes=[pltpu.VMEM((tokens, LANES), bf16)] * 4 + [pltpu.VMEM(sums, f32)],
        ),
        out_shape=[wide, wide, jax.ShapeDtypeStruct(*dkv)],
        input_output_aliases=alias,
        compiler_params=params(),
        cost_estimate=cost(8 * count),
        name="attention",
    )(info, *args)
    return dkv, mixed, dq


def split_halves(send_ref, keep_ref, low_s, cols, at, core, half):
    for g in range(low_s.shape[0] // (2 * half)):
        to, base = pl.ds(g * half, half), g * 2 * half
        send_ref[to, at] = low_s[pl.ds(pl.multiple_of(base + (1 - core) * half, half), half), :cols]
        keep_ref[to, at] = low_s[pl.ds(pl.multiple_of(base + core * half, half), half), :cols]


def row_sum(v):
    return jnp.sum(v, axis=1, keepdims=True)


def grads_kernel(info, ha_ref, gy_ref, mix_ref, dq_ref, dkv_ref, w_ref, vec_ref, send_ref, keep_ref, sums, cols, low_s, *, dims, half):
    width, kv_width, step, per_row, per_kv = dims
    j = pl.program_id(0)
    c_out = width + kv_width
    c_vec = c_out + width
    core = info[1]

    @pl.when(j == 0)
    def _():
        cols[...] = jnp.zeros_like(cols)
        sums[...] = jnp.zeros_like(sums)

    def put(value, at, size):
        low_s[:, :size] = value.astype(bf16)
        split_halves(send_ref, keep_ref, low_s, size, pl.ds(at, size), core, half)

    def weight_sums(w, grad, lines):
        w = w.astype(f32)
        cols[:, SHIFT : SHIFT + 1] += row_sum(w * lines)
        cols[:, INNER : INNER + 1] += row_sum(w * grad)

    at = pl.multiple_of(j * step, LANES)
    grad = dot(ha_ref[...], dq_ref[...], 0, 0)
    lines = col_sum(dq_ref[...].astype(f32))
    sums[QB : QB + 1, pl.ds(at, step)] = lines
    sums[OB : OB + 1, pl.ds(at, step)] = col_sum(gy_ref[...].astype(f32))
    weight_sums(w_ref[:, pl.ds(at, step)], grad, lines)
    put(grad, at, step)
    put(dot(mix_ref[...], gy_ref[...], 0, 0), pl.multiple_of(c_out + at, LANES), step)

    @pl.when(j == pl.num_programs(0) - 1)
    def _():
        grad = dot(ha_ref[...], dkv_ref[...], 0, 0)
        lines = col_sum(dkv_ref[...].astype(f32))
        weight_sums(w_ref[:, width:c_out], grad, lines)
        put(grad, width, kv_width)
        vec = vec_ref[...].astype(f32)
        shift = cols[:, SHIFT : SHIFT + 1]
        gain = (cols[:, INNER : INNER + 1] - vec[:, BA : BA + 1] * shift) / vec[:, GA : GA + 1]
        spread = spread_key_bias(width, kv_width, per_row, per_kv)
        key = dot(jnp.broadcast_to(lines, (16, kv_width)).astype(bf16), spread, 1, 1)
        row = lax.broadcasted_iota(jnp.int32, (16, width), 0)
        both = jnp.where(row == 8, key, sums[...])
        both = jnp.concatenate([both, jnp.zeros((LANES - 16, width), f32)], 0).T
        lane = lax.broadcasted_iota(jnp.int32, (width, LANES), 1)
        put(jnp.where(lane == GA, gain, jnp.where(lane == BA, shift, both)), c_vec, LANES)


def attention_grads(info, ha, gy, mixed, dq, dkv, w_q, w_o, shards, half):
    tokens, width = ha.shape
    kv_width = dkv.shape[1]
    step = 2 * LANES
    one = lambda s: pl.BlockSpec(s, lambda *_: (0, 0), pipeline_mode=pl.Buffered(1))
    col = pl.BlockSpec((tokens, step), lambda j, *_: (0, j))
    dims = (width, kv_width, step, width // shards, kv_width // shards)
    cut = (width // 2, w_q.shape[1] + w_o.shape[1])
    return pl.pallas_call(
        functools.partial(grads_kernel, dims=dims, half=half),
        grid_spec=pltpu.PrefetchScalarGridSpec(
            num_scalar_prefetch=1,
            grid=(width // step,),
            in_specs=[one(ha.shape), col, one(mixed.shape), col, one(dkv.shape), one(w_q.shape), last_lanes(w_o)],
            out_specs=[one(cut), one(cut)],
            scratch_shapes=[
                pltpu.VMEM((16, width), f32),
                pltpu.VMEM((width, LANES), f32),
                pltpu.VMEM((width, step), bf16),
            ],
        ),
        out_shape=[jax.ShapeDtypeStruct(cut, bf16)] * 2,
        compiler_params=params(),
        cost_estimate=cost(8),
        name="attention_grads",
    )(info, ha, gy, mixed, dq, dkv, w_q, w_o)


def ff_kernel(*refs, rows, chunk, first, final, half):
    refs = list(refs)
    take = lambda k: [refs.pop(0) for _ in range(k)]
    info, hm_ref, gy_ref, u0, u1, d0, d1, vec_ref = take(8)
    (col_in,) = (None,) if first else take(1)
    (vcol_ref,) = take(1) if final else (None,)
    act_ref, gup_ref = take(2)
    (col_out,) = (None,) if final else take(1)
    send_ref, keep_ref, cols, low_s, wu_ref, wd_ref = refs
    j = pl.program_id(0)
    assemble(wu_ref, slice(None), u0, u1, info[1], half)
    assemble(wd_ref, slice(None), d0, d1, info[1], half)
    tokens, width = hm_ref.shape

    @pl.when(j == 0)
    def _():
        cols[...] = jnp.zeros_like(cols) if first else col_in[...]

    bias = vec_ref[pl.ds(UB + chunk + j, 1), :]
    total = jnp.zeros((1, width), f32)
    for i in range(tokens // rows):
        r = pl.ds(i * rows, rows)
        u = dot(hm_ref[r, :], wu_ref[...], 1, 0) + bias
        cdf = 0.5 * (1.0 + lax.erf(u * ROOT_HALF))
        pdf = jnp.exp(-0.5 * u * u) * INV_ROOT_TAU
        act_ref[r, :] = (u * cdf).astype(bf16)
        grad = (dot(gy_ref[r, :], wd_ref[...], 1, 1) * (cdf + u * pdf)).astype(bf16)
        gup_ref[r, :] = grad
        total = total + col_sum(grad.astype(f32))
    at = pl.multiple_of(j * 2 * width, LANES)
    d_up = dot(hm_ref[...], gup_ref[...], 0, 0)
    low_s[...] = d_up.astype(bf16)
    w_up = wu_ref[...].astype(f32)
    lane = lax.broadcasted_iota(jnp.int32, (width, LANES), 1)
    mine = jnp.where(lane == chunk + j, jnp.broadcast_to(total, (LANES, width)).T, 0.0)
    mine = jnp.where(lane == SHIFT, row_sum(w_up * total), mine)
    cols[...] += jnp.where(lane == INNER, row_sum(w_up * d_up), mine)
    split_halves(send_ref, keep_ref, low_s, width, pl.ds(at, width), info[1], half)
    low_s[...] = dot(act_ref[...], gy_ref[...], 0, 0).astype(bf16)
    at = pl.multiple_of(at + width, LANES)
    split_halves(send_ref, keep_ref, low_s, width, pl.ds(at, width), info[1], half)

    @pl.when(j == pl.num_programs(0) - 1)
    def _():
        if not final:
            col_out[...] = cols[...]
            return
        vec = vcol_ref[...].astype(f32)
        now = cols[...]
        gain = (now[:, INNER : INNER + 1] - vec[:, BM : BM + 1] * now[:, SHIFT : SHIFT + 1]) / vec[:, GM : GM + 1]
        low_s[:, :LANES] = jnp.where(lane == INNER, gain, now).astype(bf16)
        at = pl.ds(send_ref.shape[1] - LANES, LANES)
        split_halves(send_ref, keep_ref, low_s, LANES, at, info[1], half)


def feed_forward(info, hm, gy, up_rows, dn_rows, vec, w_o, state, chunk, count, half):
    tokens, width = hm.shape
    blocks = up_rows[0].shape[1] // width
    tok = (tokens, width)
    first, final = state is None, chunk + count == blocks
    one = lambda s: pl.BlockSpec(s, lambda *_: (0, 0), pipeline_mode=pl.Buffered(1))
    col = pl.BlockSpec(tok, lambda j, *_: (0, j))
    wgt = pl.BlockSpec((width // 2, width), lambda j, *_: (0, j + chunk))
    args = [hm, gy, *in_hbm(*up_rows, *dn_rows), vec]
    specs = [one(tok), one(tok), wgt, wgt, wgt, wgt, one(vec.shape)]
    if not first:
        args += [state]
        specs += [one((width, LANES))]
    if final:
        args += [w_o]
        specs += [last_lanes(w_o)]
    long = pltpu.HBM((tokens, count * width), bf16)
    shapes, outs = [long, long], [col, col]
    if not final:
        shapes += [jax.ShapeDtypeStruct((width, LANES), f32)]
        outs += [one((width, LANES))]
    cut = (width // 2, count * 2 * width + (LANES if final else 0))
    shapes += [jax.ShapeDtypeStruct(cut, bf16)] * 2
    outs += [one(cut)] * 2
    got = pl.pallas_call(
        functools.partial(ff_kernel, rows=256, chunk=chunk, first=first, final=final, half=half),
        grid_spec=pltpu.PrefetchScalarGridSpec(
            num_scalar_prefetch=1,
            grid=(count,),
            in_specs=specs,
            out_specs=outs,
            scratch_shapes=[pltpu.VMEM((width, LANES), f32)] + [pltpu.VMEM((width, width), bf16)] * 3,
        ),
        out_shape=shapes,
        compiler_params=params(),
        cost_estimate=cost(7 * count),
        name="feed_forward",
    )(info, *args)
    act, gup = got[:2]
    return act, gup, None if final else got[2], got[-2], got[-1]


def out_kernel(*refs, pieces, rows, half):
    info, x_ref, mix_ref, wo_ref, d0, d1, vec_ref = refs[:7]
    acts, out_ref, wd_ref = refs[7:-2], refs[-2], refs[-1]

    @pl.when(pl.program_id(0) == 0)
    def _():
        assemble(wd_ref, slice(None), d0, d1, info[1], half)

    width = x_ref.shape[1]
    total = dot(mix_ref[...], wo_ref[...], 1, 0) + vec_ref[OB : OB + 1] + vec_ref[DB : DB + 1]
    at = 0
    for act_ref, count in zip(acts, pieces):
        for k in range(count):
            act = act_ref[:, k * width : (k + 1) * width]
            total = total + dot(act, wd_ref[:, at : at + width], 1, 0)
            at += width
    keep = kept_rows(pl.program_id(0), rows, info[0])
    out_ref[...] = (x_ref[...].astype(f32) + keep * total).astype(bf16)


def layer_output(info, x, mixed, w_o, dn_rows, vec, acts, half):
    tokens, width = x.shape
    rows = 256
    long = dn_rows[0].shape[1]
    blk = lambda n: pl.BlockSpec((rows, n), lambda i, *_: (i, 0))
    one = lambda s, *at: pl.BlockSpec(s, lambda *_: at, pipeline_mode=pl.Buffered(1))
    return pl.pallas_call(
        functools.partial(out_kernel, pieces=[a.shape[1] // width for a in acts], rows=rows, half=half),
        grid_spec=pltpu.PrefetchScalarGridSpec(
            num_scalar_prefetch=1,
            grid=(tokens // rows,),
            in_specs=[blk(width), blk(width), one((width, width), 0, 0)]
            + [one((width // 2, long), 0, 0)] * 2
            + [one(vec.shape, 0, 0)]
            + [blk(a.shape[1]) for a in acts],
            out_specs=blk(width),
            scratch_shapes=[pltpu.VMEM((width, long), bf16)],
        ),
        out_shape=jax.ShapeDtypeStruct((tokens, width), bf16),
        compiler_params=params(),
        cost_estimate=cost(9),
        name="layer_output",
    )(info, x, mixed, w_o, *in_hbm(*dn_rows), vec, *in_hbm(*acts))


def token_kernel(*refs, pieces, kv_width, half):
    info, x_ref, cot_ref, dq_ref, dkv_ref, wq_ref, u0, u1, vec_ref = refs[:9]
    gups, out_ref, wu_ref = refs[9:-2], refs[-2], refs[-1]

    @pl.when(pl.program_id(0) == 0)
    def _():
        assemble(wu_ref, slice(None), u0, u1, info[1], half)

    width = x_ref.shape[1]
    normed, scaled = standardise(x_ref[...].astype(f32))
    grad = dot(dq_ref[...], wq_ref[:, :width], 1, 1) + dot(dkv_ref[...], wq_ref[:, width : width + kv_width], 1, 1)
    total = norm_back(grad, normed, scaled, vec_ref[GA : GA + 1])
    at, grad = 0, None
    for gup_ref, count in zip(gups, pieces):
        part = dot(gup_ref[...], wu_ref[:, at : at + count * width], 1, 1)
        grad = part if grad is None else grad + part
        at += count * width
    total = total + norm_back(grad, normed, scaled, vec_ref[GM : GM + 1])
    out_ref[...] = cot_ref[...].astype(f32) + total


def token_grads(info, x, cot, dq, dkv, w_q, up_rows, vec, gups, half):
    tokens, width = x.shape
    rows = 256
    long = up_rows[0].shape[1]
    blk = lambda n: pl.BlockSpec((rows, n), lambda i, *_: (i, 0))
    one = lambda s: pl.BlockSpec(s, lambda *_: (0, 0), pipeline_mode=pl.Buffered(1))
    pieces = [g.shape[1] // width for g in gups]
    return pl.pallas_call(
        functools.partial(token_kernel, pieces=pieces, kv_width=dkv.shape[1], half=half),
        grid_spec=pltpu.PrefetchScalarGridSpec(
            num_scalar_prefetch=1,
            grid=(tokens // rows,),
            in_specs=[blk(width), blk(width), blk(width), blk(dkv.shape[1]), one(w_q.shape)]
            + [one((width // 2, long))] * 2
            + [one(vec.shape)]
            + [blk(g.shape[1]) for g in gups],
            out_specs=blk(width),
            scratch_shapes=[pltpu.VMEM((width, long), bf16)],
        ),
        out_shape=jax.ShapeDtypeStruct((tokens, width), f32),
        compiler_params=params(),
        cost_estimate=cost(11),
        name="token_grads",
    )(info, x, cot, dq, dkv, w_q, *in_hbm(*up_rows), vec, *in_hbm(*gups))


def end_kernel(*refs, sizes, width, kv_width, blocks, counts, shards):
    terms, outs = list(refs[:-14]), refs[-14:]
    gq, gkv, go, gu, gd = outs[:5]
    sums = [sum(terms.pop(0)[...].astype(f32) for _ in range(size)) for size in sizes]
    rows = sums[0].shape[0]
    c_out = width + kv_width
    gq[...] = sums[0][:, :width]
    gkv[...] = sums[0][:, width:c_out]
    go[...] = sums[0][:, c_out : c_out + width]
    ups = []
    for part, count in zip(sums[1:], counts):
        for k in range(count):
            at = 2 * k * width
            gd[len(ups) * rows : (len(ups) + 1) * rows, :] = part[:, at + width : at + 2 * width]
            ups.append(part[:, at : at + width])
    if shards * blocks <= 128:
        pieces = [ups[q][:, i * rows : (i + 1) * rows] for i in range(shards) for q in range(blocks)]
        gu[...] = jnp.concatenate(pieces, 1)
    else:
        gu[...] = jnp.concatenate(ups, 1)
    square = lambda v: jnp.concatenate([v, jnp.zeros((LANES - rows, LANES), f32)], 0).T
    v1 = square(sums[0][:, c_out + width :])
    v2 = square(sums[-1][:, -LANES:])
    lines = [v1[QB], v1[8], v1[OB], v1[GA], v1[BA], v2[INNER], v2[SHIFT]]
    for ref, line in zip(outs[5:12], lines):
        ref[...] = line[None, : ref.shape[1]]
    outs[12][...] = jnp.concatenate([v2[q : q + 1, :rows] for q in range(blocks)], 1)
    outs[13][...] = outs[7][...]


def end(streams, width, kv_width, blocks, counts, shards):
    terms = [v for s in streams for v in s.result]
    sizes = [len(s.result) for s in streams]
    rows = terms[0].shape[0]
    ff = blocks * width
    shapes = [(rows, width), (rows, kv_width), (rows, width), (rows, ff), (blocks * rows, width)]
    shapes += [(1, rows), (1, kv_width // shards)] + [(1, rows)] * 5 + [(1, blocks * rows), (1, rows)]
    return pl.pallas_call(
        functools.partial(
            end_kernel, sizes=sizes, width=width, kv_width=kv_width, blocks=blocks, counts=counts, shards=shards
        ),
        out_shape=[jax.ShapeDtypeStruct(s, f32) for s in shapes],
        compiler_params=params(),
        cost_estimate=cost(3),
        name="end",
    )(*terms)


def bits_of(axis, size):
    return [(axis, b) for b in range(size.bit_length() - 1)]


def swap(v, axis, bit):
    size = lax.axis_size(axis)
    return lax.ppermute(v, axis, [(i, i ^ (1 << bit)) for i in range(size)])


def total(terms):
    return sum(t.astype(f32) for t in terms).astype(bf16)


def tie(*values):
    return lax.optimization_barrier(values)


class Scatter:
    def __init__(self, halves, parts, tail, index_order):
        self.index_order = index_order
        dims = [1 if b == ("dp", 0) else 2 for b in index_order]
        self.pending = []
        for send, keep in halves:
            rows = send.shape[0] >> (len(index_order) - 1)
            self.pending.append((send, [keep.reshape(*dims, rows, send.shape[1])]))
        self.cols = sum(send.shape[1] for send, _ in halves)
        self.steps = [[("dp", 0)] * len(halves)] + [list(s) for s in zip(*parts)] + [[b] for b in tail]
        self.flying = None
        self.result = None

    def ready(self):
        return [send for send, _ in self.pending]

    def set_ready(self, values):
        self.pending = [(send, keep) for send, (_, keep) in zip(values, self.pending)]

    def start(self):
        bits = self.steps.pop(0)
        self.flying = [(swap(send, *bit), keep) for (send, keep), bit in zip(self.pending, bits)]

    def arrived(self):
        return [got for got, _ in self.flying]

    def finish(self, arrived):
        parts = [keep + [got.reshape(keep[0].shape)] for got, (_, keep) in zip(arrived, self.flying)]
        if not self.steps:
            (terms,) = parts
            self.result = [t.reshape(-1, self.cols) for t in terms]
            return
        bits = self.steps[0]
        if len(parts) > len(bits):
            parts = [[jnp.concatenate([total(terms) for terms in parts], -1)]]
        if len(parts) < len(bits):
            (terms,) = parts
            step = self.cols // LANES // len(bits) * LANES
            edges = [k * step for k in range(len(bits))] + [self.cols]
            parts = [[t[..., lo:hi] for t in terms] for lo, hi in zip(edges, edges[1:])]
        self.pending = []
        for terms, (axis, bit) in zip(parts, bits):
            here, where = (lax.axis_index(axis) >> bit) & 1, self.index_order.index((axis, bit))
            send = total([lax.dynamic_slice_in_dim(t, 1 - here, 1, where) for t in terms])
            keep = [lax.dynamic_slice_in_dim(t, here, 1, where) for t in terms]
            if len(keep) > 2:
                keep = [total(keep)]
            self.pending.append((send.reshape(-1, send.shape[-1]), keep))


class Gather:
    def __init__(self, local, head, orders, index_order):
        self.index_order = index_order
        self.pending = [local.reshape((1,) * len(index_order) + local.shape)]
        self.steps = [[b] for b in head] + [list(s) for s in zip(*orders)] + [[("dp", 0)] * len(orders)]
        self.flying = None
        self.result = None

    def ready(self):
        return self.pending

    def set_ready(self, values):
        self.pending = values

    def start(self):
        bits = self.steps.pop(0)
        if len(bits) > len(self.pending):
            (cur,) = self.pending
            step = cur.shape[-1] // len(bits)
            self.pending = [cur[..., k * step : (k + 1) * step] for k in range(len(bits))]
        self.flying = [(swap(cur.reshape(-1, cur.shape[-1]), *bit), cur, bit) for cur, bit in zip(self.pending, bits)]

    def arrived(self):
        return [got for got, _, _ in self.flying]

    def finish(self, arrived):
        if not self.steps:
            self.result = [(cur.reshape(got.shape), got) for got, (_, cur, _) in zip(arrived, self.flying)]
            return
        self.pending = []
        for got, (_, cur, (axis, bit)) in zip(arrived, self.flying):
            got = got.reshape(cur.shape)
            here = (lax.axis_index(axis) >> bit) & 1
            low = jnp.where(here == 0, cur, got)
            high = jnp.where(here == 0, got, cur)
            self.pending.append(jnp.concatenate([low, high], self.index_order.index((axis, bit))))


def launch(streams, *values):
    streams = [s for s in streams if s.result is None]
    ready, values = tie([s.ready() for s in streams], values)
    for stream, sends in zip(streams, ready):
        stream.set_ready(sends)
        stream.start()
    return values


def land(streams, *values):
    streams = [s for s in streams if s.result is None]
    if any(isinstance(s, Gather) for s in streams):
        arrived, values = tie([s.arrived() for s in streams], values)
    else:
        arrived = [tie(s.arrived(), values)[0] for s in streams]
    for stream, got in zip(streams, arrived):
        stream.finish(got)
    return values


def beside(streams, work, *inputs):
    out = work(*launch(streams, *inputs))
    return land(streams, *out) if isinstance(out, (tuple, list)) else land(streams, out)[0]


def body(
    tokens,
    lengths,
    cotangent,
    query_weight,
    query_bias,
    keyval_weight,
    keyval_bias,
    out_weight,
    out_bias,
    norm_attn_gain,
    norm_attn_bias,
    norm_mlp_gain,
    norm_mlp_bias,
    up_weight,
    up_bias,
    down_weight,
    down_bias,
):
    n_dp, n_fsdp = lax.axis_size("dp"), lax.axis_size("fsdp")
    shards = n_dp * n_fsdp
    rows, width = query_weight.shape
    kv_width = keyval_weight.shape[1]
    ff = up_weight.shape[1]
    blocks = ff // width
    seq_len = tokens.shape[1]
    x = tokens.reshape(seq_len, width)
    cot = cotangent.reshape(seq_len, width)

    half = rows * n_fsdp
    info = jnp.concatenate([lengths, (lax.axis_index("dp") & 1)[None].astype(jnp.int32)])
    dp_bits, fs_bits = bits_of("dp", n_dp), bits_of("fsdp", n_fsdp)
    index_order = dp_bits[::-1] + fs_bits[::-1]
    x_bits, y_bits, z_bits = fs_bits[:1], dp_bits[1:], fs_bits[1:]
    xy = [x_bits + y_bits, y_bits + x_bits]

    up_bias_cols = up_bias.reshape(blocks, rows)
    key_bias_col = jnp.pad(keyval_bias, (0, rows - keyval_bias.shape[0]))
    vecs = [query_bias, out_bias, norm_attn_gain, norm_attn_bias, norm_mlp_gain, norm_mlp_bias, down_bias]
    vecs = jnp.concatenate([jnp.stack(vecs), up_bias_cols, key_bias_col[None]], 0)
    vecs = jnp.pad(vecs, ((0, LANES - vecs.shape[0]), (0, 0))).T
    first = Gather(jnp.concatenate([query_weight, keyval_weight, out_weight, vecs], 1), z_bits[::-1], xy, index_order)
    up_weight, down_weight = land([first], *launch([first], up_weight, down_weight))
    up_weight, down_weight = launch([first], up_weight, down_weight)
    up_local = up_weight.reshape(rows, shards, blocks, rows).transpose(0, 2, 1, 3).reshape(rows, ff)
    dn_local = down_weight.reshape(blocks, rows, width).transpose(1, 0, 2).reshape(rows, ff)
    up_local, dn_local = land([first], up_local, dn_local)
    for _ in z_bits[2:]:
        up_local, dn_local = land([first], *launch([first], up_local, dn_local))
    ups = Gather(up_local, z_bits[::-1], [x_bits + y_bits], index_order)
    dns = Gather(dn_local, z_bits[::-1], [y_bits + x_bits], index_order)
    (x,) = land([first, ups], *launch([first, ups], x))
    (x,) = land([first, dns], *launch([first, dns], x))
    while first.result is None:
        (x,) = land([first], *launch([first], x))

    tables = rotary_tables(seq_len, kv_width // 2)
    one, two = first.result
    q, kv, ha, hm, gy, gm, vec, w_q, w_o = beside(
        [ups, dns], lambda x: pre(info, x, cot, one, two, tables, kv_width, shards, half), x
    )
    pairs = width // LANES
    second = [ups, dns]
    state = beside(second, lambda q: attention(info, q, gm, kv, tables, None, 0, 2), q)
    (state,) = launch(second, state)
    for start in range(2, pairs, 2):
        state = attention(info, q, gm, kv, tables, state, start, 2)
    dkv, mixed, dq = land(second, *state)
    send, keep = beside(second, lambda mixed: attention_grads(info, ha, gy, mixed, dq, dkv, w_q, w_o, shards, half), mixed)
    while any(s.result is None for s in second):
        send, keep = beside(second, lambda *v: v, send, keep)
    (up_rows,), (dn_rows,) = ups.result, dns.result

    attn = Scatter([(send, keep)], [z_bits[:1] + x_bits + y_bits], z_bits[1:], index_order)
    ff_part = lambda chunk, count: lambda hm, gy, *state: feed_forward(
        info, hm, gy, up_rows, dn_rows, vec, w_o, state[0] if state else None, chunk, count, half
    )
    n0 = blocks // 2
    hm, gy = beside([attn], lambda *v: v, hm, gy)
    act0, gup0, state, send, keep = beside([attn], ff_part(0, n0), hm, gy)
    ff0 = Scatter([(send, keep)], xy, z_bits, index_order)
    hm, gy, state = launch([attn], hm, gy, state)
    hm, gy, state = beside([ff0], lambda *v: v, hm, gy, state)
    act1, gup1, _, send, keep = beside([ff0], ff_part(n0, blocks - n0), hm, gy, state)
    send, keep = land([attn], send, keep)
    ff1 = Scatter([(send, keep)], xy, z_bits, index_order)
    layer_out = beside(
        [ff0, ff1, attn],
        lambda x, *acts: layer_output(info, x, mixed, w_o, dn_rows, vec, acts, half),
        *(x, act0, act1),
    )
    gtok = beside(
        [ff1, ff0, attn],
        lambda cot, *gups: token_grads(info, x, cot, dq, dkv, w_q, up_rows, vec, gups, half),
        *(cot, gup0, gup1),
    )
    streams = [attn, ff0, ff1]
    while any(s.result is None for s in streams):
        beside(streams, lambda *v: v)
    gq, gkv, go, gu, gd, *lines = end(streams, width, kv_width, blocks, (n0, blocks - n0), shards)
    if shards * blocks > 128:
        gu = gu.reshape(rows, blocks, shards, rows).transpose(0, 2, 1, 3).reshape(rows, ff)
    bq, bkv, bo, ga, ba, g_gain, g_shift, b_up, b_dn = (v.reshape(-1) for v in lines)
    return (
        layer_out.reshape(tokens.shape),
        gtok.reshape(tokens.shape),
        gq,
        bq,
        gkv,
        bkv,
        go,
        bo,
        ga,
        ba,
        g_gain,
        g_shift,
        gu,
        b_up,
        gd,
        b_dn,
    )


def solution(mesh):
    mat, vec, seq = P(BOTH, None), P(BOTH), P(BOTH, None, None)
    return jax.shard_map(
        body,
        mesh=mesh,
        in_specs=(seq, vec, seq, mat, vec, mat, vec, mat, vec, vec, vec, vec, vec, mat, vec, mat, vec),
        out_specs=(seq, seq, mat, vec, mat, vec, mat, vec, vec, vec, vec, vec, mat, vec, mat, vec),
        check_vma=False,
    )
```

```python
import functools

import jax
import jax.numpy as jnp
import numpy as np
from jax import lax
from jax.experimental import pallas as pl
from jax.experimental.pallas import tpu as pltpu
from jax.sharding import PartitionSpec as P

f32 = jnp.float32
bf16 = jnp.bfloat16

ROT = 16
EPS = 1e-05
NEG = -1e30
ROOT_HALF = 0.7071067811865476
INV_ROOT_TAU = 0.3989422804014327
LANES = 128
BOTH = ("dp", "fsdp")
VMEM = 28 * 1024 * 1024

SHIFT, INNER = 8, 9
QB, OB, GA, BA, GM, BM, DB, UB, KB = 0, 1, 2, 3, 4, 5, 6, 7, 11


def dot(a, b, ca, cb):
    return lax.dot_general(a, b, (((ca,), (cb,)), ((), ())), preferred_element_type=f32)


def params(**kw):
    return pltpu.CompilerParams(vmem_limit_bytes=VMEM, **kw)


def cost(us):
    return pl.CostEstimate(flops=int(us * 1.0e9), bytes_accessed=int(us * 3.0e6), transcendentals=0)


def in_hbm(*arrays):
    return [pltpu.with_memory_space_constraint(a, pltpu.HBM) for a in arrays]


def last_lanes(w):
    at = w.shape[1] // LANES - 1
    return pl.BlockSpec((w.shape[0], LANES), lambda *_: (0, at), pipeline_mode=pl.Buffered(1))


def whole(shape):
    return pl.BlockSpec(shape, lambda *_: (0,) * len(shape))


def rotary_tables(seq_len, head_dim):
    half = ROT // 2
    inverse_freq = np.float32(10000.0) ** (-(np.float32(2.0) * np.arange(half, dtype=np.float32)) / np.float32(ROT))
    angles = np.arange(seq_len, dtype=np.float32)[:, None] * inverse_freq[None, :]
    cos, sin = np.cos(angles.astype(np.float64)), np.sin(angles.astype(np.float64))
    tables = np.zeros((3, seq_len, LANES), np.float32)
    tables[0] = 1.0
    for at in range(0, LANES, head_dim):
        tables[0, :, at : at + half] = cos
        tables[0, :, at + half : at + ROT] = cos
        tables[1, :, at : at + half] = sin
        tables[2, :, at + half : at + ROT] = sin
    return jnp.asarray(tables)


def partners(v):
    half = ROT // 2
    return pltpu.roll(v, LANES - half, 1), pltpu.roll(v, half, 1)


def rotate(v, own, up, down):
    ahead, behind = partners(v)
    return v * own - ahead * up + behind * down


def rotate_back(v, own, up, down):
    ahead, behind = partners(v)
    return v * own + ahead * up - behind * down


def standardise(rows):
    average = jnp.mean(rows, axis=-1, keepdims=True)
    centred = rows - average
    scaled = lax.rsqrt(jnp.mean(centred * centred, axis=-1, keepdims=True) + EPS)
    return centred * scaled, scaled


def norm_back(grad, normed, scaled, gain):
    e = grad * gain
    return scaled * (
        e - jnp.mean(e, axis=-1, keepdims=True) - normed * jnp.mean(e * normed, axis=-1, keepdims=True)
    )


def col_sum(v):
    return jnp.sum(v, axis=0, keepdims=True)


def kept_rows(block, rows, length):
    pos = lax.broadcasted_iota(jnp.int32, (rows, 1), 0) + block * rows
    return (pos < length).astype(f32)


def spread_key_bias(width, kv_width, per_row, per_kv):
    row = lax.broadcasted_iota(jnp.int32, (width, kv_width), 0)
    col = lax.broadcasted_iota(jnp.int32, (width, kv_width), 1)
    owner = col // per_kv
    return (row == owner * per_row + (col - owner * per_kv)).astype(bf16)


def assemble(to, at, mine, other, core, half):
    for g in range(to.shape[0] // (2 * half)):
        rows, base = slice(g * half, (g + 1) * half), g * 2 * half
        to[pl.ds(pl.multiple_of(base + core * half, half), half), at] = mine[rows, :]
        to[pl.ds(pl.multiple_of(base + (1 - core) * half, half), half), at] = other[rows, :]


def pre_kernel(info, x_ref, cot_ref, a0, a1, b0, b1, tab_ref, q_ref, kv_ref, ha_ref, hm_ref, gy_ref, gm_ref, vec_ref, wq_ref, wo_ref, vec_s, *, dims, half):
    width, kv_width, rows, per_row, per_kv = dims
    i = pl.program_id(0)
    @pl.when(i == 0)
    def _():
        assemble(wq_ref, slice(None), a0, a1, info[1], half)
        assemble(wo_ref, slice(None), b0, b1, info[1], half)
        low = wo_ref[:, width:]
        lines = low.astype(f32).T[:16]
        vec_s[:16, :] = lines
        spread = spread_key_bias(width, kv_width, per_row, per_kv)
        vec_s[16:32, :kv_width] = dot(lines.astype(bf16), spread, 1, 0)
        vec_ref[...] = vec_s[...]

    normed, _ = standardise(x_ref[...].astype(f32))
    vec = vec_s[...]
    ha = (normed * vec[GA : GA + 1] + vec[BA : BA + 1]).astype(bf16)
    hm = (normed * vec[GM : GM + 1] + vec[BM : BM + 1]).astype(bf16)
    ha_ref[...] = ha
    hm_ref[...] = hm
    own, up, down = tab_ref[0], tab_ref[1], tab_ref[2]
    scale = (kv_width // 2) ** -0.5
    lin = dot(ha, wq_ref[...], 1, 0)
    query = lin[:, :width] + vec[QB : QB + 1]
    for p in range(width // LANES):
        cols = slice(p * LANES, (p + 1) * LANES)
        rot = rotate(query[:, cols], own, up, down).astype(bf16)
        q_ref[:, cols] = (rot.astype(f32) * scale).astype(bf16)
    lin = lin[:, width:] + vec[16 + KB : 17 + KB, :kv_width]
    lane = lax.broadcasted_iota(jnp.int32, (rows, kv_width), 1)
    kv_ref[...] = jnp.where(lane < kv_width // 2, rotate(lin, own, up, down), lin).astype(bf16)
    keep = kept_rows(i, rows, info[0])
    gy = (cot_ref[...].astype(f32) * keep).astype(bf16)
    gy_ref[...] = gy
    gm_ref[...] = dot(gy, wo_ref[:, :width], 1, 1).astype(bf16)


def pre(info, x, cot, a, b, tables, kv_width, shards, half):
    tokens, width = x.shape
    rows = 256
    blk = pl.BlockSpec((rows, width), lambda i, *_: (i, 0))
    kvb = pl.BlockSpec((rows, kv_width), lambda i, *_: (i, 0))
    dims = (width, kv_width, rows, width // shards, kv_width // shards)
    wide = jax.ShapeDtypeStruct((tokens, width), bf16)
    one = lambda v: pl.BlockSpec(v.shape, lambda *_: (0, 0), pipeline_mode=pl.Buffered(1))
    w_q, w_o = (width, width + kv_width), (width, width + LANES)
    return pl.pallas_call(
        functools.partial(pre_kernel, dims=dims, half=half),
        grid_spec=pltpu.PrefetchScalarGridSpec(
            num_scalar_prefetch=1,
            grid=(tokens // rows,),
            in_specs=[blk, blk, one(a[0]), one(a[1]), one(b[0]), one(b[1])]
            + [pl.BlockSpec((3, rows, LANES), lambda i, *_: (0, i, 0))],
            out_specs=[blk, kvb, blk, blk, blk, blk, whole((32, width)), whole(w_q), whole(w_o)],
            scratch_shapes=[pltpu.VMEM((32, width), f32)],
        ),
        out_shape=[
            wide,
            jax.ShapeDtypeStruct((tokens, kv_width), bf16),
            wide,
            wide,
            wide,
            wide,
            jax.ShapeDtypeStruct((32, width), f32),
            jax.ShapeDtypeStruct(w_q, bf16),
            jax.ShapeDtypeStruct(w_o, bf16),
        ],
        compiler_params=params(),
        cost_estimate=cost(9),
        name="pre",
    )(info, x, cot, *a, *b, tables)


def attn_kernel(len_ref, q_ref, gm_ref, kv_ref, tab_ref, *refs, qb, first, final):
    if not first:
        acc_in, refs = refs[0], refs[3:]
    mix_ref, dq_ref, dkv_ref, k0, k1, v0, v1, acc = refs
    p = pl.program_id(0)
    tokens, kv_width = kv_ref.shape
    head = kv_width // 2

    @pl.when(p == 0)
    def _():
        kv = kv_ref[...]
        zero = jnp.zeros((tokens, head), bf16)
        k, v = kv[:, :head], kv[:, head:]
        k0[...] = jnp.concatenate([k, zero], 1)
        k1[...] = jnp.concatenate([zero, k], 1)
        v0[...] = jnp.concatenate([v, zero], 1)
        v1[...] = jnp.concatenate([zero, v], 1)
        acc[...] = jnp.zeros_like(acc) if first else acc_in[...]

    last = len_ref[0] - 1
    scale = head**-0.5
    pads = ((k0, v0), (k1, v1))
    units = [(i, h) for i in range(tokens // qb) for h in range(LANES // head)]
    scored, weighed, mixes, dqs = {}, {}, {}, {}

    def score(unit):
        i, h = unit
        r, kn = pl.ds(i * qb, qb), (i + 1) * qb
        k, v = pads[h]
        scored[unit] = (dot(q_ref[r, :], k[:kn, :], 1, 1), dot(gm_ref[r, :], v[:kn, :], 1, 1))

    def weigh(unit):
        i, h = unit
        r, kn = pl.ds(i * qb, qb), (i + 1) * qb
        s, dp = scored.pop(unit)
        col = lax.broadcasted_iota(jnp.int32, (qb, kn), 1)
        limit = jnp.minimum(lax.broadcasted_iota(jnp.int32, (qb, 1), 0) + i * qb, last)
        s = jnp.where(col <= limit, s, NEG)
        e = jnp.exp(s - jnp.max(s, axis=1, keepdims=True))
        pr = e * (1.0 / jnp.sum(e, axis=1, keepdims=True))
        low = pr.astype(bf16)
        mixed = dot(low, pads[h][1][:kn, :], 1, 0)
        acc[head:, :kn] += dot(gm_ref[r, head * h : head * (h + 1)].T, low, 1, 0)
        weighed[unit] = (pr, dp, mixed)

    def back(unit):
        i, h = unit
        r, kn = pl.ds(i * qb, qb), (i + 1) * qb
        pr, dp, mixed = weighed.pop(unit)
        row = jnp.sum(gm_ref[r, :].astype(f32) * mixed, axis=1, keepdims=True)
        ds = (pr * (dp - row)).astype(bf16)
        dq = dot(ds, pads[h][0][:kn, :], 1, 0)
        acc[:head, :kn] += dot(q_ref[r, head * h : head * (h + 1)].T, ds, 1, 0)
        if h == 0:
            mixes[i], dqs[i] = mixed, dq
        else:
            mix_ref[r, :] = (mixes.pop(i) + mixed).astype(bf16)
            dq = (dqs.pop(i) + dq) * scale
            dq_ref[r, :] = rotate_back(dq, tab_ref[0, r, :], tab_ref[1, r, :], tab_ref[2, r, :]).astype(bf16)

    for t in range(len(units) + 3):
        for stage, lag in ((score, 0), (weigh, 1), (back, 3)):
            if 0 <= t - lag < len(units):
                stage(units[t - lag])

    @pl.when(p == pl.num_programs(0) - 1)
    def _():
        if not final:
            dkv_ref[...] = acc[...]
            return
        dkv = acc[...].T
        lanes = lax.broadcasted_iota(jnp.int32, (tokens, kv_width), 1)
        back = rotate_back(dkv, tab_ref[0], tab_ref[1], tab_ref[2])
        dkv_ref[...] = jnp.where(lanes < head, back, dkv).astype(bf16)


def attention(info, q, gm, kv, tables, state, start, count):
    tokens, width = q.shape
    kv_width = kv.shape[1]
    first, final = state is None, start + count == width // LANES
    blk = pl.BlockSpec((tokens, LANES), lambda p, *_: (0, p + start))
    wide = jax.ShapeDtypeStruct((tokens, width), bf16)
    sums = (kv_width, tokens)
    args, specs, alias = [q, gm, kv, tables], [blk, blk, whole((tokens, kv_width)), whole((3, tokens, LANES))], {}
    if not first:
        args += list(state)
        specs += [whole(sums), pl.BlockSpec(memory_space=pl.ANY), pl.BlockSpec(memory_space=pl.ANY)]
        alias = {6: 0, 7: 1}
    dkv = ((tokens, kv_width), bf16) if final else (sums, f32)
    mixed, dq, dkv = pl.pallas_call(
        functools.partial(attn_kernel, qb=256, first=first, final=final),
        grid_spec=pltpu.PrefetchScalarGridSpec(
            num_scalar_prefetch=1,
            grid=(count,),
            in_specs=specs,
            out_specs=[blk, blk, whole(dkv[0])],
            scratch_shapes=[pltpu.VMEM((tokens, LANES), bf16)] * 4 + [pltpu.VMEM(sums, f32)],
        ),
        out_shape=[wide, wide, jax.ShapeDtypeStruct(*dkv)],
        input_output_aliases=alias,
        compiler_params=params(),
        cost_estimate=cost(8 * count),
        name="attention",
    )(info, *args)
    return dkv, mixed, dq


def split_halves(send_ref, keep_ref, low_s, cols, at, core, half):
    for g in range(low_s.shape[0] // (2 * half)):
        to, base = pl.ds(g * half, half), g * 2 * half
        send_ref[to, at] = low_s[pl.ds(pl.multiple_of(base + (1 - core) * half, half), half), :cols]
        keep_ref[to, at] = low_s[pl.ds(pl.multiple_of(base + core * half, half), half), :cols]


def row_sum(v):
    return jnp.sum(v, axis=1, keepdims=True)


def grads_kernel(info, ha_ref, gy_ref, mix_ref, dq_ref, dkv_ref, w_ref, vec_ref, send_ref, keep_ref, sums, cols, low_s, *, dims, half):
    width, kv_width, step, per_row, per_kv = dims
    j = pl.program_id(0)
    c_out = width + kv_width
    c_vec = c_out + width
    core = info[1]

    @pl.when(j == 0)
    def _():
        cols[...] = jnp.zeros_like(cols)
        sums[...] = jnp.zeros_like(sums)

    def put(value, at, size):
        low_s[:, :size] = value.astype(bf16)
        split_halves(send_ref, keep_ref, low_s, size, pl.ds(at, size), core, half)

    def weight_sums(w, grad, lines):
        w = w.astype(f32)
        cols[:, SHIFT : SHIFT + 1] += row_sum(w * lines)
        cols[:, INNER : INNER + 1] += row_sum(w * grad)

    at = pl.multiple_of(j * step, LANES)
    grad = dot(ha_ref[...], dq_ref[...], 0, 0)
    lines = col_sum(dq_ref[...].astype(f32))
    sums[QB : QB + 1, pl.ds(at, step)] = lines
    sums[OB : OB + 1, pl.ds(at, step)] = col_sum(gy_ref[...].astype(f32))
    weight_sums(w_ref[:, pl.ds(at, step)], grad, lines)
    put(grad, at, step)
    put(dot(mix_ref[...], gy_ref[...], 0, 0), pl.multiple_of(c_out + at, LANES), step)

    @pl.when(j == pl.num_programs(0) - 1)
    def _():
        grad = dot(ha_ref[...], dkv_ref[...], 0, 0)
        lines = col_sum(dkv_ref[...].astype(f32))
        weight_sums(w_ref[:, width:c_out], grad, lines)
        put(grad, width, kv_width)
        vec = vec_ref[...].astype(f32)
        shift = cols[:, SHIFT : SHIFT + 1]
        gain = (cols[:, INNER : INNER + 1] - vec[:, BA : BA + 1] * shift) / vec[:, GA : GA + 1]
        spread = spread_key_bias(width, kv_width, per_row, per_kv)
        key = dot(jnp.broadcast_to(lines, (16, kv_width)).astype(bf16), spread, 1, 1)
        row = lax.broadcasted_iota(jnp.int32, (16, width), 0)
        both = jnp.where(row == 8, key, sums[...])
        both = jnp.concatenate([both, jnp.zeros((LANES - 16, width), f32)], 0).T
        lane = lax.broadcasted_iota(jnp.int32, (width, LANES), 1)
        put(jnp.where(lane == GA, gain, jnp.where(lane == BA, shift, both)), c_vec, LANES)


def attention_grads(info, ha, gy, mixed, dq, dkv, w_q, w_o, shards, half):
    tokens, width = ha.shape
    kv_width = dkv.shape[1]
    step = 2 * LANES
    one = lambda s: pl.BlockSpec(s, lambda *_: (0, 0), pipeline_mode=pl.Buffered(1))
    col = pl.BlockSpec((tokens, step), lambda j, *_: (0, j))
    dims = (width, kv_width, step, width // shards, kv_width // shards)
    cut = (width // 2, w_q.shape[1] + w_o.shape[1])
    return pl.pallas_call(
        functools.partial(grads_kernel, dims=dims, half=half),
        grid_spec=pltpu.PrefetchScalarGridSpec(
            num_scalar_prefetch=1,
            grid=(width // step,),
            in_specs=[one(ha.shape), col, one(mixed.shape), col, one(dkv.shape), one(w_q.shape), last_lanes(w_o)],
            out_specs=[one(cut), one(cut)],
            scratch_shapes=[
                pltpu.VMEM((16, width), f32),
                pltpu.VMEM((width, LANES), f32),
                pltpu.VMEM((width, step), bf16),
            ],
        ),
        out_shape=[jax.ShapeDtypeStruct(cut, bf16)] * 2,
        compiler_params=params(),
        cost_estimate=cost(8),
        name="attention_grads",
    )(info, ha, gy, mixed, dq, dkv, w_q, w_o)


def ff_kernel(*refs, rows, chunk, first, final, half):
    refs = list(refs)
    take = lambda k: [refs.pop(0) for _ in range(k)]
    info, hm_ref, gy_ref, u0, u1, d0, d1, vec_ref = take(8)
    (col_in,) = (None,) if first else take(1)
    (vcol_ref,) = take(1) if final else (None,)
    act_ref, gup_ref = take(2)
    (col_out,) = (None,) if final else take(1)
    send_ref, keep_ref, cols, low_s, wu_ref, wd_ref = refs
    j = pl.program_id(0)
    assemble(wu_ref, slice(None), u0, u1, info[1], half)
    assemble(wd_ref, slice(None), d0, d1, info[1], half)
    tokens, width = hm_ref.shape

    @pl.when(j == 0)
    def _():
        cols[...] = jnp.zeros_like(cols) if first else col_in[...]

    bias = vec_ref[pl.ds(UB + chunk + j, 1), :]
    total = jnp.zeros((1, width), f32)
    for i in range(tokens // rows):
        r = pl.ds(i * rows, rows)
        u = dot(hm_ref[r, :], wu_ref[...], 1, 0) + bias
        cdf = 0.5 * (1.0 + lax.erf(u * ROOT_HALF))
        pdf = jnp.exp(-0.5 * u * u) * INV_ROOT_TAU
        act_ref[r, :] = (u * cdf).astype(bf16)
        grad = (dot(gy_ref[r, :], wd_ref[...], 1, 1) * (cdf + u * pdf)).astype(bf16)
        gup_ref[r, :] = grad
        total = total + col_sum(grad.astype(f32))
    at = pl.multiple_of(j * 2 * width, LANES)
    d_up = dot(hm_ref[...], gup_ref[...], 0, 0)
    low_s[...] = d_up.astype(bf16)
    w_up = wu_ref[...].astype(f32)
    lane = lax.broadcasted_iota(jnp.int32, (width, LANES), 1)
    mine = jnp.where(lane == chunk + j, jnp.broadcast_to(total, (LANES, width)).T, 0.0)
    mine = jnp.where(lane == SHIFT, row_sum(w_up * total), mine)
    cols[...] += jnp.where(lane == INNER, row_sum(w_up * d_up), mine)
    split_halves(send_ref, keep_ref, low_s, width, pl.ds(at, width), info[1], half)
    low_s[...] = dot(act_ref[...], gy_ref[...], 0, 0).astype(bf16)
    at = pl.multiple_of(at + width, LANES)
    split_halves(send_ref, keep_ref, low_s, width, pl.ds(at, width), info[1], half)

    @pl.when(j == pl.num_programs(0) - 1)
    def _():
        if not final:
            col_out[...] = cols[...]
            return
        vec = vcol_ref[...].astype(f32)
        now = cols[...]
        gain = (now[:, INNER : INNER + 1] - vec[:, BM : BM + 1] * now[:, SHIFT : SHIFT + 1]) / vec[:, GM : GM + 1]
        low_s[:, :LANES] = jnp.where(lane == INNER, gain, now).astype(bf16)
        at = pl.ds(send_ref.shape[1] - LANES, LANES)
        split_halves(send_ref, keep_ref, low_s, LANES, at, info[1], half)


def feed_forward(info, hm, gy, up_rows, dn_rows, vec, w_o, state, chunk, count, half):
    tokens, width = hm.shape
    blocks = up_rows[0].shape[1] // width
    tok = (tokens, width)
    first, final = state is None, chunk + count == blocks
    one = lambda s: pl.BlockSpec(s, lambda *_: (0, 0), pipeline_mode=pl.Buffered(1))
    col = pl.BlockSpec(tok, lambda j, *_: (0, j))
    wgt = pl.BlockSpec((width // 2, width), lambda j, *_: (0, j + chunk))
    args = [hm, gy, *in_hbm(*up_rows, *dn_rows), vec]
    specs = [one(tok), one(tok), wgt, wgt, wgt, wgt, one(vec.shape)]
    if not first:
        args += [state]
        specs += [one((width, LANES))]
    if final:
        args += [w_o]
        specs += [last_lanes(w_o)]
    long = pltpu.HBM((tokens, count * width), bf16)
    shapes, outs = [long, long], [col, col]
    if not final:
        shapes += [jax.ShapeDtypeStruct((width, LANES), f32)]
        outs += [one((width, LANES))]
    cut = (width // 2, count * 2 * width + (LANES if final else 0))
    shapes += [jax.ShapeDtypeStruct(cut, bf16)] * 2
    outs += [one(cut)] * 2
    got = pl.pallas_call(
        functools.partial(ff_kernel, rows=256, chunk=chunk, first=first, final=final, half=half),
        grid_spec=pltpu.PrefetchScalarGridSpec(
            num_scalar_prefetch=1,
            grid=(count,),
            in_specs=specs,
            out_specs=outs,
            scratch_shapes=[pltpu.VMEM((width, LANES), f32)] + [pltpu.VMEM((width, width), bf16)] * 3,
        ),
        out_shape=shapes,
        compiler_params=params(),
        cost_estimate=cost(7 * count),
        name="feed_forward",
    )(info, *args)
    act, gup = got[:2]
    return act, gup, None if final else got[2], got[-2], got[-1]


def out_kernel(*refs, pieces, rows, half):
    info, x_ref, mix_ref, wo_ref, d0, d1, vec_ref = refs[:7]
    acts, out_ref, wd_ref = refs[7:-2], refs[-2], refs[-1]

    @pl.when(pl.program_id(0) == 0)
    def _():
        assemble(wd_ref, slice(None), d0, d1, info[1], half)

    width = x_ref.shape[1]
    total = dot(mix_ref[...], wo_ref[...], 1, 0) + vec_ref[OB : OB + 1] + vec_ref[DB : DB + 1]
    at = 0
    for act_ref, count in zip(acts, pieces):
        for k in range(count):
            act = act_ref[:, k * width : (k + 1) * width]
            total = total + dot(act, wd_ref[:, at : at + width], 1, 0)
            at += width
    keep = kept_rows(pl.program_id(0), rows, info[0])
    out_ref[...] = (x_ref[...].astype(f32) + keep * total).astype(bf16)


def layer_output(info, x, mixed, w_o, dn_rows, vec, acts, half):
    tokens, width = x.shape
    rows = 256
    long = dn_rows[0].shape[1]
    blk = lambda n: pl.BlockSpec((rows, n), lambda i, *_: (i, 0))
    one = lambda s, *at: pl.BlockSpec(s, lambda *_: at, pipeline_mode=pl.Buffered(1))
    return pl.pallas_call(
        functools.partial(out_kernel, pieces=[a.shape[1] // width for a in acts], rows=rows, half=half),
        grid_spec=pltpu.PrefetchScalarGridSpec(
            num_scalar_prefetch=1,
            grid=(tokens // rows,),
            in_specs=[blk(width), blk(width), one((width, width), 0, 0)]
            + [one((width // 2, long), 0, 0)] * 2
            + [one(vec.shape, 0, 0)]
            + [blk(a.shape[1]) for a in acts],
            out_specs=blk(width),
            scratch_shapes=[pltpu.VMEM((width, long), bf16)],
        ),
        out_shape=jax.ShapeDtypeStruct((tokens, width), bf16),
        compiler_params=params(),
        cost_estimate=cost(9),
        name="layer_output",
    )(info, x, mixed, w_o, *in_hbm(*dn_rows), vec, *in_hbm(*acts))


def token_kernel(*refs, pieces, kv_width, half):
    info, x_ref, cot_ref, dq_ref, dkv_ref, wq_ref, u0, u1, vec_ref = refs[:9]
    gups, out_ref, wu_ref = refs[9:-2], refs[-2], refs[-1]

    @pl.when(pl.program_id(0) == 0)
    def _():
        assemble(wu_ref, slice(None), u0, u1, info[1], half)

    width = x_ref.shape[1]
    normed, scaled = standardise(x_ref[...].astype(f32))
    grad = dot(dq_ref[...], wq_ref[:, :width], 1, 1) + dot(dkv_ref[...], wq_ref[:, width : width + kv_width], 1, 1)
    total = norm_back(grad, normed, scaled, vec_ref[GA : GA + 1])
    at, grad = 0, None
    for gup_ref, count in zip(gups, pieces):
        part = dot(gup_ref[...], wu_ref[:, at : at + count * width], 1, 1)
        grad = part if grad is None else grad + part
        at += count * width
    total = total + norm_back(grad, normed, scaled, vec_ref[GM : GM + 1])
    out_ref[...] = cot_ref[...].astype(f32) + total


def token_grads(info, x, cot, dq, dkv, w_q, up_rows, vec, gups, half):
    tokens, width = x.shape
    rows = 256
    long = up_rows[0].shape[1]
    blk = lambda n: pl.BlockSpec((rows, n), lambda i, *_: (i, 0))
    one = lambda s: pl.BlockSpec(s, lambda *_: (0, 0), pipeline_mode=pl.Buffered(1))
    pieces = [g.shape[1] // width for g in gups]
    return pl.pallas_call(
        functools.partial(token_kernel, pieces=pieces, kv_width=dkv.shape[1], half=half),
        grid_spec=pltpu.PrefetchScalarGridSpec(
            num_scalar_prefetch=1,
            grid=(tokens // rows,),
            in_specs=[blk(width), blk(width), blk(width), blk(dkv.shape[1]), one(w_q.shape)]
            + [one((width // 2, long))] * 2
            + [one(vec.shape)]
            + [blk(g.shape[1]) for g in gups],
            out_specs=blk(width),
            scratch_shapes=[pltpu.VMEM((width, long), bf16)],
        ),
        out_shape=jax.ShapeDtypeStruct((tokens, width), f32),
        compiler_params=params(),
        cost_estimate=cost(11),
        name="token_grads",
    )(info, x, cot, dq, dkv, w_q, *in_hbm(*up_rows), vec, *in_hbm(*gups))


def end_kernel(*refs, sizes, width, kv_width, blocks, counts, shards):
    terms, outs = list(refs[:-14]), refs[-14:]
    gq, gkv, go, gu, gd = outs[:5]
    sums = [sum(terms.pop(0)[...].astype(f32) for _ in range(size)) for size in sizes]
    rows = sums[0].shape[0]
    c_out = width + kv_width
    gq[...] = sums[0][:, :width]
    gkv[...] = sums[0][:, width:c_out]
    go[...] = sums[0][:, c_out : c_out + width]
    ups = []
    for part, count in zip(sums[1:], counts):
        for k in range(count):
            at = 2 * k * width
            gd[len(ups) * rows : (len(ups) + 1) * rows, :] = part[:, at + width : at + 2 * width]
            ups.append(part[:, at : at + width])
    if shards * blocks <= 128:
        pieces = [ups[q][:, i * rows : (i + 1) * rows] for i in range(shards) for q in range(blocks)]
        gu[...] = jnp.concatenate(pieces, 1)
    else:
        gu[...] = jnp.concatenate(ups, 1)
    square = lambda v: jnp.concatenate([v, jnp.zeros((LANES - rows, LANES), f32)], 0).T
    v1 = square(sums[0][:, c_out + width :])
    v2 = square(sums[-1][:, -LANES:])
    lines = [v1[QB], v1[8], v1[OB], v1[GA], v1[BA], v2[INNER], v2[SHIFT]]
    for ref, line in zip(outs[5:12], lines):
        ref[...] = line[None, : ref.shape[1]]
    outs[12][...] = jnp.concatenate([v2[q : q + 1, :rows] for q in range(blocks)], 1)
    outs[13][...] = outs[7][...]


def end(streams, width, kv_width, blocks, counts, shards):
    terms = [v for s in streams for v in s.result]
    sizes = [len(s.result) for s in streams]
    rows = terms[0].shape[0]
    ff = blocks * width
    shapes = [(rows, width), (rows, kv_width), (rows, width), (rows, ff), (blocks * rows, width)]
    shapes += [(1, rows), (1, kv_width // shards)] + [(1, rows)] * 5 + [(1, blocks * rows), (1, rows)]
    return pl.pallas_call(
        functools.partial(
            end_kernel, sizes=sizes, width=width, kv_width=kv_width, blocks=blocks, counts=counts, shards=shards
        ),
        out_shape=[jax.ShapeDtypeStruct(s, f32) for s in shapes],
        compiler_params=params(),
        cost_estimate=cost(3),
        name="end",
    )(*terms)


def bits_of(axis, size):
    return [(axis, b) for b in range(size.bit_length() - 1)]


def swap(v, axis, bit):
    size = lax.axis_size(axis)
    return lax.ppermute(v, axis, [(i, i ^ (1 << bit)) for i in range(size)])


def total(terms):
    return sum(t.astype(f32) for t in terms).astype(bf16)


def tie(*values):
    return lax.optimization_barrier(values)


class Scatter:
    def __init__(self, halves, parts, tail, index_order):
        self.index_order = index_order
        dims = [1 if b == ("dp", 0) else 2 for b in index_order]
        self.pending = []
        for send, keep in halves:
            rows = send.shape[0] >> (len(index_order) - 1)
            self.pending.append((send, [keep.reshape(*dims, rows, send.shape[1])]))
        self.cols = sum(send.shape[1] for send, _ in halves)
        self.steps = [[("dp", 0)] * len(halves)] + [list(s) for s in zip(*parts)] + [[b] for b in tail]
        self.flying = None
        self.result = None

    def ready(self):
        return [send for send, _ in self.pending]

    def set_ready(self, values):
        self.pending = [(send, keep) for send, (_, keep) in zip(values, self.pending)]

    def start(self):
        bits = self.steps.pop(0)
        self.flying = [(swap(send, *bit), keep) for (send, keep), bit in zip(self.pending, bits)]

    def arrived(self):
        return [got for got, _ in self.flying]

    def finish(self, arrived):
        parts = [keep + [got.reshape(keep[0].shape)] for got, (_, keep) in zip(arrived, self.flying)]
        if not self.steps:
            (terms,) = parts
            self.result = [t.reshape(-1, self.cols) for t in terms]
            return
        bits = self.steps[0]
        if len(parts) > len(bits):
            parts = [[jnp.concatenate([total(terms) for terms in parts], -1)]]
        if len(parts) < len(bits):
            (terms,) = parts
            step = self.cols // LANES // len(bits) * LANES
            edges = [k * step for k in range(len(bits))] + [self.cols]
            parts = [[t[..., lo:hi] for t in terms] for lo, hi in zip(edges, edges[1:])]
        self.pending = []
        for terms, (axis, bit) in zip(parts, bits):
            here, where = (lax.axis_index(axis) >> bit) & 1, self.index_order.index((axis, bit))
            send = total([lax.dynamic_slice_in_dim(t, 1 - here, 1, where) for t in terms])
            keep = [lax.dynamic_slice_in_dim(t, here, 1, where) for t in terms]
            if len(keep) > 2:
                keep = [total(keep)]
            self.pending.append((send.reshape(-1, send.shape[-1]), keep))


class Gather:
    def __init__(self, local, head, orders, index_order):
        self.index_order = index_order
        self.pending = [local.reshape((1,) * len(index_order) + local.shape)]
        self.steps = [[b] for b in head] + [list(s) for s in zip(*orders)] + [[("dp", 0)] * len(orders)]
        self.flying = None
        self.result = None

    def ready(self):
        return self.pending

    def set_ready(self, values):
        self.pending = values

    def start(self):
        bits = self.steps.pop(0)
        if len(bits) > len(self.pending):
            (cur,) = self.pending
            step = cur.shape[-1] // len(bits)
            self.pending = [cur[..., k * step : (k + 1) * step] for k in range(len(bits))]
        self.flying = [(swap(cur.reshape(-1, cur.shape[-1]), *bit), cur, bit) for cur, bit in zip(self.pending, bits)]

    def arrived(self):
        return [got for got, _, _ in self.flying]

    def finish(self, arrived):
        if not self.steps:
            self.result = [(cur.reshape(got.shape), got) for got, (_, cur, _) in zip(arrived, self.flying)]
            return
        self.pending = []
        for got, (_, cur, (axis, bit)) in zip(arrived, self.flying):
            got = got.reshape(cur.shape)
            here = (lax.axis_index(axis) >> bit) & 1
            low = jnp.where(here == 0, cur, got)
            high = jnp.where(here == 0, got, cur)
            self.pending.append(jnp.concatenate([low, high], self.index_order.index((axis, bit))))


def launch(streams, *values):
    streams = [s for s in streams if s.result is None]
    ready, values = tie([s.ready() for s in streams], values)
    for stream, sends in zip(streams, ready):
        stream.set_ready(sends)
        stream.start()
    return values


def land(streams, *values):
    streams = [s for s in streams if s.result is None]
    if any(isinstance(s, Gather) for s in streams):
        arrived, values = tie([s.arrived() for s in streams], values)
    else:
        arrived = [tie(s.arrived(), values)[0] for s in streams]
    for stream, got in zip(streams, arrived):
        stream.finish(got)
    return values


def beside(streams, work, *inputs):
    out = work(*launch(streams, *inputs))
    return land(streams, *out) if isinstance(out, (tuple, list)) else land(streams, out)[0]


def body(
    tokens,
    lengths,
    cotangent,
    query_weight,
    query_bias,
    keyval_weight,
    keyval_bias,
    out_weight,
    out_bias,
    norm_attn_gain,
    norm_attn_bias,
    norm_mlp_gain,
    norm_mlp_bias,
    up_weight,
    up_bias,
    down_weight,
    down_bias,
):
    n_dp, n_fsdp = lax.axis_size("dp"), lax.axis_size("fsdp")
    shards = n_dp * n_fsdp
    rows, width = query_weight.shape
    kv_width = keyval_weight.shape[1]
    ff = up_weight.shape[1]
    blocks = ff // width
    seq_len = tokens.shape[1]
    x = tokens.reshape(seq_len, width)
    cot = cotangent.reshape(seq_len, width)

    half = rows * n_fsdp
    info = jnp.concatenate([lengths, (lax.axis_index("dp") & 1)[None].astype(jnp.int32)])
    dp_bits, fs_bits = bits_of("dp", n_dp), bits_of("fsdp", n_fsdp)
    index_order = dp_bits[::-1] + fs_bits[::-1]
    x_bits, y_bits, z_bits = fs_bits[:1], dp_bits[1:], fs_bits[1:]
    xy = [x_bits + y_bits, y_bits + x_bits]

    up_bias_cols = up_bias.reshape(blocks, rows)
    key_bias_col = jnp.pad(keyval_bias, (0, rows - keyval_bias.shape[0]))
    vecs = [query_bias, out_bias, norm_attn_gain, norm_attn_bias, norm_mlp_gain, norm_mlp_bias, down_bias]
    vecs = jnp.concatenate([jnp.stack(vecs), up_bias_cols, key_bias_col[None]], 0)
    vecs = jnp.pad(vecs, ((0, LANES - vecs.shape[0]), (0, 0))).T
    first = Gather(jnp.concatenate([query_weight, keyval_weight, out_weight, vecs], 1), z_bits[::-1], xy, index_order)
    up_weight, down_weight = land([first], *launch([first], up_weight, down_weight))
    up_weight, down_weight = launch([first], up_weight, down_weight)
    up_local = up_weight.reshape(rows, shards, blocks, rows).transpose(0, 2, 1, 3).reshape(rows, ff)
    dn_local = down_weight.reshape(blocks, rows, width).transpose(1, 0, 2).reshape(rows, ff)
    up_local, dn_local = land([first], up_local, dn_local)
    for _ in z_bits[2:]:
        up_local, dn_local = land([first], *launch([first], up_local, dn_local))
    ups = Gather(up_local, z_bits[::-1], [x_bits + y_bits], index_order)
    dns = Gather(dn_local, z_bits[::-1], [y_bits + x_bits], index_order)
    (x,) = land([first, ups], *launch([first, ups], x))
    (x,) = land([first, dns], *launch([first, dns], x))
    while first.result is None:
        (x,) = land([first], *launch([first], x))

    tables = rotary_tables(seq_len, kv_width // 2)
    one, two = first.result
    q, kv, ha, hm, gy, gm, vec, w_q, w_o = beside(
        [ups, dns], lambda x: pre(info, x, cot, one, two, tables, kv_width, shards, half), x
    )
    pairs = width // LANES
    second = [ups, dns]
    state = beside(second, lambda q: attention(info, q, gm, kv, tables, None, 0, 2), q)
    (state,) = launch(second, state)
    for start in range(2, pairs, 2):
        state = attention(info, q, gm, kv, tables, state, start, 2)
    dkv, mixed, dq = land(second, *state)
    send, keep = beside(second, lambda mixed: attention_grads(info, ha, gy, mixed, dq, dkv, w_q, w_o, shards, half), mixed)
    while any(s.result is None for s in second):
        send, keep = beside(second, lambda *v: v, send, keep)
    (up_rows,), (dn_rows,) = ups.result, dns.result

    attn = Scatter([(send, keep)], [x_bits + z_bits[:1] + y_bits], z_bits[1:], index_order)
    ff_part = lambda chunk, count: lambda hm, gy, *state: feed_forward(
        info, hm, gy, up_rows, dn_rows, vec, w_o, state[0] if state else None, chunk, count, half
    )
    n0 = blocks // 2
    hm, gy = beside([attn], lambda *v: v, hm, gy)
    act0, gup0, state, send, keep = beside([attn], ff_part(0, n0), hm, gy)
    ff0 = Scatter([(send, keep)], xy, z_bits, index_order)
    hm, gy, state = launch([attn], hm, gy, state)
    hm, gy, state = beside([ff0], lambda *v: v, hm, gy, state)
    act1, gup1, _, send, keep = beside([ff0], ff_part(n0, blocks - n0), hm, gy, state)
    send, keep = land([attn], send, keep)
    ff1 = Scatter([(send, keep)], xy, z_bits, index_order)
    layer_out = beside(
        [ff0, ff1, attn],
        lambda x, *acts: layer_output(info, x, mixed, w_o, dn_rows, vec, acts, half),
        *(x, act0, act1),
    )
    gtok = beside(
        [ff1, ff0, attn],
        lambda cot, *gups: token_grads(info, x, cot, dq, dkv, w_q, up_rows, vec, gups, half),
        *(cot, gup0, gup1),
    )
    streams = [attn, ff0, ff1]
    while any(s.result is None for s in streams):
        beside(streams, lambda *v: v)
    gq, gkv, go, gu, gd, *lines = end(streams, width, kv_width, blocks, (n0, blocks - n0), shards)
    if shards * blocks > 128:
        gu = gu.reshape(rows, blocks, shards, rows).transpose(0, 2, 1, 3).reshape(rows, ff)
    bq, bkv, bo, ga, ba, g_gain, g_shift, b_up, b_dn = (v.reshape(-1) for v in lines)
    return (
        layer_out.reshape(tokens.shape),
        gtok.reshape(tokens.shape),
        gq,
        bq,
        gkv,
        bkv,
        go,
        bo,
        ga,
        ba,
        g_gain,
        g_shift,
        gu,
        b_up,
        gd,
        b_dn,
    )


def solution(mesh):
    mat, vec, seq = P(BOTH, None), P(BOTH), P(BOTH, None, None)
    return jax.shard_map(
        body,
        mesh=mesh,
        in_specs=(seq, vec, seq, mat, vec, mat, vec, mat, vec, vec, vec, vec, vec, mat, vec, mat, vec),
        out_specs=(seq, seq, mat, vec, mat, vec, mat, vec, vec, vec, vec, vec, mat, vec, mat, vec),
        check_vma=False,
    )
```

```python
import functools

import jax
import jax.numpy as jnp
import numpy as np
from jax import lax
from jax.experimental import pallas as pl
from jax.experimental.pallas import tpu as pltpu
from jax.sharding import PartitionSpec as P

f32 = jnp.float32
bf16 = jnp.bfloat16

ROT = 16
EPS = 1e-05
NEG = -1e30
ROOT_HALF = 0.7071067811865476
INV_ROOT_TAU = 0.3989422804014327
LANES = 128
BOTH = ("dp", "fsdp")
VMEM = 28 * 1024 * 1024

SHIFT, INNER = 8, 9
QB, OB, GA, BA, GM, BM, DB, UB, KB = 0, 1, 2, 3, 4, 5, 6, 7, 11


def dot(a, b, ca, cb):
    return lax.dot_general(a, b, (((ca,), (cb,)), ((), ())), preferred_element_type=f32)


def params(**kw):
    return pltpu.CompilerParams(vmem_limit_bytes=VMEM, **kw)


def cost(us):
    return pl.CostEstimate(flops=int(us * 1.0e9), bytes_accessed=int(us * 3.0e6), transcendentals=0)


def in_hbm(*arrays):
    return [pltpu.with_memory_space_constraint(a, pltpu.HBM) for a in arrays]


def last_lanes(w):
    at = w.shape[1] // LANES - 1
    return pl.BlockSpec((w.shape[0], LANES), lambda *_: (0, at), pipeline_mode=pl.Buffered(1))


def whole(shape):
    return pl.BlockSpec(shape, lambda *_: (0,) * len(shape))


def rotary_tables(seq_len, head_dim):
    half = ROT // 2
    inverse_freq = np.float32(10000.0) ** (-(np.float32(2.0) * np.arange(half, dtype=np.float32)) / np.float32(ROT))
    angles = np.arange(seq_len, dtype=np.float32)[:, None] * inverse_freq[None, :]
    cos, sin = np.cos(angles.astype(np.float64)), np.sin(angles.astype(np.float64))
    tables = np.zeros((3, seq_len, LANES), np.float32)
    tables[0] = 1.0
    for at in range(0, LANES, head_dim):
        tables[0, :, at : at + half] = cos
        tables[0, :, at + half : at + ROT] = cos
        tables[1, :, at : at + half] = sin
        tables[2, :, at + half : at + ROT] = sin
    return jnp.asarray(tables)


def partners(v):
    half = ROT // 2
    return pltpu.roll(v, LANES - half, 1), pltpu.roll(v, half, 1)


def rotate(v, own, up, down):
    ahead, behind = partners(v)
    return v * own - ahead * up + behind * down


def rotate_back(v, own, up, down):
    ahead, behind = partners(v)
    return v * own + ahead * up - behind * down


def standardise(rows):
    average = jnp.mean(rows, axis=-1, keepdims=True)
    centred = rows - average
    scaled = lax.rsqrt(jnp.mean(centred * centred, axis=-1, keepdims=True) + EPS)
    return centred * scaled, scaled


def norm_back(grad, normed, scaled, gain):
    e = grad * gain
    return scaled * (
        e - jnp.mean(e, axis=-1, keepdims=True) - normed * jnp.mean(e * normed, axis=-1, keepdims=True)
    )


def col_sum(v):
    return jnp.sum(v, axis=0, keepdims=True)


def kept_rows(block, rows, length):
    pos = lax.broadcasted_iota(jnp.int32, (rows, 1), 0) + block * rows
    return (pos < length).astype(f32)


def spread_key_bias(width, kv_width, per_row, per_kv):
    row = lax.broadcasted_iota(jnp.int32, (width, kv_width), 0)
    col = lax.broadcasted_iota(jnp.int32, (width, kv_width), 1)
    owner = col // per_kv
    return (row == owner * per_row + (col - owner * per_kv)).astype(bf16)


def assemble(to, at, mine, other, core, half):
    for g in range(to.shape[0] // (2 * half)):
        rows, base = slice(g * half, (g + 1) * half), g * 2 * half
        to[pl.ds(pl.multiple_of(base + core * half, half), half), at] = mine[rows, :]
        to[pl.ds(pl.multiple_of(base + (1 - core) * half, half), half), at] = other[rows, :]


def pre_kernel(info, x_ref, cot_ref, a0, a1, b0, b1, tab_ref, q_ref, kv_ref, ha_ref, hm_ref, gy_ref, gm_ref, vec_ref, wq_ref, wo_ref, vec_s, *, dims, half):
    width, kv_width, rows, per_row, per_kv = dims
    i = pl.program_id(0)
    @pl.when(i == 0)
    def _():
        assemble(wq_ref, slice(None), a0, a1, info[1], half)
        assemble(wo_ref, slice(None), b0, b1, info[1], half)
        low = wo_ref[:, width:]
        lines = low.astype(f32).T[:16]
        vec_s[:16, :] = lines
        spread = spread_key_bias(width, kv_width, per_row, per_kv)
        vec_s[16:32, :kv_width] = dot(lines.astype(bf16), spread, 1, 0)
        vec_ref[...] = vec_s[...]

    normed, _ = standardise(x_ref[...].astype(f32))
    vec = vec_s[...]
    ha = (normed * vec[GA : GA + 1] + vec[BA : BA + 1]).astype(bf16)
    hm = (normed * vec[GM : GM + 1] + vec[BM : BM + 1]).astype(bf16)
    ha_ref[...] = ha
    hm_ref[...] = hm
    own, up, down = tab_ref[0], tab_ref[1], tab_ref[2]
    scale = (kv_width // 2) ** -0.5
    lin = dot(ha, wq_ref[...], 1, 0)
    query = lin[:, :width] + vec[QB : QB + 1]
    for p in range(width // LANES):
        cols = slice(p * LANES, (p + 1) * LANES)
        rot = rotate(query[:, cols], own, up, down).astype(bf16)
        q_ref[:, cols] = (rot.astype(f32) * scale).astype(bf16)
    lin = lin[:, width:] + vec[16 + KB : 17 + KB, :kv_width]
    lane = lax.broadcasted_iota(jnp.int32, (rows, kv_width), 1)
    kv_ref[...] = jnp.where(lane < kv_width // 2, rotate(lin, own, up, down), lin).astype(bf16)
    keep = kept_rows(i, rows, info[0])
    gy = (cot_ref[...].astype(f32) * keep).astype(bf16)
    gy_ref[...] = gy
    gm_ref[...] = dot(gy, wo_ref[:, :width], 1, 1).astype(bf16)


def pre(info, x, cot, a, b, tables, kv_width, shards, half):
    tokens, width = x.shape
    rows = 256
    blk = pl.BlockSpec((rows, width), lambda i, *_: (i, 0))
    kvb = pl.BlockSpec((rows, kv_width), lambda i, *_: (i, 0))
    dims = (width, kv_width, rows, width // shards, kv_width // shards)
    wide = jax.ShapeDtypeStruct((tokens, width), bf16)
    one = lambda v: pl.BlockSpec(v.shape, lambda *_: (0, 0), pipeline_mode=pl.Buffered(1))
    w_q, w_o = (width, width + kv_width), (width, width + LANES)
    return pl.pallas_call(
        functools.partial(pre_kernel, dims=dims, half=half),
        grid_spec=pltpu.PrefetchScalarGridSpec(
            num_scalar_prefetch=1,
            grid=(tokens // rows,),
            in_specs=[blk, blk, one(a[0]), one(a[1]), one(b[0]), one(b[1])]
            + [pl.BlockSpec((3, rows, LANES), lambda i, *_: (0, i, 0))],
            out_specs=[blk, kvb, blk, blk, blk, blk, whole((32, width)), whole(w_q), whole(w_o)],
            scratch_shapes=[pltpu.VMEM((32, width), f32)],
        ),
        out_shape=[
            wide,
            jax.ShapeDtypeStruct((tokens, kv_width), bf16),
            pltpu.HBM((tokens, width), bf16),
            pltpu.HBM((tokens, width), bf16),
            wide,
            wide,
            jax.ShapeDtypeStruct((32, width), f32),
            jax.ShapeDtypeStruct(w_q, bf16),
            jax.ShapeDtypeStruct(w_o, bf16),
        ],
        compiler_params=params(),
        cost_estimate=cost(9),
        name="pre",
    )(info, x, cot, *a, *b, tables)


def attn_kernel(len_ref, q_ref, gm_ref, kv_ref, tab_ref, *refs, qb, first, final):
    if not first:
        acc_in, refs = refs[0], refs[3:]
    mix_ref, dq_ref, dkv_ref, k0, k1, v0, v1, acc = refs
    p = pl.program_id(0)
    tokens, kv_width = kv_ref.shape
    head = kv_width // 2

    @pl.when(p == 0)
    def _():
        kv = kv_ref[...]
        zero = jnp.zeros((tokens, head), bf16)
        k, v = kv[:, :head], kv[:, head:]
        k0[...] = jnp.concatenate([k, zero], 1)
        k1[...] = jnp.concatenate([zero, k], 1)
        v0[...] = jnp.concatenate([v, zero], 1)
        v1[...] = jnp.concatenate([zero, v], 1)
        acc[...] = jnp.zeros_like(acc) if first else acc_in[...]

    last = len_ref[0] - 1
    scale = head**-0.5
    pads = ((k0, v0), (k1, v1))
    units = [(i, h) for i in range(tokens // qb) for h in range(LANES // head)]
    scored, weighed, mixes, dqs = {}, {}, {}, {}

    def score(unit):
        i, h = unit
        r, kn = pl.ds(i * qb, qb), (i + 1) * qb
        k, v = pads[h]
        scored[unit] = (dot(q_ref[r, :], k[:kn, :], 1, 1), dot(gm_ref[r, :], v[:kn, :], 1, 1))

    def weigh(unit):
        i, h = unit
        r, kn = pl.ds(i * qb, qb), (i + 1) * qb
        s, dp = scored.pop(unit)
        col = lax.broadcasted_iota(jnp.int32, (qb, kn), 1)
        limit = jnp.minimum(lax.broadcasted_iota(jnp.int32, (qb, 1), 0) + i * qb, last)
        s = jnp.where(col <= limit, s, NEG)
        e = jnp.exp(s - jnp.max(s, axis=1, keepdims=True))
        pr = e * (1.0 / jnp.sum(e, axis=1, keepdims=True))
        low = pr.astype(bf16)
        mixed = dot(low, pads[h][1][:kn, :], 1, 0)
        acc[head:, :kn] += dot(gm_ref[r, head * h : head * (h + 1)].T, low, 1, 0)
        weighed[unit] = (pr, dp, mixed)

    def back(unit):
        i, h = unit
        r, kn = pl.ds(i * qb, qb), (i + 1) * qb
        pr, dp, mixed = weighed.pop(unit)
        row = jnp.sum(gm_ref[r, :].astype(f32) * mixed, axis=1, keepdims=True)
        ds = (pr * (dp - row)).astype(bf16)
        dq = dot(ds, pads[h][0][:kn, :], 1, 0)
        acc[:head, :kn] += dot(q_ref[r, head * h : head * (h + 1)].T, ds, 1, 0)
        if h == 0:
            mixes[i], dqs[i] = mixed, dq
        else:
            mix_ref[r, :] = (mixes.pop(i) + mixed).astype(bf16)
            dq = (dqs.pop(i) + dq) * scale
            dq_ref[r, :] = rotate_back(dq, tab_ref[0, r, :], tab_ref[1, r, :], tab_ref[2, r, :]).astype(bf16)

    for t in range(len(units) + 3):
        for stage, lag in ((score, 0), (weigh, 1), (back, 3)):
            if 0 <= t - lag < len(units):
                stage(units[t - lag])

    @pl.when(p == pl.num_programs(0) - 1)
    def _():
        if not final:
            dkv_ref[...] = acc[...]
            return
        dkv = acc[...].T
        lanes = lax.broadcasted_iota(jnp.int32, (tokens, kv_width), 1)
        back = rotate_back(dkv, tab_ref[0], tab_ref[1], tab_ref[2])
        dkv_ref[...] = jnp.where(lanes < head, back, dkv).astype(bf16)


def attention(info, q, gm, kv, tables, state, start, count):
    tokens, width = q.shape
    kv_width = kv.shape[1]
    first, final = state is None, start + count == width // LANES
    blk = pl.BlockSpec((tokens, LANES), lambda p, *_: (0, p + start))
    wide = jax.ShapeDtypeStruct((tokens, width), bf16)
    sums = (kv_width, tokens)
    args, specs, alias = [q, gm, kv, tables], [blk, blk, whole((tokens, kv_width)), whole((3, tokens, LANES))], {}
    if not first:
        args += list(state)
        specs += [whole(sums), pl.BlockSpec(memory_space=pl.ANY), pl.BlockSpec(memory_space=pl.ANY)]
        alias = {6: 0, 7: 1}
    dkv = ((tokens, kv_width), bf16) if final else (sums, f32)
    mixed, dq, dkv = pl.pallas_call(
        functools.partial(attn_kernel, qb=256, first=first, final=final),
        grid_spec=pltpu.PrefetchScalarGridSpec(
            num_scalar_prefetch=1,
            grid=(count,),
            in_specs=specs,
            out_specs=[blk, blk, whole(dkv[0])],
            scratch_shapes=[pltpu.VMEM((tokens, LANES), bf16)] * 4 + [pltpu.VMEM(sums, f32)],
        ),
        out_shape=[wide, wide, jax.ShapeDtypeStruct(*dkv)],
        input_output_aliases=alias,
        compiler_params=params(),
        cost_estimate=cost(8 * count),
        name="attention",
    )(info, *args)
    return dkv, mixed, dq


def split_halves(send_ref, keep_ref, low_s, cols, at, core, half):
    for g in range(low_s.shape[0] // (2 * half)):
        to, base = pl.ds(g * half, half), g * 2 * half
        send_ref[to, at] = low_s[pl.ds(pl.multiple_of(base + (1 - core) * half, half), half), :cols]
        keep_ref[to, at] = low_s[pl.ds(pl.multiple_of(base + core * half, half), half), :cols]


def row_sum(v):
    return jnp.sum(v, axis=1, keepdims=True)


def grads_kernel(info, ha_ref, gy_ref, mix_ref, dq_ref, dkv_ref, w_ref, vec_ref, send_ref, keep_ref, sums, cols, low_s, *, dims, half):
    width, kv_width, step, per_row, per_kv = dims
    j = pl.program_id(0)
    c_out = width + kv_width
    c_vec = c_out + width
    core = info[1]

    @pl.when(j == 0)
    def _():
        cols[...] = jnp.zeros_like(cols)
        sums[...] = jnp.zeros_like(sums)

    def put(value, at, size):
        low_s[:, :size] = value.astype(bf16)
        split_halves(send_ref, keep_ref, low_s, size, pl.ds(at, size), core, half)

    def weight_sums(w, grad, lines):
        w = w.astype(f32)
        cols[:, SHIFT : SHIFT + 1] += row_sum(w * lines)
        cols[:, INNER : INNER + 1] += row_sum(w * grad)

    at = pl.multiple_of(j * step, LANES)
    grad = dot(ha_ref[...], dq_ref[...], 0, 0)
    lines = col_sum(dq_ref[...].astype(f32))
    sums[QB : QB + 1, pl.ds(at, step)] = lines
    sums[OB : OB + 1, pl.ds(at, step)] = col_sum(gy_ref[...].astype(f32))
    weight_sums(w_ref[:, pl.ds(at, step)], grad, lines)
    put(grad, at, step)
    put(dot(mix_ref[...], gy_ref[...], 0, 0), pl.multiple_of(c_out + at, LANES), step)

    @pl.when(j == pl.num_programs(0) - 1)
    def _():
        grad = dot(ha_ref[...], dkv_ref[...], 0, 0)
        lines = col_sum(dkv_ref[...].astype(f32))
        weight_sums(w_ref[:, width:c_out], grad, lines)
        put(grad, width, kv_width)
        vec = vec_ref[...].astype(f32)
        shift = cols[:, SHIFT : SHIFT + 1]
        gain = (cols[:, INNER : INNER + 1] - vec[:, BA : BA + 1] * shift) / vec[:, GA : GA + 1]
        spread = spread_key_bias(width, kv_width, per_row, per_kv)
        key = dot(jnp.broadcast_to(lines, (16, kv_width)).astype(bf16), spread, 1, 1)
        row = lax.broadcasted_iota(jnp.int32, (16, width), 0)
        both = jnp.where(row == 8, key, sums[...])
        both = jnp.concatenate([both, jnp.zeros((LANES - 16, width), f32)], 0).T
        lane = lax.broadcasted_iota(jnp.int32, (width, LANES), 1)
        put(jnp.where(lane == GA, gain, jnp.where(lane == BA, shift, both)), c_vec, LANES)


def attention_grads(info, ha, gy, mixed, dq, dkv, w_q, w_o, shards, half):
    tokens, width = ha.shape
    kv_width = dkv.shape[1]
    step = 2 * LANES
    one = lambda s: pl.BlockSpec(s, lambda *_: (0, 0), pipeline_mode=pl.Buffered(1))
    col = pl.BlockSpec((tokens, step), lambda j, *_: (0, j))
    dims = (width, kv_width, step, width // shards, kv_width // shards)
    cut = (width // 2, w_q.shape[1] + w_o.shape[1])
    return pl.pallas_call(
        functools.partial(grads_kernel, dims=dims, half=half),
        grid_spec=pltpu.PrefetchScalarGridSpec(
            num_scalar_prefetch=1,
            grid=(width // step,),
            in_specs=[one(ha.shape), col, one(mixed.shape), col, one(dkv.shape), one(w_q.shape), last_lanes(w_o)],
            out_specs=[one(cut), one(cut)],
            scratch_shapes=[
                pltpu.VMEM((16, width), f32),
                pltpu.VMEM((width, LANES), f32),
                pltpu.VMEM((width, step), bf16),
            ],
        ),
        out_shape=[jax.ShapeDtypeStruct(cut, bf16)] * 2,
        compiler_params=params(),
        cost_estimate=cost(8),
        name="attention_grads",
    )(info, ha, gy, mixed, dq, dkv, w_q, w_o)


def ff_kernel(*refs, rows, chunk, first, final, half):
    refs = list(refs)
    take = lambda k: [refs.pop(0) for _ in range(k)]
    info, hm_ref, gy_ref, u0, u1, d0, d1, vec_ref = take(8)
    (col_in,) = (None,) if first else take(1)
    (vcol_ref,) = take(1) if final else (None,)
    act_ref, gup_ref = take(2)
    (col_out,) = (None,) if final else take(1)
    send_ref, keep_ref, cols, low_s, wu_ref, wd_ref = refs
    j = pl.program_id(0)
    assemble(wu_ref, slice(None), u0, u1, info[1], half)
    assemble(wd_ref, slice(None), d0, d1, info[1], half)
    tokens, width = hm_ref.shape

    @pl.when(j == 0)
    def _():
        cols[...] = jnp.zeros_like(cols) if first else col_in[...]

    bias = vec_ref[pl.ds(UB + chunk + j, 1), :]
    total = jnp.zeros((1, width), f32)
    for i in range(tokens // rows):
        r = pl.ds(i * rows, rows)
        u = dot(hm_ref[r, :], wu_ref[...], 1, 0) + bias
        cdf = 0.5 * (1.0 + lax.erf(u * ROOT_HALF))
        pdf = jnp.exp(-0.5 * u * u) * INV_ROOT_TAU
        act_ref[r, :] = (u * cdf).astype(bf16)
        grad = (dot(gy_ref[r, :], wd_ref[...], 1, 1) * (cdf + u * pdf)).astype(bf16)
        gup_ref[r, :] = grad
        total = total + col_sum(grad.astype(f32))
    at = pl.multiple_of(j * 2 * width, LANES)
    d_up = dot(hm_ref[...], gup_ref[...], 0, 0)
    low_s[...] = d_up.astype(bf16)
    w_up = wu_ref[...].astype(f32)
    lane = lax.broadcasted_iota(jnp.int32, (width, LANES), 1)
    mine = jnp.where(lane == chunk + j, jnp.broadcast_to(total, (LANES, width)).T, 0.0)
    mine = jnp.where(lane == SHIFT, row_sum(w_up * total), mine)
    cols[...] += jnp.where(lane == INNER, row_sum(w_up * d_up), mine)
    split_halves(send_ref, keep_ref, low_s, width, pl.ds(at, width), info[1], half)
    low_s[...] = dot(act_ref[...], gy_ref[...], 0, 0).astype(bf16)
    at = pl.multiple_of(at + width, LANES)
    split_halves(send_ref, keep_ref, low_s, width, pl.ds(at, width), info[1], half)

    @pl.when(j == pl.num_programs(0) - 1)
    def _():
        if not final:
            col_out[...] = cols[...]
            return
        vec = vcol_ref[...].astype(f32)
        now = cols[...]
        gain = (now[:, INNER : INNER + 1] - vec[:, BM : BM + 1] * now[:, SHIFT : SHIFT + 1]) / vec[:, GM : GM + 1]
        low_s[:, :LANES] = jnp.where(lane == INNER, gain, now).astype(bf16)
        at = pl.ds(send_ref.shape[1] - LANES, LANES)
        split_halves(send_ref, keep_ref, low_s, LANES, at, info[1], half)


def feed_forward(info, hm, gy, up_rows, dn_rows, vec, w_o, state, chunk, count, half):
    tokens, width = hm.shape
    blocks = up_rows[0].shape[1] // width
    tok = (tokens, width)
    first, final = state is None, chunk + count == blocks
    one = lambda s: pl.BlockSpec(s, lambda *_: (0, 0), pipeline_mode=pl.Buffered(1))
    col = pl.BlockSpec(tok, lambda j, *_: (0, j))
    wgt = pl.BlockSpec((width // 2, width), lambda j, *_: (0, j + chunk))
    args = [*in_hbm(hm), gy, *in_hbm(*up_rows, *dn_rows), vec]
    specs = [one(tok), one(tok), wgt, wgt, wgt, wgt, one(vec.shape)]
    if not first:
        args += [state]
        specs += [one((width, LANES))]
    if final:
        args += [w_o]
        specs += [last_lanes(w_o)]
    long = pltpu.HBM((tokens, count * width), bf16)
    shapes, outs = [long, long], [col, col]
    if not final:
        shapes += [jax.ShapeDtypeStruct((width, LANES), f32)]
        outs += [one((width, LANES))]
    cut = (width // 2, count * 2 * width + (LANES if final else 0))
    shapes += [jax.ShapeDtypeStruct(cut, bf16)] * 2
    outs += [one(cut)] * 2
    got = pl.pallas_call(
        functools.partial(ff_kernel, rows=256, chunk=chunk, first=first, final=final, half=half),
        grid_spec=pltpu.PrefetchScalarGridSpec(
            num_scalar_prefetch=1,
            grid=(count,),
            in_specs=specs,
            out_specs=outs,
            scratch_shapes=[pltpu.VMEM((width, LANES), f32)] + [pltpu.VMEM((width, width), bf16)] * 3,
        ),
        out_shape=shapes,
        compiler_params=params(),
        cost_estimate=cost(7 * count),
        name="feed_forward",
    )(info, *args)
    act, gup = got[:2]
    return act, gup, None if final else got[2], got[-2], got[-1]


def out_kernel(*refs, pieces, rows, half):
    info, x_ref, mix_ref, wo_ref, d0, d1, vec_ref = refs[:7]
    acts, out_ref, wd_ref = refs[7:-2], refs[-2], refs[-1]

    @pl.when(pl.program_id(0) == 0)
    def _():
        assemble(wd_ref, slice(None), d0, d1, info[1], half)

    width = x_ref.shape[1]
    total = dot(mix_ref[...], wo_ref[...], 1, 0) + vec_ref[OB : OB + 1] + vec_ref[DB : DB + 1]
    at = 0
    for act_ref, count in zip(acts, pieces):
        for k in range(count):
            act = act_ref[:, k * width : (k + 1) * width]
            total = total + dot(act, wd_ref[:, at : at + width], 1, 0)
            at += width
    keep = kept_rows(pl.program_id(0), rows, info[0])
    out_ref[...] = (x_ref[...].astype(f32) + keep * total).astype(bf16)


def layer_output(info, x, mixed, w_o, dn_rows, vec, acts, half):
    tokens, width = x.shape
    rows = 256
    long = dn_rows[0].shape[1]
    blk = lambda n: pl.BlockSpec((rows, n), lambda i, *_: (i, 0))
    one = lambda s, *at: pl.BlockSpec(s, lambda *_: at, pipeline_mode=pl.Buffered(1))
    return pl.pallas_call(
        functools.partial(out_kernel, pieces=[a.shape[1] // width for a in acts], rows=rows, half=half),
        grid_spec=pltpu.PrefetchScalarGridSpec(
            num_scalar_prefetch=1,
            grid=(tokens // rows,),
            in_specs=[blk(width), blk(width), one((width, width), 0, 0)]
            + [one((width // 2, long), 0, 0)] * 2
            + [one(vec.shape, 0, 0)]
            + [blk(a.shape[1]) for a in acts],
            out_specs=blk(width),
            scratch_shapes=[pltpu.VMEM((width, long), bf16)],
        ),
        out_shape=jax.ShapeDtypeStruct((tokens, width), bf16),
        compiler_params=params(),
        cost_estimate=cost(9),
        name="layer_output",
    )(info, x, mixed, w_o, *in_hbm(*dn_rows), vec, *in_hbm(*acts))


def token_kernel(*refs, pieces, kv_width, half):
    info, x_ref, cot_ref, dq_ref, dkv_ref, wq_ref, u0, u1, vec_ref = refs[:9]
    gups, out_ref, wu_ref = refs[9:-2], refs[-2], refs[-1]

    @pl.when(pl.program_id(0) == 0)
    def _():
        assemble(wu_ref, slice(None), u0, u1, info[1], half)

    width = x_ref.shape[1]
    normed, scaled = standardise(x_ref[...].astype(f32))
    grad = dot(dq_ref[...], wq_ref[:, :width], 1, 1) + dot(dkv_ref[...], wq_ref[:, width : width + kv_width], 1, 1)
    total = norm_back(grad, normed, scaled, vec_ref[GA : GA + 1])
    at, grad = 0, None
    for gup_ref, count in zip(gups, pieces):
        part = dot(gup_ref[...], wu_ref[:, at : at + count * width], 1, 1)
        grad = part if grad is None else grad + part
        at += count * width
    total = total + norm_back(grad, normed, scaled, vec_ref[GM : GM + 1])
    out_ref[...] = cot_ref[...].astype(f32) + total


def token_grads(info, x, cot, dq, dkv, w_q, up_rows, vec, gups, half):
    tokens, width = x.shape
    rows = 256
    long = up_rows[0].shape[1]
    blk = lambda n: pl.BlockSpec((rows, n), lambda i, *_: (i, 0))
    one = lambda s: pl.BlockSpec(s, lambda *_: (0, 0), pipeline_mode=pl.Buffered(1))
    pieces = [g.shape[1] // width for g in gups]
    return pl.pallas_call(
        functools.partial(token_kernel, pieces=pieces, kv_width=dkv.shape[1], half=half),
        grid_spec=pltpu.PrefetchScalarGridSpec(
            num_scalar_prefetch=1,
            grid=(tokens // rows,),
            in_specs=[blk(width), blk(width), blk(width), blk(dkv.shape[1]), one(w_q.shape)]
            + [one((width // 2, long))] * 2
            + [one(vec.shape)]
            + [blk(g.shape[1]) for g in gups],
            out_specs=blk(width),
            scratch_shapes=[pltpu.VMEM((width, long), bf16)],
        ),
        out_shape=jax.ShapeDtypeStruct((tokens, width), f32),
        compiler_params=params(),
        cost_estimate=cost(11),
        name="token_grads",
    )(info, x, cot, dq, dkv, w_q, *in_hbm(*up_rows), vec, *in_hbm(*gups))


def end_kernel(*refs, sizes, width, kv_width, blocks, counts, shards):
    terms, outs = list(refs[:-14]), refs[-14:]
    gq, gkv, go, gu, gd = outs[:5]
    sums = [sum(terms.pop(0)[...].astype(f32) for _ in range(size)) for size in sizes]
    rows = sums[0].shape[0]
    c_out = width + kv_width
    gq[...] = sums[0][:, :width]
    gkv[...] = sums[0][:, width:c_out]
    go[...] = sums[0][:, c_out : c_out + width]
    ups = []
    for part, count in zip(sums[1:], counts):
        for k in range(count):
            at = 2 * k * width
            gd[len(ups) * rows : (len(ups) + 1) * rows, :] = part[:, at + width : at + 2 * width]
            ups.append(part[:, at : at + width])
    if shards * blocks <= 128:
        pieces = [ups[q][:, i * rows : (i + 1) * rows] for i in range(shards) for q in range(blocks)]
        gu[...] = jnp.concatenate(pieces, 1)
    else:
        gu[...] = jnp.concatenate(ups, 1)
    square = lambda v: jnp.concatenate([v, jnp.zeros((LANES - rows, LANES), f32)], 0).T
    v1 = square(sums[0][:, c_out + width :])
    v2 = square(sums[-1][:, -LANES:])
    lines = [v1[QB], v1[8], v1[OB], v1[GA], v1[BA], v2[INNER], v2[SHIFT]]
    for ref, line in zip(outs[5:12], lines):
        ref[...] = line[None, : ref.shape[1]]
    outs[12][...] = jnp.concatenate([v2[q : q + 1, :rows] for q in range(blocks)], 1)
    outs[13][...] = outs[7][...]


def end(streams, width, kv_width, blocks, counts, shards):
    terms = [v for s in streams for v in s.result]
    sizes = [len(s.result) for s in streams]
    rows = terms[0].shape[0]
    ff = blocks * width
    shapes = [(rows, width), (rows, kv_width), (rows, width), (rows, ff), (blocks * rows, width)]
    shapes += [(1, rows), (1, kv_width // shards)] + [(1, rows)] * 5 + [(1, blocks * rows), (1, rows)]
    return pl.pallas_call(
        functools.partial(
            end_kernel, sizes=sizes, width=width, kv_width=kv_width, blocks=blocks, counts=counts, shards=shards
        ),
        out_shape=[jax.ShapeDtypeStruct(s, f32) for s in shapes],
        compiler_params=params(),
        cost_estimate=cost(3),
        name="end",
    )(*terms)


def bits_of(axis, size):
    return [(axis, b) for b in range(size.bit_length() - 1)]


def swap(v, axis, bit):
    size = lax.axis_size(axis)
    return lax.ppermute(v, axis, [(i, i ^ (1 << bit)) for i in range(size)])


def total(terms):
    return sum(t.astype(f32) for t in terms).astype(bf16)


def tie(*values):
    return lax.optimization_barrier(values)


class Scatter:
    def __init__(self, halves, parts, tail, index_order):
        self.index_order = index_order
        dims = [1 if b == ("dp", 0) else 2 for b in index_order]
        self.pending = []
        for send, keep in halves:
            rows = send.shape[0] >> (len(index_order) - 1)
            self.pending.append((send, [keep.reshape(*dims, rows, send.shape[1])]))
        self.cols = sum(send.shape[1] for send, _ in halves)
        self.steps = [[("dp", 0)] * len(halves)] + [list(s) for s in zip(*parts)] + [[b] for b in tail]
        self.flying = None
        self.result = None

    def ready(self):
        return [send for send, _ in self.pending]

    def set_ready(self, values):
        self.pending = [(send, keep) for send, (_, keep) in zip(values, self.pending)]

    def start(self):
        bits = self.steps.pop(0)
        self.flying = [(swap(send, *bit), keep) for (send, keep), bit in zip(self.pending, bits)]

    def arrived(self):
        return [got for got, _ in self.flying]

    def finish(self, arrived):
        parts = [keep + [got.reshape(keep[0].shape)] for got, (_, keep) in zip(arrived, self.flying)]
        if not self.steps:
            (terms,) = parts
            self.result = [t.reshape(-1, self.cols) for t in terms]
            return
        bits = self.steps[0]
        if len(parts) > len(bits):
            parts = [[jnp.concatenate([total(terms) for terms in parts], -1)]]
        if len(parts) < len(bits):
            (terms,) = parts
            step = self.cols // LANES // len(bits) * LANES
            edges = [k * step for k in range(len(bits))] + [self.cols]
            parts = [[t[..., lo:hi] for t in terms] for lo, hi in zip(edges, edges[1:])]
        self.pending = []
        for terms, (axis, bit) in zip(parts, bits):
            here, where = (lax.axis_index(axis) >> bit) & 1, self.index_order.index((axis, bit))
            send = total([lax.dynamic_slice_in_dim(t, 1 - here, 1, where) for t in terms])
            keep = [lax.dynamic_slice_in_dim(t, here, 1, where) for t in terms]
            if len(keep) > 2:
                keep = [total(keep)]
            self.pending.append((send.reshape(-1, send.shape[-1]), keep))


class Gather:
    def __init__(self, local, head, orders, index_order):
        self.index_order = index_order
        self.pending = [local.reshape((1,) * len(index_order) + local.shape)]
        self.steps = [[b] for b in head] + [list(s) for s in zip(*orders)] + [[("dp", 0)] * len(orders)]
        self.flying = None
        self.result = None

    def ready(self):
        return self.pending

    def set_ready(self, values):
        self.pending = values

    def start(self):
        bits = self.steps.pop(0)
        if len(bits) > len(self.pending):
            (cur,) = self.pending
            step = cur.shape[-1] // len(bits)
            self.pending = [cur[..., k * step : (k + 1) * step] for k in range(len(bits))]
        self.flying = [(swap(cur.reshape(-1, cur.shape[-1]), *bit), cur, bit) for cur, bit in zip(self.pending, bits)]

    def arrived(self):
        return [got for got, _, _ in self.flying]

    def finish(self, arrived):
        if not self.steps:
            self.result = [(cur.reshape(got.shape), got) for got, (_, cur, _) in zip(arrived, self.flying)]
            return
        self.pending = []
        for got, (_, cur, (axis, bit)) in zip(arrived, self.flying):
            got = got.reshape(cur.shape)
            here = (lax.axis_index(axis) >> bit) & 1
            low = jnp.where(here == 0, cur, got)
            high = jnp.where(here == 0, got, cur)
            self.pending.append(jnp.concatenate([low, high], self.index_order.index((axis, bit))))


def launch(streams, *values):
    streams = [s for s in streams if s.result is None]
    ready, values = tie([s.ready() for s in streams], values)
    for stream, sends in zip(streams, ready):
        stream.set_ready(sends)
        stream.start()
    return values


def land(streams, *values):
    streams = [s for s in streams if s.result is None]
    if any(isinstance(s, Gather) for s in streams):
        arrived, values = tie([s.arrived() for s in streams], values)
    else:
        arrived = [tie(s.arrived(), values)[0] for s in streams]
    for stream, got in zip(streams, arrived):
        stream.finish(got)
    return values


def beside(streams, work, *inputs):
    out = work(*launch(streams, *inputs))
    return land(streams, *out) if isinstance(out, (tuple, list)) else land(streams, out)[0]


def body(
    tokens,
    lengths,
    cotangent,
    query_weight,
    query_bias,
    keyval_weight,
    keyval_bias,
    out_weight,
    out_bias,
    norm_attn_gain,
    norm_attn_bias,
    norm_mlp_gain,
    norm_mlp_bias,
    up_weight,
    up_bias,
    down_weight,
    down_bias,
):
    n_dp, n_fsdp = lax.axis_size("dp"), lax.axis_size("fsdp")
    shards = n_dp * n_fsdp
    rows, width = query_weight.shape
    kv_width = keyval_weight.shape[1]
    ff = up_weight.shape[1]
    blocks = ff // width
    seq_len = tokens.shape[1]
    x = tokens.reshape(seq_len, width)
    cot = cotangent.reshape(seq_len, width)

    half = rows * n_fsdp
    info = jnp.concatenate([lengths, (lax.axis_index("dp") & 1)[None].astype(jnp.int32)])
    dp_bits, fs_bits = bits_of("dp", n_dp), bits_of("fsdp", n_fsdp)
    index_order = dp_bits[::-1] + fs_bits[::-1]
    x_bits, y_bits, z_bits = fs_bits[:1], dp_bits[1:], fs_bits[1:]
    xy = [x_bits + y_bits, y_bits + x_bits]

    up_bias_cols = up_bias.reshape(blocks, rows)
    key_bias_col = jnp.pad(keyval_bias, (0, rows - keyval_bias.shape[0]))
    vecs = [query_bias, out_bias, norm_attn_gain, norm_attn_bias, norm_mlp_gain, norm_mlp_bias, down_bias]
    vecs = jnp.concatenate([jnp.stack(vecs), up_bias_cols, key_bias_col[None]], 0)
    vecs = jnp.pad(vecs, ((0, LANES - vecs.shape[0]), (0, 0))).T
    first = Gather(jnp.concatenate([query_weight, keyval_weight, out_weight, vecs], 1), z_bits[::-1], xy, index_order)
    up_weight, down_weight = land([first], *launch([first], up_weight, down_weight))
    up_weight, down_weight = launch([first], up_weight, down_weight)
    up_local = up_weight.reshape(rows, shards, blocks, rows).transpose(0, 2, 1, 3).reshape(rows, ff)
    dn_local = down_weight.reshape(blocks, rows, width).transpose(1, 0, 2).reshape(rows, ff)
    up_local, dn_local = land([first], up_local, dn_local)
    for _ in z_bits[2:]:
        up_local, dn_local = land([first], *launch([first], up_local, dn_local))
    ups = Gather(up_local, z_bits[::-1], [x_bits + y_bits], index_order)
    dns = Gather(dn_local, z_bits[::-1], [y_bits + x_bits], index_order)
    (x,) = land([first, ups], *launch([first, ups], x))
    (x,) = land([first, dns], *launch([first, dns], x))
    while first.result is None:
        (x,) = land([first], *launch([first], x))

    tables = rotary_tables(seq_len, kv_width // 2)
    one, two = first.result
    q, kv, ha, hm, gy, gm, vec, w_q, w_o = beside(
        [ups, dns], lambda x: pre(info, x, cot, one, two, tables, kv_width, shards, half), x
    )
    pairs = width // LANES
    second = [ups, dns]
    state = beside(second, lambda q: attention(info, q, gm, kv, tables, None, 0, 2), q)
    (state,) = launch(second, state)
    for start in range(2, pairs, 2):
        state = attention(info, q, gm, kv, tables, state, start, 2)
    dkv, mixed, dq = land(second, *state)
    send, keep = beside(second, lambda mixed: attention_grads(info, ha, gy, mixed, dq, dkv, w_q, w_o, shards, half), mixed)
    while any(s.result is None for s in second):
        send, keep = beside(second, lambda *v: v, send, keep)
    (up_rows,), (dn_rows,) = ups.result, dns.result

    attn = Scatter([(send, keep)], [x_bits + z_bits[:1] + y_bits], z_bits[1:], index_order)
    ff_part = lambda chunk, count: lambda hm, gy, *state: feed_forward(
        info, hm, gy, up_rows, dn_rows, vec, w_o, state[0] if state else None, chunk, count, half
    )
    n0 = blocks // 2
    hm, gy = beside([attn], lambda *v: v, hm, gy)
    act0, gup0, state, send, keep = beside([attn], ff_part(0, n0), hm, gy)
    ff0 = Scatter([(send, keep)], xy, z_bits, index_order)
    hm, gy, state = launch([attn], hm, gy, state)
    hm, gy, state = beside([ff0], lambda *v: v, hm, gy, state)
    act1, gup1, _, send, keep = beside([ff0], ff_part(n0, blocks - n0), hm, gy, state)
    send, keep = land([attn], send, keep)
    ff1 = Scatter([(send, keep)], xy, z_bits, index_order)
    layer_out = beside(
        [ff0, ff1, attn],
        lambda x, *acts: layer_output(info, x, mixed, w_o, dn_rows, vec, acts, half),
        *(x, act0, act1),
    )
    gtok = beside(
        [ff1, ff0, attn],
        lambda cot, *gups: token_grads(info, x, cot, dq, dkv, w_q, up_rows, vec, gups, half),
        *(cot, gup0, gup1),
    )
    streams = [attn, ff0, ff1]
    while any(s.result is None for s in streams):
        beside(streams, lambda *v: v)
    gq, gkv, go, gu, gd, *lines = end(streams, width, kv_width, blocks, (n0, blocks - n0), shards)
    if shards * blocks > 128:
        gu = gu.reshape(rows, blocks, shards, rows).transpose(0, 2, 1, 3).reshape(rows, ff)
    bq, bkv, bo, ga, ba, g_gain, g_shift, b_up, b_dn = (v.reshape(-1) for v in lines)
    return (
        layer_out.reshape(tokens.shape),
        gtok.reshape(tokens.shape),
        gq,
        bq,
        gkv,
        bkv,
        go,
        bo,
        ga,
        ba,
        g_gain,
        g_shift,
        gu,
        b_up,
        gd,
        b_dn,
    )


def solution(mesh):
    mat, vec, seq = P(BOTH, None), P(BOTH), P(BOTH, None, None)
    return jax.shard_map(
        body,
        mesh=mesh,
        in_specs=(seq, vec, seq, mat, vec, mat, vec, mat, vec, vec, vec, vec, vec, mat, vec, mat, vec),
        out_specs=(seq, seq, mat, vec, mat, vec, mat, vec, vec, vec, vec, vec, mat, vec, mat, vec),
        check_vma=False,
    )
```
